32 devices in a mesh: wide: 8 (over y, x, core), narrow: 4 (over z).
Axes of the slice: x: 2, y: 2, z: 4, core: 2. Of those that a mesh axis runs over, the one named last changes fastest.
Arguments:
- tokens: bfloat16 [32, 4, 49, 768], P('wide', 'narrow'), may hold values from -6 to 6
- cotangent: bfloat16 [32, 4, 49, 768], P('wide', 'narrow'), may hold values from -6 to 6
- crops: int32 [32, 2], P('wide'), may hold values from 4 to 14, as said below
- labels: int32 [32, 4, 49], P('wide', 'narrow'), may hold values from 0 to 3
- norm_gains: float32 [2, 768], replicated, may hold values from 0.25 to 1.75
- biases: float32 [6, 768], replicated, may hold values from -2 to 2
- rel_table: float32 [169, 24], replicated, may hold values from -3 to 3
- w_qkv: bfloat16 [768, 2304], replicated, may hold values from -0.21875 to 0.21875
- w_proj: bfloat16 [768, 768], replicated, may hold values from -0.625 to 0.625
- w_fc1: bfloat16 [768, 3072], replicated, may hold values from -0.21875 to 0.21875
- fc1_bias: float32 [3072], replicated, may hold values from -2 to 2
- w_fc2: bfloat16 [3072, 768], replicated, may hold values from -0.109375 to 0.109375
Outputs:
- result: bfloat16 [32, 4, 49, 768], P('wide', 'narrow')
- grad_tokens: bfloat16 [32, 4, 49, 768], P('wide', 'narrow')
- grad_qkv: float32 [768, 2304], P('narrow', 'wide')
- grad_proj: float32 [768, 768], P('narrow', 'wide')
- grad_fc1: float32 [768, 3072], P('narrow', 'wide')
- grad_fc2: float32 [3072, 768], P('narrow', 'wide')
- grad_gains: float32 [2, 768], replicated
- grad_biases: float32 [6, 768], replicated
- grad_fc1_bias: float32 [3072], replicated
- grad_rel: float32 [169, 24], replicated
- stats: float32 [3], replicated
The draws below stay inside these ranges and needn't reach their ends.
Inputs may be any that keep to these rules, and one draw needn't show every extreme that they name: `crops`: every block of 4 images on one index of wide holds an image with a full 14 x 14 grid; some image has a 4 x 4 crop.
All inputs are finite; a program needn't handle non-finite values.
Results may differ from the reference program's by a relative error of at most 0.013.
Values may be sent and summed in bfloat16 or wider, within the bound.
A program may use at most 128 MiB of HBM per device.

```python
import jax
import jax.numpy as jnp
from jax import lax

D = 768
HEADS = 24
HEAD = 32
FF = 3072
IMG_DEV = 4
IMAGES = 32


def draw_crops(key, part):
    key = jax.random.fold_in(key, 7)
    first = jax.random.randint(jax.random.fold_in(key, 1), (IMAGES, 2), 4, 15)
    second = jax.random.randint(jax.random.fold_in(key, 2), (IMAGES, 2), 4, 15)
    crop_sizes = jnp.minimum(first, second)
    picked = jax.random.randint(jax.random.fold_in(key, 3), (IMAGES // IMG_DEV,), 0, IMG_DEV)
    slot_index = jnp.arange(IMAGES, dtype=jnp.int32) % IMG_DEV
    chosen = jnp.repeat(picked, IMG_DEV, total_repeat_length=IMAGES)
    crop_sizes = jnp.where((slot_index == chosen)[:, None], 14, crop_sizes)
    smallest = (slot_index == (chosen + 1) % IMG_DEV) & (jnp.arange(IMAGES, dtype=jnp.int32) < IMG_DEV)
    crop_sizes = jnp.where(smallest[:, None], 4, crop_sizes)
    return crop_sizes.astype(jnp.int32)


def plant(array, stream_key, low, top_value):
    place = [jax.random.randint(jax.random.fold_in(stream_key, axis), (), 0, length) for axis, length in enumerate(array.shape)]
    longest = array.shape.index(max(array.shape))
    beside = place[:longest] + [(place[longest] + 1) % array.shape[longest]] + place[longest + 1:]
    return array.at[tuple(place)].set(low).at[tuple(beside)].set(top_value)


def level_of(key, dims, cuts, low, top_value):
    level = 1.0
    for axis_at, shards_of in cuts:
        steps = jax.random.uniform(jax.random.fold_in(jax.random.fold_in(key, 6), axis_at), (shards_of,), jnp.float32, low / len(cuts), top_value / len(cuts))
        level = level * jnp.repeat(jnp.exp(steps), dims[axis_at] // shards_of).reshape((-1,) + (1,) * (len(dims) - 1 - axis_at))
    return level


def bell_draw(own_key, extent, width, reach, pieces=(), held_as=jnp.bfloat16):
    values = width * jax.random.normal(own_key, extent, jnp.float32)
    if pieces:
        values = values * level_of(own_key, extent, pieces, -0.22, 0.18)
    return jnp.clip(values, -reach, reach).astype(held_as)


def setup_inputs(seed: int = 0) -> dict:
    keys = jax.random.split(jax.random.key(seed), 13)
    return {
        "tokens": bell_draw(keys[0], (IMAGES, 4, 49, D), 1.0, 6.0, ((0, 8), (1, 4))),
        "cotangent": bell_draw(keys[1], (IMAGES, 4, 49, D), 1.0, 6.0, ((0, 8), (1, 4))),
        "crops": draw_crops(jax.random.fold_in(keys[12], 71), 0),
        "labels": plant(jax.random.randint(keys[3], (IMAGES, 4, 49), 0, 4), jax.random.fold_in(keys[3], 1), 0, 3).astype(jnp.int32),
        "norm_gains": jnp.clip(1.0 + 0.15 * jax.random.normal(keys[4], (2, D), jnp.float32), 0.25, 1.75),
        "biases": bell_draw(keys[5], (6, D), 0.3, 2.0, (), jnp.float32),
        "rel_table": bell_draw(keys[6], (169, HEADS), 0.5, 3.0, (), jnp.float32),
        "w_qkv": bell_draw(keys[7], (D, 3 * D), D ** -0.5, 0.21875),
        "w_proj": bell_draw(keys[8], (D, D), (D // 8) ** -0.5, 0.625),
        "w_fc1": bell_draw(keys[9], (D, FF), D ** -0.5, 0.21875),
        "fc1_bias": bell_draw(keys[10], (FF,), 0.3, 2.0, (), jnp.float32),
        "w_fc2": bell_draw(keys[11], (FF, D), FF ** -0.5, 0.109375),
    }


@jax.custom_vjp
def low(v):
    return lax.optimization_barrier(v.astype(jnp.bfloat16)).astype(jnp.float32)

@jax.custom_vjp
def low_back(v):
    return v

def low_keep(v):
    return (low(v), None)

def low_pass(kept, grad):
    return (grad,)

def back_keep(v):
    return (v, None)

def back_low(kept, grad):
    return (low(grad),)
low.defvjp(low_keep, low_pass)
low_back.defvjp(back_keep, back_low)

def layer_norm(values, gain, shift):
    centre = lax.optimization_barrier(jnp.mean(values, axis=-1, keepdims=True))
    centred = values - centre
    spread = lax.optimization_barrier(jnp.mean(centred * centred, axis=-1, keepdims=True))
    return centred * lax.rsqrt(spread + 1e-05) * gain + shift

def matmul_high(left, right):
    return jnp.dot(left, right, precision=lax.Precision.HIGHEST, preferred_element_type=jnp.float32)

def to_grid(field):
    group_size = field.shape[0]
    feature_count = field.shape[-1]
    return field.reshape(group_size, 2, 2, 7, 7, feature_count).transpose(0, 1, 3, 2, 4, 5).reshape(group_size, 14, 14, feature_count)

def from_grid(field):
    group_size = field.shape[0]
    feature_count = field.shape[-1]
    return field.reshape(group_size, 2, 7, 2, 7, feature_count).transpose(0, 1, 3, 2, 4, 5).reshape(group_size, 4, 49, feature_count)

def grid_places(offset):
    positions = jnp.arange(196, dtype=jnp.int32)
    window = positions // 49
    inner = positions % 49
    grid_rows = (7 * (window // 2) + offset + inner // 7) % 14
    grid_cols = (7 * (window % 2) + offset + inner % 7) % 14
    return (grid_rows.reshape(4, 49), grid_cols.reshape(4, 49))

def relative_index():
    positions = jnp.arange(49, dtype=jnp.int32)
    inner_rows = positions // 7
    inner_cols = positions % 7
    return (inner_rows[:, None] - inner_rows[None, :] + 6) * 13 + inner_cols[:, None] - inner_cols[None, :] + 6

def block(tokens, norm_gains, biases, rel_table, w_qkv, w_proj, w_fc1, fc1_bias, w_fc2, allowed):
    group_size = tokens.shape[0]
    normed = low(low_back(layer_norm(tokens, norm_gains[0], biases[4])))
    windows = from_grid(jnp.roll(to_grid(normed), (-3, -3), (1, 2)))
    projected = matmul_high(windows.reshape(-1, D), w_qkv).reshape(group_size, 4, 49, 3, HEADS, HEAD)
    query_rows = low(low_back(projected[:, :, :, 0] + biases[0].reshape(HEADS, HEAD)))
    key_rows = low(low_back(projected[:, :, :, 1]))
    value_rows = low(low_back(projected[:, :, :, 2] + biases[1].reshape(HEADS, HEAD)))
    bias_table = rel_table[relative_index()].transpose(2, 0, 1)
    scores = jnp.einsum('gwphe,gwqhe->gwhpq', query_rows, key_rows, precision=lax.Precision.HIGHEST) * HEAD ** (-0.5) + bias_table
    scores = low_back(scores)
    masked = jnp.where(allowed[:, :, None], scores, -1000000000.0)
    row_top = lax.optimization_barrier(jnp.max(masked, axis=-1, keepdims=True))
    exponent = jnp.exp(masked - row_top)
    attn_probs = low(exponent / lax.optimization_barrier(jnp.sum(exponent, axis=-1, keepdims=True)))
    attended = jnp.einsum('gwhpq,gwqhe->gwphe', attn_probs, value_rows, precision=lax.Precision.HIGHEST).reshape(group_size, 4, 49, D)
    attended = low(low_back(attended))
    restored = from_grid(jnp.roll(to_grid(attended), (3, 3), (1, 2)))
    branch_attn = low_back(matmul_high(restored.reshape(-1, D), w_proj).reshape(group_size, 4, 49, D) + biases[2])
    middle = tokens + branch_attn
    normed_two = low(layer_norm(middle, norm_gains[1], biases[5]))
    hidden = low_back(matmul_high(normed_two.reshape(-1, D), w_fc1) + fc1_bias)
    activated = low(jax.nn.gelu(hidden, approximate=False))
    branch_mlp = matmul_high(activated, w_fc2).reshape(group_size, 4, 49, D) + biases[3]
    return (middle + branch_mlp, (branch_attn, branch_mlp))

def reference(tokens, cotangent, crops, labels, norm_gains, biases, rel_table, w_qkv, w_proj, w_fc1, fc1_bias, w_fc2):
    groups = IMAGES // 8
    shift_rows, shift_cols = grid_places(3)
    own_rows, own_cols = grid_places(0)
    diagonal_on = jnp.eye(49, dtype=bool)
    weights = (norm_gains, biases, rel_table, w_qkv.astype(jnp.float32), w_proj.astype(jnp.float32), w_fc1.astype(jnp.float32), fc1_bias, w_fc2.astype(jnp.float32))

    def scan_step(carry, batch_piece):
        piece, cot_piece, crop_piece, label_piece = batch_piece
        valid_shift = (shift_rows[None] < crop_piece[:, 0, None, None]) & (shift_cols[None] < crop_piece[:, 1, None, None])
        allowed = (label_piece[..., :, None] == label_piece[..., None, :]) & valid_shift[..., None, :] | diagonal_on
        inputs = piece.astype(jnp.float32)

        def forward(values, *params):
            return block(values, *params, allowed)
        output, pull, branches = jax.vjp(forward, inputs, *weights, has_aux=True)
        grads = pull(cot_piece.astype(jnp.float32))
        valid_own = ((own_rows[None] < crop_piece[:, 0, None, None]) & (own_cols[None] < crop_piece[:, 1, None, None])).astype(jnp.float32)
        stat_sums = jnp.stack([jnp.sum(valid_own), jnp.sum(valid_own * lax.optimization_barrier(jnp.sum(inputs * inputs, axis=-1))), jnp.sum(valid_own * lax.optimization_barrier(jnp.sum(branches[0] * branches[0], axis=-1))), jnp.sum(valid_own * lax.optimization_barrier(jnp.sum(branches[1] * branches[1], axis=-1)))])
        totals, sums_before = carry
        totals = tuple((before + grad for before, grad in zip(totals, grads[1:])))
        return ((totals, sums_before + stat_sums), (output.astype(jnp.bfloat16), grads[0].astype(jnp.bfloat16)))
    start = (tuple((jnp.zeros(weight.shape, jnp.float32) for weight in weights)), jnp.zeros((4,), jnp.float32))
    batches = (tokens.reshape(groups, 8, 4, 49, D), cotangent.reshape(groups, 8, 4, 49, D), crops.reshape(groups, 8, 2), labels.reshape(groups, 8, 4, 49))
    (totals, stat_sums), (result, grad_tokens) = lax.scan(scan_step, start, batches)
    grad_gains, grad_biases, grad_rel, grad_qkv, grad_proj, grad_fc1, grad_fc1_bias, grad_fc2 = totals
    stats = jnp.sqrt(stat_sums[1:] / (D * stat_sums[0]))
    return (result.reshape(IMAGES, 4, 49, D), grad_tokens.reshape(IMAGES, 4, 49, D), grad_qkv, grad_proj, grad_fc1, grad_fc2, grad_gains, grad_biases, grad_fc1_bias, grad_rel, stats)
```

```python
from functools import partial

import jax
import jax.numpy as jnp
import numpy as np
from jax import lax
from jax.experimental import pallas as pl
from jax.experimental.pallas import tpu as pltpu
from jax.sharding import PartitionSpec as P


def from_partner(shard, axis, stride):
    return lax.ppermute(shard, axis, [(i, i ^ 1 << stride) for i in range(lax.axis_size(axis))])


def layer_norm(values, gain, shift):
    centre = jnp.mean(values, axis=-1, keepdims=True)
    centred = values - centre
    spread = jnp.mean(centred * centred, axis=-1, keepdims=True)
    return centred * lax.rsqrt(spread + 1e-05) * gain + shift


def into_window(field, swap_rows, swap_cols):
    tall = jnp.concatenate([field[:, 3:], swap_rows(field[:, :3])], axis=1)
    return jnp.concatenate([tall[:, :, 3:], swap_cols(tall[:, :, :3])], axis=2)


def out_of_window(field, swap_rows, swap_cols):
    broad = jnp.concatenate([swap_cols(field[:, :, 4:]), field[:, :, :4]], axis=2)
    return jnp.concatenate([swap_rows(broad[:, 4:]), broad[:, :4]], axis=1)


def relative_index():
    positions = jnp.arange(49, dtype=jnp.int32)
    inner_rows = positions // 7
    inner_cols = positions % 7
    return (
        (inner_rows[:, None] - inner_rows[None, :] + 6) * 13
        + inner_cols[:, None]
        - inner_cols[None, :]
        + 6
    )


def column_sum(values):
    return jnp.sum(values, axis=0, dtype=jnp.float32)


def on_device(
    tokens,
    cotangent,
    crops,
    labels,
    norm_gains,
    biases,
    rel_table,
    w_qkv,
    w_proj,
    w_fc1,
    fc1_bias,
    w_fc2,
):
    images = tokens.shape[0]
    model_width = tokens.shape[-1]
    head_count = rel_table.shape[1]
    head_size = model_width // head_count
    rows_all = images * 49
    score_scale = head_size ** (-0.5)
    where_narrow = lax.axis_index("narrow")
    row_half = where_narrow // 2
    col_half = where_narrow % 2
    positions = jnp.arange(49, dtype=jnp.int32)
    own_row = 7 * row_half + positions // 7
    own_col = 7 * col_half + positions % 7
    shift_row = (own_row + 3) % 14
    shift_col = (own_col + 3) % 14
    valid_own = (own_row[None] < crops[:, 0:1]) & (own_col[None] < crops[:, 1:2])
    valid_shift = (shift_row[None] < crops[:, 0:1]) & (shift_col[None] < crops[:, 1:2])
    label_rows = labels[:, 0]
    allowed = (label_rows[:, :, None] == label_rows[:, None, :]) & valid_shift[
        :, None, :
    ] | jnp.eye(49, dtype=bool)[None]
    allowed_heads = allowed[:, None]
    inputs = tokens[:, 0].astype(jnp.float32)
    normed, ln1_back = jax.vjp(layer_norm, inputs, norm_gains[0], biases[4])
    normed_low = normed.astype(jnp.bfloat16).reshape(images, 7, 7, model_width)
    windows = into_window(
        normed_low,
        lambda strip: from_partner(strip, "narrow", 1),
        lambda strip: from_partner(strip, "narrow", 0),
    ).reshape(rows_all, model_width)
    projected = jnp.dot(windows, w_qkv, preferred_element_type=jnp.float32)
    head_shape = (images, 49, head_count, head_size)
    query_rows = (projected[:, :model_width] + biases[0]).astype(jnp.bfloat16).reshape(head_shape)
    key_rows = projected[:, model_width : 2 * model_width].astype(jnp.bfloat16).reshape(head_shape)
    value_rows = (
        (projected[:, 2 * model_width :] + biases[1]).astype(jnp.bfloat16).reshape(head_shape)
    )
    one_hot = (
        (relative_index()[:, :, None] == jnp.arange(169, dtype=jnp.int32))
        .reshape(2401, 169)
        .astype(jnp.float32)
    )
    bias_table = (
        jnp.dot(one_hot, rel_table, precision=lax.Precision.HIGHEST)
        .reshape(49, 49, head_count)
        .transpose(2, 0, 1)
    )

    def masked_scores():
        raw = jnp.einsum(
            "nphe,nqhe->nhpq", query_rows, key_rows, preferred_element_type=jnp.float32
        )
        return jnp.where(allowed_heads, raw * score_scale + bias_table[None], -1000000000.0)

    masked = masked_scores()
    row_top = jnp.max(masked, axis=-1, keepdims=True)
    log_total = row_top + jnp.log(jnp.sum(jnp.exp(masked - row_top), axis=-1, keepdims=True))
    attn_probs = jnp.exp(masked - log_total)
    probs_low = attn_probs.astype(jnp.bfloat16)
    attended = jnp.einsum(
        "nhpq,nqhe->nphe", probs_low, value_rows, preferred_element_type=jnp.float32
    ).astype(jnp.bfloat16)
    restored = out_of_window(
        attended.reshape(images, 7, 7, model_width),
        lambda strip: from_partner(strip, "narrow", 1),
        lambda strip: from_partner(strip, "narrow", 0),
    ).reshape(rows_all, model_width)
    branch_attn = jnp.dot(restored, w_proj, preferred_element_type=jnp.float32) + biases[2]
    middle = inputs.reshape(rows_all, model_width) + branch_attn
    normed_two, ln2_back = jax.vjp(layer_norm, middle, norm_gains[1], biases[5])
    normed_two_low = normed_two.astype(jnp.bfloat16)
    hidden = jnp.dot(normed_two_low, w_fc1, preferred_element_type=jnp.float32) + fc1_bias
    activated, gelu_back = jax.vjp(partial(jax.nn.gelu, approximate=False), hidden)
    activated_low = activated.astype(jnp.bfloat16)
    branch_mlp = jnp.dot(activated_low, w_fc2, preferred_element_type=jnp.float32) + biases[3]
    result = (middle + branch_mlp).astype(jnp.bfloat16).reshape(images, 1, 49, model_width)
    cot_rows = cotangent.reshape(rows_all, model_width)
    grad_fc2 = jnp.dot(activated_low.T, cot_rows, preferred_element_type=jnp.float32)
    d_activated = jnp.dot(cot_rows, w_fc2.T, preferred_element_type=jnp.float32)
    (d_hidden,) = gelu_back(d_activated)
    d_hidden_low = d_hidden.astype(jnp.bfloat16)
    grad_fc1 = jnp.dot(normed_two_low.T, d_hidden_low, preferred_element_type=jnp.float32)
    grad_fc1_bias = column_sum(d_hidden_low)
    d_normed_two = jnp.dot(d_hidden_low, w_fc1.T, preferred_element_type=jnp.float32)
    d_middle_norm, d_gain_two, d_shift_two = ln2_back(d_normed_two)
    d_middle = cot_rows.astype(jnp.float32) + d_middle_norm
    d_branch = d_middle.astype(jnp.bfloat16)
    grad_proj = jnp.dot(restored.T, d_branch, preferred_element_type=jnp.float32)
    d_restored = jnp.dot(d_branch, w_proj.T, preferred_element_type=jnp.float32).astype(
        jnp.bfloat16
    )
    d_attended = into_window(
        d_restored.reshape(images, 7, 7, model_width),
        lambda strip: from_partner(strip, "narrow", 1),
        lambda strip: from_partner(strip, "narrow", 0),
    ).reshape(head_shape)
    again = jnp.exp(masked_scores() - log_total)
    d_probs = jnp.einsum(
        "nphe,nqhe->nhpq", d_attended, value_rows, preferred_element_type=jnp.float32
    )
    d_scores = (again * (d_probs - jnp.sum(again * d_probs, axis=-1, keepdims=True))).astype(
        jnp.bfloat16
    )
    d_table = jnp.sum(d_scores, axis=0, dtype=jnp.float32).reshape(head_count, 2401)
    grad_rel = jnp.dot(d_table, one_hot, precision=lax.Precision.HIGHEST).T
    d_query = (
        jnp.einsum("nhpq,nqhe->nphe", d_scores, key_rows, preferred_element_type=jnp.float32)
        * score_scale
    ).astype(jnp.bfloat16)
    d_key = (
        jnp.einsum("nhpq,nphe->nqhe", d_scores, query_rows, preferred_element_type=jnp.float32)
        * score_scale
    ).astype(jnp.bfloat16)
    d_value = jnp.einsum(
        "nhpq,nphe->nqhe", probs_low, d_attended, preferred_element_type=jnp.float32
    ).astype(jnp.bfloat16)
    d_projected = jnp.concatenate(
        [
            d_query.reshape(rows_all, model_width),
            d_key.reshape(rows_all, model_width),
            d_value.reshape(rows_all, model_width),
        ],
        axis=1,
    )
    grad_qkv = jnp.dot(windows.T, d_projected, preferred_element_type=jnp.float32)
    d_windows = jnp.dot(d_projected, w_qkv.T, preferred_element_type=jnp.float32).astype(
        jnp.bfloat16
    )
    d_normed = out_of_window(
        d_windows.reshape(images, 7, 7, model_width),
        lambda strip: from_partner(strip, "narrow", 1),
        lambda strip: from_partner(strip, "narrow", 0),
    ).reshape(images, 49, model_width)
    d_inputs_norm, d_gain_one, d_shift_one = ln1_back(d_normed.astype(jnp.float32))
    grad_tokens = (
        (d_middle.reshape(images, 49, model_width) + d_inputs_norm)
        .astype(jnp.bfloat16)
        .reshape(images, 1, 49, model_width)
    )
    grad_biases = jnp.stack(
        [
            column_sum(d_query.reshape(rows_all, model_width)),
            column_sum(d_value.reshape(rows_all, model_width)),
            column_sum(d_branch),
            column_sum(cot_rows),
            d_shift_one,
            d_shift_two,
        ]
    )
    grad_gains = jnp.stack([d_gain_one, d_gain_two])
    valid_weight = valid_own.astype(jnp.float32).reshape(rows_all)
    flat_inputs = inputs.reshape(rows_all, model_width)
    stat_sums = jnp.stack(
        [
            jnp.sum(valid_weight),
            jnp.sum(valid_weight * jnp.sum(flat_inputs * flat_inputs, axis=-1)),
            jnp.sum(valid_weight * jnp.sum(branch_attn * branch_attn, axis=-1)),
            jnp.sum(valid_weight * jnp.sum(branch_mlp * branch_mlp, axis=-1)),
        ]
    )
    grad_biases, grad_gains, grad_fc1_bias, grad_rel, stat_sums = lax.psum(
        (grad_biases, grad_gains, grad_fc1_bias, grad_rel, stat_sums), ("wide", "narrow")
    )
    stats = jnp.sqrt(stat_sums[1:] / (model_width * stat_sums[0]))
    matrices = (grad_qkv, grad_proj, grad_fc1, grad_fc2)
    partial_sums = (
        lax.psum_scatter(matrices[0], "wide", scatter_dimension=1, tiled=True),
        lax.psum_scatter(matrices[1], "wide", scatter_dimension=1, tiled=True),
        lax.psum_scatter(matrices[2], "wide", scatter_dimension=1, tiled=True),
        lax.psum_scatter(matrices[3], "wide", scatter_dimension=1, tiled=True),
    )
    reduced = (
        lax.psum_scatter(
            partial_sums[0].astype(jnp.bfloat16), "narrow", scatter_dimension=0, tiled=True
        ).astype(jnp.float32),
        lax.psum_scatter(
            partial_sums[1].astype(jnp.bfloat16), "narrow", scatter_dimension=0, tiled=True
        ).astype(jnp.float32),
        lax.psum_scatter(
            partial_sums[2].astype(jnp.bfloat16), "narrow", scatter_dimension=0, tiled=True
        ).astype(jnp.float32),
        lax.psum_scatter(
            partial_sums[3].astype(jnp.bfloat16), "narrow", scatter_dimension=0, tiled=True
        ).astype(jnp.float32),
    )
    grad_qkv, grad_proj, grad_fc1, grad_fc2 = reduced
    return (
        result,
        grad_tokens,
        grad_qkv,
        grad_proj,
        grad_fc1,
        grad_fc2,
        grad_gains,
        grad_biases,
        grad_fc1_bias,
        grad_rel,
        stats,
    )


def plain(mesh):
    return jax.shard_map(
        on_device,
        mesh=mesh,
        in_specs=(
            P("wide", "narrow", None, None),
            P("wide", "narrow", None, None),
            P("wide", None),
            P("wide", "narrow", None),
            P(),
            P(),
            P(),
            P(),
            P(),
            P(),
            P(),
            P(),
        ),
        out_specs=(
            P("wide", "narrow", None, None),
            P("wide", "narrow", None, None),
            P("narrow", "wide"),
            P("narrow", "wide"),
            P("narrow", "wide"),
            P("narrow", "wide"),
            P(),
            P(),
            P(),
            P(),
            P(),
        ),
        check_vma=False,
    )


ROWS = 208
KEYS = 256
MESH = pl.DeviceIdType.MESH
LOW = jnp.bfloat16
FULL = jnp.float32


def place_tables():
    places = []
    for rows_i in (range(0, 4), range(4, 7)):
        pass
    for tall, broad in ((0, 0), (1, 0), (0, 1), (1, 1)):
        for image in range(4):
            for i in range(4, 7) if tall else range(4):
                for j in range(4, 7) if broad else range(4):
                    places.append((image, i, j, i - 4 if tall else i + 3, j - 4 if broad else j + 3))
    own = np.zeros((ROWS, 256), np.float32)
    spread = np.zeros((ROWS, 128), np.float32)
    pick = np.zeros((256, KEYS), np.float32)
    gather = np.zeros((64, ROWS), np.float32)
    offsets = np.zeros((KEYS, 128), np.float32)
    info = np.zeros((ROWS, 8), np.int32)
    info[:, 3] = -1
    for row in range(ROWS):
        if row >= len(places):
            info[row, 0] = 4 + row - len(places)
            continue
        image, i, j, a, b = places[row]
        own[row, 64 * image + 7 * a + b] = 1
        spread[row, 7 * i + j] = 1
        spread[row, 64 + 7 * i + j] = 1
        shift = (6 - i) * 13 + 6 - j
        pick[shift, row] = 1
        pick[128 + shift, row] = 1
        gather[7 * i + j, row] = 1
        offsets[row, shift] = 1
        info[row, :6] = (image, i, j, 7 * i + j, a, b)
    low = lambda table: table.astype(jnp.bfloat16)
    return low(own), low(own.T.copy()), low(spread), low(pick), low(gather), low(offsets), info


def dot(left, right):
    return jnp.dot(left, right, preferred_element_type=FULL)


def dot_t(left, right):
    return lax.dot_general(left, right, (((1,), (1,)), ((), ())), preferred_element_type=FULL)


def lanes(index, width):
    return pl.ds(pl.multiple_of(index * width, width), width)


def normed(values):
    centred = values - jnp.mean(values, axis=-1, keepdims=True)
    scale = lax.rsqrt(jnp.mean(centred * centred, axis=-1, keepdims=True) + 1e-05)
    return centred * scale, scale


def normed_back(grad, gain, unit, scale):
    inner = grad * gain
    along = jnp.mean(inner, axis=-1, keepdims=True)
    across = jnp.mean(inner * unit, axis=-1, keepdims=True)
    return scale * (inner - along - unit * across)


def sum_rows(values):
    return jnp.sum(values, axis=0, keepdims=True)


GROUPS = ((64, 48), (112, 48), (160, 48))

S_H1 = 0
S_ATT = 3
S_DRES = 21
S_DWIN = 39
S_GT = 48
S_XWT = 49
S_AOT = 50
S_H2T = 51
S_ACT = 52
S_DH = 56
S_DBK = 60
S_DYK = 61
S_AR = 65
S_F1 = 72
S_Q = 84
S_F2 = 96
S_COUNT = 120


def block_kernel(
    tokens,
    cotangent,
    crops,
    labels,
    gains,
    biases,
    rel_table,
    wq_hbm,
    wp_hbm,
    w1_hbm,
    fc1_bias,
    w2_hbm,
    own_t,
    back_t,
    spread_t,
    pick_t,
    gather_t,
    offsets_t,
    info,
    out_result,
    out_tokens,
    out_qp,
    out_f1,
    out_f2,
    out_small,
    wq,
    wp,
    w1,
    w2,
    stack,
    stack_two,
    x_own,
    g_low,
    g_t,
    g_tp,
    h1,
    xw,
    xw_t,
    xw_tp,
    query,
    key,
    value,
    bias_mask,
    probs,
    att,
    att_own,
    att_t,
    att_tp,
    middle,
    h2,
    h2_t,
    h2_tp,
    act,
    act_p,
    dh,
    dh_p,
    gf1,
    gf2,
    gq,
    r1f1,
    r1f2,
    r1q,
    r2f1,
    r2f2,
    r2q,
    r3f1,
    r3f2,
    r3q,
    r4f1,
    r4f2,
    r4q,
    d_mid,
    d_branch,
    db_pack,
    db_pack_p,
    d_res,
    d_att,
    d_proj,
    dy_pack,
    dy_pack_p,
    d_win,
    d_own,
    rel_rows,
    rel_grads,
    rel_pad,
    mask_add,
    valid_col,
    sums,
    sums_one,
    sums_two,
    got_core,
    got_wide,
    got_narrow,
    local_sem,
    send_sem,
    recv_sem,
):
    model = x_own.shape[1]
    width = lax.axis_index("wide")
    depth = lax.axis_index("narrow")
    core = width % 2
    mine = width // 2
    mate = {"wide": width ^ 1, "narrow": depth}
    beside = [None] + [{"wide": width ^ (2 * k), "narrow": depth} for k in (1, 2, 3)]
    along = [None] + [{"wide": width, "narrow": depth ^ k} for k in (1, 2, 3)]
    partners = [mate] + beside[1:] + along[1:]
    quadrant = (along[2], along[1], along[3])

    pending = []

    def copy_of(src, dst, index, device):
        return pltpu.make_async_remote_copy(
            src_ref=src,
            dst_ref=dst,
            send_sem=send_sem.at[index],
            recv_sem=recv_sem.at[index],
            device_id=device,
            device_id_type=MESH,
        )

    def send(src, dst, index, device):
        copy_of(src, dst, index, device).start()
        pending.append((src, dst, index, device))

    def got(src, dst, index, device):
        copy_of(src, dst, index, device).wait_recv()

    barrier = pltpu.get_barrier_semaphore()
    for partner in partners:
        pl.semaphore_signal(barrier, inc=1, device_id=partner, device_id_type=MESH)
    loads = [
        pltpu.make_async_copy(src, dst, local_sem.at[k])
        for k, (src, dst) in enumerate(((wq_hbm, wq), (wp_hbm, wp), (w1_hbm, w1), (w2_hbm, w2)))
    ]
    for load in loads:
        load.start()

    stack[...] = jnp.zeros_like(stack)
    for image in range(4):
        stack[64 * image : 64 * image + 49, :] = tokens[image]
    x_value = dot(own_t[...], stack[...])
    x_own[...] = x_value
    unit, _ = normed(x_value)
    h1[...] = (unit * gains[0:1, :] + biases[4:5, :]).astype(LOW)
    xw[0:64, :] = h1[0:64, :]

    pl.semaphore_wait(barrier, len(partners))
    for k, (row, count) in enumerate(GROUPS):
        send(h1.at[pl.ds(row, count)], xw.at[pl.ds(row, count)], S_H1 + k, quadrant[k])

    stack_two[...] = jnp.zeros_like(stack_two)
    for image in range(4):
        stack_two[64 * image : 64 * image + 49, :] = cotangent[image]
    g_value = dot(own_t[...], stack_two[...])
    g_low[...] = g_value.astype(LOW)
    g_t[...] = g_low[...].T
    send(g_t, g_tp, S_GT, mate)

    sums[...] = jnp.zeros_like(sums)
    sums[5:6, :] = sum_rows(g_value)

    row_half = depth // 2
    col_half = depth % 2
    image_col = info[:, 0:1]
    i_col = info[:, 1:2]
    j_col = info[:, 2:3]
    place_col = info[:, 3:4]
    zero_col = jnp.zeros((ROWS, 1), jnp.int32)
    crop_row = zero_col
    crop_col = zero_col
    label = jnp.zeros((ROWS, 1), FULL)
    lane49 = lax.broadcasted_iota(jnp.int32, (ROWS, 49), 1)
    for image in range(4):
        is_image = image_col == image
        crop_row = jnp.where(is_image, crops[image : image + 1, 0:1], crop_row)
        crop_col = jnp.where(is_image, crops[image : image + 1, 1:2], crop_col)
        picked = jnp.where(
            lane49 == place_col, labels[image : image + 1, :].astype(FULL), jnp.zeros((ROWS, 49), FULL)
        )
        label = jnp.where(is_image, jnp.sum(picked, axis=1, keepdims=True), label)
    valid = ((7 * row_half + info[:, 4:5]) < crop_row) & ((7 * col_half + info[:, 5:6]) < crop_col)
    valid_value = jnp.where(valid, 1.0, 0.0).astype(FULL)
    valid_col[...] = valid_value
    shift_row = 7 * row_half + i_col + 3
    shift_row = jnp.where(shift_row >= 14, shift_row - 14, shift_row)
    shift_col = 7 * col_half + j_col + 3
    shift_col = jnp.where(shift_col >= 14, shift_col - 14, shift_col)
    valid_key = (shift_row < crop_row) & (shift_col < crop_col)
    code = label + 8.0 * image_col.astype(FULL)
    key_code = jnp.where(valid_key, code, -1.0)
    diagonal = lax.broadcasted_iota(jnp.int32, (ROWS, KEYS), 0) == lax.broadcasted_iota(
        jnp.int32, (ROWS, KEYS), 1
    )
    key_row = jnp.sum(jnp.where(diagonal, key_code + 2.0, 0.0), axis=0, keepdims=True) - 2.0
    mask_add[...] = jnp.where((code == key_row) | diagonal, 0.0, -1000000000.0)

    rel_pad[...] = jnp.zeros_like(rel_pad)
    rel_pad[0:169, 0:24] = rel_table[...]
    table = rel_pad[...].T[0:24, :]
    rel_rows[...] = jnp.zeros_like(rel_rows)

    def shifted(i, carry):
        start = 13 * (i // 7) + i % 7
        rel_rows[pl.ds(pl.multiple_of(24 * i, 8), 24), :] = pltpu.roll(table, 256 - start, 1)[:, 0:128]
        return carry

    lax.fori_loop(0, 49, shifted, 0)

    def high_low(values):
        high = values.astype(LOW)
        return high, (values - high.astype(FULL)).astype(LOW)

    def head_bias(head, carry):
        rows = rel_rows[pl.ds(head, 64, stride=24), :]
        spread = dot(spread_t[...], jnp.concatenate(high_low(rows), axis=0))
        bias = dot(jnp.concatenate(high_low(spread), axis=1), pick_t[...])
        bias_mask[head] = bias + mask_add[...]
        return carry

    lax.fori_loop(0, 24, head_bias, 0)

    flat = x_own[...]
    stat_total = jnp.sum(valid_value, axis=0, keepdims=True)
    stat_input = sum_rows(valid_value * jnp.sum(flat * flat, axis=-1, keepdims=True))

    key[ROWS:KEYS, :] = jnp.zeros((KEYS - ROWS, model), LOW)
    value[ROWS:KEYS, :] = jnp.zeros((KEYS - ROWS, model), LOW)
    for k, (row, count) in enumerate(GROUPS):
        got(h1.at[pl.ds(row, count)], xw.at[pl.ds(row, count)], S_H1 + k, quadrant[k])
    loads[0].wait()

    def project(n, carry):
        at = lanes(n, 256)
        window = xw[...]
        query[:, at] = (dot(window, wq[:, at]) + biases[0:1, at]).astype(LOW)
        key[0:ROWS, at] = dot(window, wq[:, lanes(n + 3, 256)]).astype(LOW)
        value[0:ROWS, at] = (dot(window, wq[:, lanes(n + 6, 256)]) + biases[1:2, at]).astype(LOW)
        return carry

    lax.fori_loop(0, 3, project, 0)

    lane_head = lax.broadcasted_iota(jnp.int32, (1, 128), 1) // 32
    only = [(lane_head == h).astype(FULL).astype(LOW) for h in range(4)]
    here = [lax.broadcasted_iota(jnp.int32, (ROWS, 128), 1) // 32 == h for h in range(4)]
    scale = 32 ** (-0.5)

    def att_copies(t):
        at = lanes(t, 128)
        return [
            (att.at[pl.ds(row, count), at], att_own.at[pl.ds(row, count), at], S_ATT + 3 * t + k, quadrant[k])
            for k, (row, count) in enumerate(GROUPS)
        ]

    def attend(t, carry):
        at = lanes(t, 128)
        q = query[:, at]
        k = key[:, at]
        v = value[:, at]
        total = jnp.zeros((ROWS, 128), FULL)
        for h in range(4):
            scores = dot_t(q * only[h], k) * scale + bias_mask[4 * t + h]
            top = jnp.max(scores, axis=-1, keepdims=True)
            power = jnp.exp(scores - top)
            part = (power * (1.0 / jnp.sum(power, axis=-1, keepdims=True))).astype(LOW)
            probs[4 * t + h] = part
            total = jnp.where(here[h], dot(part, v), total)
        total = total.astype(LOW)
        att[:, at] = total
        att_own[0:64, at] = total[0:64, :]
        for args in att_copies(t):
            copy_of(*args).start()
        return carry

    lax.fori_loop(0, 6, attend, 0)

    xw_t[...] = xw[...].T
    send(xw_t, xw_tp, S_XWT, mate)

    def att_wait(t, carry):
        for args in att_copies(t):
            copy_of(*args).wait_recv()
        return carry

    lax.fori_loop(0, 6, att_wait, 0)
    att_t[...] = att_own[...].T
    send(att_t, att_tp, S_AOT, mate)
    loads[1].wait()

    def attn_branch(n, carry):
        at = lanes(n, 256)
        branch = dot(att_own[...], wp[:, at]) + biases[2:3, at]
        middle[:, at] = x_own[:, at] + branch
        return carry + jnp.sum(branch * branch, axis=-1, keepdims=True)

    branch_square = lax.fori_loop(0, 3, attn_branch, jnp.zeros((ROWS, 1), FULL))
    stat_attn = sum_rows(valid_col[...] * branch_square)

    unit, _ = normed(middle[...])
    h2[...] = (unit * gains[1:2, :] + biases[5:6, :]).astype(LOW)
    h2_t[...] = h2[...].T
    send(h2_t, h2_tp, S_H2T, mate)
    loads[2].wait()
    loads[3].wait()

    def turn(r):
        return mine ^ jnp.where(r == 0, 3, jnp.where(r == 3, 0, r))

    def mlp_copies(r):
        at = lanes(turn(r), 768)
        return [
            (act.at[:, at], act_p.at[:, at], S_ACT + r, mate),
            (dh.at[:, at], dh_p.at[:, at], S_DH + r, mate),
        ]

    def hidden_quarter(r):
        quarter = turn(r)

        def hidden_part(n, carry):
            at = lanes(quarter * 3 + n, 256)
            hidden = dot(h2[...], w1[:, at]) + fc1_bias[:, at]
            d_act = dot_t(g_low[...], w2[at, :])
            below = 0.5 + 0.5 * lax.erf(hidden * 0.7071067811865476)
            act[:, at] = (hidden * below).astype(LOW)
            slope = below + hidden * (0.3989422804014327 * jnp.exp(-0.5 * hidden * hidden))
            d_hidden = (slope * d_act).astype(LOW)
            dh[:, at] = d_hidden
            sums[pl.ds(8 + quarter, 1), lanes(n, 256)] = sum_rows(d_hidden.astype(FULL))
            return carry

        lax.fori_loop(0, 3, hidden_part, 0)
        for args in mlp_copies(r):
            copy_of(*args).start()

    first = (beside[1], beside[2])
    second = (beside[2], beside[1])
    second_block = (mine ^ 2, mine ^ 1)
    groups = {"f1": (gf1, r1f1, r2f1, r3f1, r4f1, S_F1, 4), "q": (gq, r1q, r2q, r3q, r4q, S_Q, 4)}
    groups["f2"] = (gf2, r1f2, r2f2, r3f2, r4f2, S_F2, 16)

    def step_one(name, route, slot):
        grads, landing, _, _, _, base, _ = groups[name]
        block = mine ^ 3 if slot == 0 else mine ^ (1 + route)
        return grads.at[block, route], landing.at[route, slot], base + 2 * route + slot, first[route]

    def step_one_f2(route, slot, r):
        block = mine ^ 3 if slot == 0 else mine ^ (1 + route)
        place = turn(r)
        return (
            gf2.at[block, route, place],
            r1f2.at[route, slot, place],
            S_F2 + 4 * r + 2 * route + slot,
            first[route],
        )

    def step_two(name, route):
        grads, _, landing, _, _, base, ones = groups[name]
        return grads.at[second_block[route], route], landing.at[route], base + ones + route, second[route]

    def step_three(name, route, slot):
        grads, _, _, landing, _, base, ones = groups[name]
        place = depth ^ 3 if slot == 0 else depth ^ 1
        return (
            grads.at[mine, route, place],
            landing.at[route, slot],
            base + ones + 2 + 2 * route + slot,
            along[1],
        )

    def step_four(name, route):
        grads, _, _, _, landing, base, ones = groups[name]
        return grads.at[mine, route, depth ^ 2], landing.at[route], base + ones + 6 + route, along[2]

    def grads_quarter(r):
        quarter = turn(r)
        for args in mlp_copies(r):
            copy_of(*args).wait_recv()
        at = lanes(2 * quarter + core, 384)

        def fc1_part(n, carry):
            rows = pl.ds(pl.multiple_of(n * 192, 64), 192)
            total = dot(h2_t[rows, :], dh[:, at]) + dot(h2_tp[rows, :], dh_p[:, at])
            gf1[quarter, 0, n] = total[0:96].astype(LOW)
            gf1[quarter, 1, n] = total[96:192].astype(LOW)
            return carry

        lax.fori_loop(0, 4, fc1_part, 0)

        @pl.when(r == 0)
        def _():
            copy_of(*step_one("f1", 0, 0)).start()
            copy_of(*step_one("f1", 1, 0)).start()

        @pl.when(r == 1)
        def _():
            copy_of(*step_one("f1", 0, 1)).start()

        @pl.when(r == 2)
        def _():
            copy_of(*step_one("f1", 1, 1)).start()

        wide_at = lanes(quarter, 768)

        def fc2_part(n, carry):
            rows = pl.ds(pl.multiple_of(n * 192 + core * 96, 32), 96)
            total = dot(g_t[rows, :], act[:, wide_at]) + dot(g_tp[rows, :], act_p[:, wide_at])
            gf2[n, 0, quarter] = total[0:48].astype(LOW)
            gf2[n, 1, quarter] = total[48:96].astype(LOW)
            return carry

        lax.fori_loop(0, 4, fc2_part, 0)
        for route in range(2):
            for slot in range(2):
                copy_of(*step_one_f2(route, slot, r)).start()

    got(g_t, g_tp, S_GT, mate)
    got(h2_t, h2_tp, S_H2T, mate)
    hidden_quarter(jnp.int32(0))

    def quarters(r, carry):
        hidden_quarter(r)
        grads_quarter(r - 1)
        return carry

    lax.fori_loop(1, 4, quarters, 0)
    grads_quarter(jnp.int32(3))

    def d_normed_part(n, carry):
        at = lanes(n, 256)
        d_mid[:, at] = dot_t(dh[...], w1[at, :])
        return carry

    lax.fori_loop(0, 3, d_normed_part, 0)
    unit, spread_two = normed(middle[...])
    d_normed = d_mid[...]
    sums[1:2, :] = sum_rows(d_normed * unit)
    sums[7:8, :] = sum_rows(d_normed)
    d_middle = g_low[...].astype(FULL) + normed_back(d_normed, gains[1:2, :], unit, spread_two)
    d_mid[...] = d_middle
    d_low = d_middle.astype(LOW)
    d_branch[...] = d_low
    sums[4:5, :] = sum_rows(d_low.astype(FULL))

    def res_copies(t):
        at = lanes(t, 128)
        return [
            (d_res.at[pl.ds(row, count), at], d_att.at[pl.ds(row, count), at], S_DRES + 3 * t + k, quadrant[k])
            for k, (row, count) in enumerate(GROUPS)
        ]

    def d_res_part(n, carry):
        at = lanes(n, 256)
        part = dot_t(d_branch[...], wp[at, :]).astype(LOW)
        d_res[:, at] = part
        d_att[0:64, at] = part[0:64, :]
        for t in range(2):
            for args in res_copies(2 * n + t):
                copy_of(*args).start()
        return carry

    lax.fori_loop(0, 3, d_res_part, 0)

    for j in range(8):
        db_pack[:, 128 * j : 128 * j + 128] = jnp.concatenate(
            [jnp.zeros((ROWS, 32), LOW), d_branch[:, 96 * j : 96 * j + 96]], axis=1
        )
    send(db_pack, db_pack_p, S_DBK, mate)

    def mlp_branch(n, carry):
        at = lanes(n, 256)
        branch = dot(act[...], w2[:, at]) + biases[3:4, at]
        stack_two[:, at] = dot(back_t[...], (middle[:, at] + branch).astype(LOW)).astype(LOW)
        return carry + jnp.sum(branch * branch, axis=-1, keepdims=True)

    branch_square = lax.fori_loop(0, 3, mlp_branch, jnp.zeros((ROWS, 1), FULL))
    stat_mlp = sum_rows(valid_col[...] * branch_square)
    for image in range(4):
        out_result[image] = stack_two[64 * image : 64 * image + 49, :]
    lane = lax.broadcasted_iota(jnp.int32, (1, 128), 1)
    stat_row = jnp.zeros((1, 128), FULL)
    for k, total in enumerate((stat_total, stat_input, stat_attn, stat_mlp)):
        stat_row = jnp.where(lane == k, total, stat_row)
    sums[12:13, 0:128] = stat_row

    def attend_back(t, carry):
        for args in res_copies(t):
            copy_of(*args).wait_recv()
        at = lanes(t, 128)
        q = query[:, at]
        k = key[:, at]
        v = value[:, at]
        d_out = d_att[:, at]
        q_t = q.T
        d_out_t = d_out.T
        d_query = jnp.zeros((ROWS, 128), FULL)
        d_key = []
        d_value = []
        for h in range(4):
            d_probs = dot_t(d_out * only[h], v)
            low_probs = probs[4 * t + h]
            part = low_probs.astype(FULL)
            common = jnp.sum(part * d_probs, axis=-1, keepdims=True)
            d_scores = (part * (d_probs - common)).astype(LOW)
            d_query = jnp.where(here[h], dot(d_scores, k), d_query)
            both = dot(jnp.concatenate([q_t[32 * h : 32 * h + 32], gather_t[...]], axis=0), d_scores)
            d_key.append(both[0:32])
            rel_grads[pl.ds(pl.multiple_of(64 * (4 * t + h), 64), 64), :] = dot(
                both[32:96].astype(LOW), offsets_t[...]
            )
            d_value.append(dot(d_out_t[32 * h : 32 * h + 32], low_probs))
        d_query = (d_query * scale).astype(LOW)
        d_key = (jnp.concatenate(d_key, axis=0) * scale).astype(LOW).T[0:ROWS]
        d_value = jnp.concatenate(d_value, axis=0).astype(LOW).T[0:ROWS]
        d_proj[:, at] = d_query
        d_proj[:, lanes(6 + t, 128)] = d_key
        d_proj[:, lanes(12 + t, 128)] = d_value
        sums[2:3, at] = sum_rows(d_query.astype(FULL))
        sums[3:4, at] = sum_rows(d_value.astype(FULL))
        return carry

    lax.fori_loop(0, 6, attend_back, 0)

    for j in range(8):
        dy_pack[:, 384 * j : 384 * j + 384] = jnp.concatenate(
            [d_proj[:, 288 * j : 288 * j + 288], jnp.zeros((ROWS, 96), LOW)], axis=1
        )

    def pack_copy(n):
        at = lanes(2 * n + 1 - core, 384)
        back = lanes(2 * n + core, 384)
        return dy_pack.at[:, at], dy_pack_p.at[:, at], S_DYK + n, mate

    for n in range(4):
        copy_of(*pack_copy(n)).start()

    def win_copies(n):
        at = lanes(n, 256)
        return [
            (d_win.at[pl.ds(row, count), at], d_own.at[pl.ds(row, count), at], S_DWIN + 3 * n + k, quadrant[k])
            for k, (row, count) in enumerate(GROUPS)
        ]

    def d_win_part(n, carry):
        at = lanes(n, 256)
        part = dot_t(d_proj[...], wq[at, :]).astype(LOW)
        d_win[:, at] = part
        d_own[0:64, at] = part[0:64, :]
        for args in win_copies(n):
            copy_of(*args).start()
        return carry

    lax.fori_loop(0, 3, d_win_part, 0)

    got(xw_t, xw_tp, S_XWT, mate)
    got(att_t, att_tp, S_AOT, mate)
    got(db_pack, db_pack_p, S_DBK, mate)

    def qp_block(block):
        got_at = lanes(2 * block + core, 384)

        def part(n, carry):
            rows = pl.ds(pl.multiple_of(n * 192, 64), 192)
            total = dot(xw_t[rows, :], dy_pack[:, got_at]) + dot(xw_tp[rows, :], dy_pack_p[:, got_at])
            at = lanes(2 * block + core, 128)
            more = dot(att_t[rows, :], db_pack[:, at]) + dot(att_tp[rows, :], db_pack_p[:, at])
            for half in range(2):
                cut = slice(96 * half, 96 * half + 96)
                gq[block, half, n, :, 0:256] = total[cut, 0:256].astype(LOW)
                gq[block, half, n, :, 256:384] = (total[cut, 256:384] + more[cut]).astype(LOW)
            return carry

        lax.fori_loop(0, 4, part, 0)

    def pack_wait(n):
        at = lanes(2 * n + core, 384)
        copy_of(dy_pack.at[:, at], dy_pack_p.at[:, at], S_DYK + n, mate).wait_recv()

    for n in range(4):
        pack_wait(n)
    for r in range(4):
        qp_block(turn(jnp.int32(r)))
        if r == 0:
            send(*step_one("q", 0, 0))
            send(*step_one("q", 1, 0))
        elif r == 1:
            send(*step_one("q", 0, 1))
        elif r == 2:
            send(*step_one("q", 1, 1))

    def add_in(grads, index, landing):
        grads[index] = (grads[index].astype(FULL) + landing[...].astype(FULL)).astype(LOW)

    def run_two(name, waits):
        grads, landing, _, _, _, _, _ = groups[name]
        for route in range(2):
            waits(route)
            for slot, block in ((0, second_block[route]), (1, mine)):

                def add(n, carry, slot=slot, block=block, route=route):
                    add_in(grads, (block, route, n), landing.at[route, slot, n])
                    return carry

                lax.fori_loop(0, 4, add, 0)
                if slot == 0:
                    send(*step_two(name, route))

    def wait_one(name):
        def waits(route):
            for slot in range(2):
                got(*step_one(name, route, slot))

        return waits

    def wait_one_f2(route):
        def wait(r, carry):
            for slot in range(2):
                copy_of(*step_one_f2(route, slot, r)).wait_recv()
            return carry

        lax.fori_loop(0, 4, wait, 0)

    def run_three(name):
        grads, _, landing, _, _, _, _ = groups[name]
        for route in range(2):
            got(*step_two(name, route))
            for slot, place in ((0, depth ^ 3), (1, depth ^ 1)):
                add_in(grads, (mine, route, place), landing.at[route, place])
                send(*step_three(name, route, slot))
            for place in (depth ^ 2, depth):
                add_in(grads, (mine, route, place), landing.at[route, place])

    def run_four(name):
        grads, _, _, landing, _, _, _ = groups[name]
        for route in range(2):
            for slot in range(2):
                got(*step_three(name, route, slot))
            add_in(grads, (mine, route, depth ^ 2), landing.at[route, 0])
            send(*step_four(name, route))
            add_in(grads, (mine, route, depth), landing.at[route, 1])

    def finish(name, out):
        grads, _, _, _, landing, _, _ = groups[name]
        for route in range(2):
            got(*step_four(name, route))
            out[route] = grads[mine, route, depth].astype(FULL) + landing[route].astype(FULL)

    run_two("f1", wait_one("f1"))
    run_two("f2", wait_one_f2)

    def win_wait(n, carry):
        for args in win_copies(n):
            copy_of(*args).wait_recv()
        return carry

    lax.fori_loop(0, 3, win_wait, 0)
    unit, spread_one = normed(x_own[...])
    d_value = d_own[...].astype(FULL)
    sums[0:1, :] = sum_rows(d_value * unit)
    sums[6:7, :] = sum_rows(d_value)
    d_input = (d_mid[...] + normed_back(d_value, gains[0:1, :], unit, spread_one)).astype(LOW)
    stack[...] = dot(back_t[...], d_input).astype(LOW)
    for image in range(4):
        out_tokens[image] = stack[64 * image : 64 * image + 49, :]

    def gather_rel(i, carry):
        start = 13 * (i // 7) + i % 7
        rows = rel_grads[pl.ds(i, 24, stride=64), :]
        return carry + pltpu.roll(jnp.concatenate([rows, jnp.zeros((24, 128), FULL)], axis=1), start, 1)

    rel_sum = lax.fori_loop(0, 49, gather_rel, jnp.zeros((24, 256), FULL))
    for k in range(3):
        sums[16:24, 256 * k : 256 * k + 256] = rel_sum[8 * k : 8 * k + 8, :]

    send(sums, got_core, S_AR, mate)
    run_three("f1")
    run_three("f2")
    got(sums, got_core, S_AR, mate)
    sums_one[...] = sums[...] + got_core[...]
    for k in (1, 2, 3):
        send(sums_one, got_wide.at[k - 1], S_AR + k, beside[k])
    run_two("q", wait_one("q"))
    for k in (1, 2, 3):
        got(sums_one, got_wide.at[k - 1], S_AR + k, beside[k])
    sums_two[...] = (sums_one[...] + got_wide[0]) + (got_wide[1] + got_wide[2])
    for k in (1, 2, 3):
        send(sums_two, got_narrow.at[k - 1], S_AR + 3 + k, along[k])
    run_four("f1")
    run_four("f2")
    finish("f1", out_f1)
    finish("f2", out_f2)
    for k in (1, 2, 3):
        got(sums_two, got_narrow.at[k - 1], S_AR + 3 + k, along[k])
    out_small[...] = (sums_two[...] + got_narrow[0]) + (got_narrow[1] + got_narrow[2])
    run_three("q")
    run_four("q")
    finish("q", out_qp)

    for args in pending:
        copy_of(*args).wait_send()

    def left_six(t, carry):
        for args in att_copies(t) + res_copies(t):
            copy_of(*args).wait_send()
        return carry

    lax.fori_loop(0, 6, left_six, 0)

    def left_three(n, carry):
        for args in win_copies(n):
            copy_of(*args).wait_send()
        return carry

    lax.fori_loop(0, 3, left_three, 0)

    def left_four(r, carry):
        for args in mlp_copies(r):
            copy_of(*args).wait_send()
        for route in range(2):
            for slot in range(2):
                copy_of(*step_one_f2(route, slot, r)).wait_send()
        return carry

    lax.fori_loop(0, 4, left_four, 0)
    for n in range(4):
        copy_of(*pack_copy(n)).wait_send()
    for route in range(2):
        for slot in range(2):
            copy_of(*step_one("f1", route, slot)).wait_send()


def fused_on_device(
    tokens, cotangent, crops, labels, norm_gains, biases, rel_table, w_qkv, w_proj, w_fc1, fc1_bias, w_fc2
):
    images, _, patches, model = tokens.shape
    hidden = w_fc1.shape[1]
    heads = rel_table.shape[1]
    vmem = pl.BlockSpec(memory_space=pltpu.VMEM)
    hbm = pl.BlockSpec(memory_space=pl.ANY)

    def low(*shape):
        return pltpu.VMEM(shape, LOW)

    def full(*shape):
        return pltpu.VMEM(shape, FULL)

    one_low = low(ROWS, model)
    one_t = low(model, ROWS)
    scratch = dict(
        wq=low(*w_qkv.shape),
        wp=low(*w_proj.shape),
        w1=low(*w_fc1.shape),
        w2=low(*w_fc2.shape),
        stack=low(256, model),
        stack_two=low(256, model),
        x_own=full(ROWS, model),
        g_low=one_low,
        g_t=one_t,
        g_tp=one_t,
        h1=one_low,
        xw=one_low,
        xw_t=one_t,
        xw_tp=one_t,
        query=one_low,
        key=low(KEYS, model),
        value=low(KEYS, model),
        bias_mask=full(heads, ROWS, KEYS),
        probs=low(heads, ROWS, KEYS),
        att=one_low,
        att_own=one_low,
        att_t=one_t,
        att_tp=one_t,
        middle=full(ROWS, model),
        h2=one_low,
        h2_t=one_t,
        h2_tp=one_t,
        act=low(ROWS, hidden),
        act_p=low(ROWS, hidden),
        dh=low(ROWS, hidden),
        dh_p=low(ROWS, hidden),
        gf1=low(4, 2, 4, 96, 384),
        gf2=low(4, 2, 4, 48, 768),
        gq=low(4, 2, 4, 96, 384),
        r1f1=low(2, 2, 4, 96, 384),
        r1f2=low(2, 2, 4, 48, 768),
        r1q=low(2, 2, 4, 96, 384),
        r2f1=low(2, 4, 96, 384),
        r2f2=low(2, 4, 48, 768),
        r2q=low(2, 4, 96, 384),
        r3f1=low(2, 2, 96, 384),
        r3f2=low(2, 2, 48, 768),
        r3q=low(2, 2, 96, 384),
        r4f1=low(2, 96, 384),
        r4f2=low(2, 48, 768),
        r4q=low(2, 96, 384),
        d_mid=full(ROWS, model),
        d_branch=one_low,
        db_pack=low(ROWS, 1024),
        db_pack_p=low(ROWS, 1024),
        d_res=one_low,
        d_att=one_low,
        d_proj=low(ROWS, 3 * model),
        dy_pack=low(ROWS, 3072),
        dy_pack_p=low(ROWS, 3072),
        d_win=one_low,
        d_own=one_low,
        rel_rows=full(64 * 24, 128),
        rel_grads=full(64 * 24, 128),
        rel_pad=full(256, 128),
        mask_add=full(ROWS, KEYS),
        valid_col=full(ROWS, 1),
        sums=full(24, 768),
        sums_one=full(24, 768),
        sums_two=full(24, 768),
        got_core=full(24, 768),
        got_wide=full(3, 24, 768),
        got_narrow=full(3, 24, 768),
        local_sem=pltpu.SemaphoreType.DMA((4,)),
        send_sem=pltpu.SemaphoreType.DMA((S_COUNT,)),
        recv_sem=pltpu.SemaphoreType.DMA((S_COUNT,)),
    )
    tables = [jnp.asarray(table) for table in place_tables()]
    result, grad_tokens, grad_qp, grad_f1, grad_f2, small = pl.pallas_call(
        block_kernel,
        out_shape=(
            jax.ShapeDtypeStruct((images, patches, model), LOW),
            jax.ShapeDtypeStruct((images, patches, model), LOW),
            jax.ShapeDtypeStruct((2, 96, 384), FULL),
            jax.ShapeDtypeStruct((2, 96, 384), FULL),
            jax.ShapeDtypeStruct((2, 48, 768), FULL),
            jax.ShapeDtypeStruct((24, 768), FULL),
        ),
        in_specs=[vmem] * 7 + [hbm] * 3 + [vmem, hbm] + [vmem] * 7,
        out_specs=[vmem] * 6,
        scratch_shapes=list(scratch.values()),
        compiler_params=pltpu.CompilerParams(
            collective_id=0, has_side_effects=True, vmem_limit_bytes=VMEM_LIMIT
        ),
    )(
        tokens[:, 0],
        cotangent[:, 0],
        crops,
        labels[:, 0],
        norm_gains,
        biases,
        rel_table,
        w_qkv,
        w_proj,
        w_fc1,
        fc1_bias.reshape(1, hidden),
        w_fc2,
        *tables,
    )
    grad_qp = grad_qp.reshape(192, 384)
    table = small[16:24].reshape(8, 3, 256).transpose(1, 0, 2).reshape(24, 256)[:, :169].T
    stats = jnp.sqrt(small[12, 1:4] / (model * small[12, 0]))
    return (
        result[:, None],
        grad_tokens[:, None],
        grad_qp[:, :288],
        grad_qp[:, 288:],
        grad_f1.reshape(192, 384),
        grad_f2.reshape(96, 768).T,
        small[0:2],
        small[2:8],
        small[8:12].reshape(hidden),
        table,
        stats,
    )


VMEM_LIMIT = 62 * 1024 * 1024


def fused(mesh):
    each = P("wide", "narrow", None, None)
    cut = P("narrow", "wide")
    return jax.shard_map(
        fused_on_device,
        mesh=mesh,
        in_specs=(each, each, P("wide", None), P("wide", "narrow", None)) + (P(),) * 8,
        out_specs=(each, each) + (cut,) * 4 + (P(),) * 5,
        check_vma=False,
    )


def solution(mesh):
    if mesh.shape["wide"] == 8 and mesh.shape["narrow"] == 4:
        return fused(mesh)
    return plain(mesh)
```

```python
from functools import partial

import jax
import jax.numpy as jnp
import numpy as np
from jax import lax
from jax.experimental import pallas as pl
from jax.experimental.pallas import tpu as pltpu
from jax.sharding import PartitionSpec as P


def from_partner(shard, axis, stride):
    return lax.ppermute(shard, axis, [(i, i ^ 1 << stride) for i in range(lax.axis_size(axis))])


def layer_norm(values, gain, shift):
    centre = jnp.mean(values, axis=-1, keepdims=True)
    centred = values - centre
    spread = jnp.mean(centred * centred, axis=-1, keepdims=True)
    return centred * lax.rsqrt(spread + 1e-05) * gain + shift


def into_window(field, swap_rows, swap_cols):
    tall = jnp.concatenate([field[:, 3:], swap_rows(field[:, :3])], axis=1)
    return jnp.concatenate([tall[:, :, 3:], swap_cols(tall[:, :, :3])], axis=2)


def out_of_window(field, swap_rows, swap_cols):
    broad = jnp.concatenate([swap_cols(field[:, :, 4:]), field[:, :, :4]], axis=2)
    return jnp.concatenate([swap_rows(broad[:, 4:]), broad[:, :4]], axis=1)


def relative_index():
    positions = jnp.arange(49, dtype=jnp.int32)
    inner_rows = positions // 7
    inner_cols = positions % 7
    return (
        (inner_rows[:, None] - inner_rows[None, :] + 6) * 13
        + inner_cols[:, None]
        - inner_cols[None, :]
        + 6
    )


def column_sum(values):
    return jnp.sum(values, axis=0, dtype=jnp.float32)


def on_device(
    tokens,
    cotangent,
    crops,
    labels,
    norm_gains,
    biases,
    rel_table,
    w_qkv,
    w_proj,
    w_fc1,
    fc1_bias,
    w_fc2,
):
    images = tokens.shape[0]
    model_width = tokens.shape[-1]
    head_count = rel_table.shape[1]
    head_size = model_width // head_count
    rows_all = images * 49
    score_scale = head_size ** (-0.5)
    where_narrow = lax.axis_index("narrow")
    row_half = where_narrow // 2
    col_half = where_narrow % 2
    positions = jnp.arange(49, dtype=jnp.int32)
    own_row = 7 * row_half + positions // 7
    own_col = 7 * col_half + positions % 7
    shift_row = (own_row + 3) % 14
    shift_col = (own_col + 3) % 14
    valid_own = (own_row[None] < crops[:, 0:1]) & (own_col[None] < crops[:, 1:2])
    valid_shift = (shift_row[None] < crops[:, 0:1]) & (shift_col[None] < crops[:, 1:2])
    label_rows = labels[:, 0]
    allowed = (label_rows[:, :, None] == label_rows[:, None, :]) & valid_shift[
        :, None, :
    ] | jnp.eye(49, dtype=bool)[None]
    allowed_heads = allowed[:, None]
    inputs = tokens[:, 0].astype(jnp.float32)
    normed, ln1_back = jax.vjp(layer_norm, inputs, norm_gains[0], biases[4])
    normed_low = normed.astype(jnp.bfloat16).reshape(images, 7, 7, model_width)
    windows = into_window(
        normed_low,
        lambda strip: from_partner(strip, "narrow", 1),
        lambda strip: from_partner(strip, "narrow", 0),
    ).reshape(rows_all, model_width)
    projected = jnp.dot(windows, w_qkv, preferred_element_type=jnp.float32)
    head_shape = (images, 49, head_count, head_size)
    query_rows = (projected[:, :model_width] + biases[0]).astype(jnp.bfloat16).reshape(head_shape)
    key_rows = projected[:, model_width : 2 * model_width].astype(jnp.bfloat16).reshape(head_shape)
    value_rows = (
        (projected[:, 2 * model_width :] + biases[1]).astype(jnp.bfloat16).reshape(head_shape)
    )
    one_hot = (
        (relative_index()[:, :, None] == jnp.arange(169, dtype=jnp.int32))
        .reshape(2401, 169)
        .astype(jnp.float32)
    )
    bias_table = (
        jnp.dot(one_hot, rel_table, precision=lax.Precision.HIGHEST)
        .reshape(49, 49, head_count)
        .transpose(2, 0, 1)
    )

    def masked_scores():
        raw = jnp.einsum(
            "nphe,nqhe->nhpq", query_rows, key_rows, preferred_element_type=jnp.float32
        )
        return jnp.where(allowed_heads, raw * score_scale + bias_table[None], -1000000000.0)

    masked = masked_scores()
    row_top = jnp.max(masked, axis=-1, keepdims=True)
    log_total = row_top + jnp.log(jnp.sum(jnp.exp(masked - row_top), axis=-1, keepdims=True))
    attn_probs = jnp.exp(masked - log_total)
    probs_low = attn_probs.astype(jnp.bfloat16)
    attended = jnp.einsum(
        "nhpq,nqhe->nphe", probs_low, value_rows, preferred_element_type=jnp.float32
    ).astype(jnp.bfloat16)
    restored = out_of_window(
        attended.reshape(images, 7, 7, model_width),
        lambda strip: from_partner(strip, "narrow", 1),
        lambda strip: from_partner(strip, "narrow", 0),
    ).reshape(rows_all, model_width)
    branch_attn = jnp.dot(restored, w_proj, preferred_element_type=jnp.float32) + biases[2]
    middle = inputs.reshape(rows_all, model_width) + branch_attn
    normed_two, ln2_back = jax.vjp(layer_norm, middle, norm_gains[1], biases[5])
    normed_two_low = normed_two.astype(jnp.bfloat16)
    hidden = jnp.dot(normed_two_low, w_fc1, preferred_element_type=jnp.float32) + fc1_bias
    activated, gelu_back = jax.vjp(partial(jax.nn.gelu, approximate=False), hidden)
    activated_low = activated.astype(jnp.bfloat16)
    branch_mlp = jnp.dot(activated_low, w_fc2, preferred_element_type=jnp.float32) + biases[3]
    result = (middle + branch_mlp).astype(jnp.bfloat16).reshape(images, 1, 49, model_width)
    cot_rows = cotangent.reshape(rows_all, model_width)
    grad_fc2 = jnp.dot(activated_low.T, cot_rows, preferred_element_type=jnp.float32)
    d_activated = jnp.dot(cot_rows, w_fc2.T, preferred_element_type=jnp.float32)
    (d_hidden,) = gelu_back(d_activated)
    d_hidden_low = d_hidden.astype(jnp.bfloat16)
    grad_fc1 = jnp.dot(normed_two_low.T, d_hidden_low, preferred_element_type=jnp.float32)
    grad_fc1_bias = column_sum(d_hidden_low)
    d_normed_two = jnp.dot(d_hidden_low, w_fc1.T, preferred_element_type=jnp.float32)
    d_middle_norm, d_gain_two, d_shift_two = ln2_back(d_normed_two)
    d_middle = cot_rows.astype(jnp.float32) + d_middle_norm
    d_branch = d_middle.astype(jnp.bfloat16)
    grad_proj = jnp.dot(restored.T, d_branch, preferred_element_type=jnp.float32)
    d_restored = jnp.dot(d_branch, w_proj.T, preferred_element_type=jnp.float32).astype(
        jnp.bfloat16
    )
    d_attended = into_window(
        d_restored.reshape(images, 7, 7, model_width),
        lambda strip: from_partner(strip, "narrow", 1),
        lambda strip: from_partner(strip, "narrow", 0),
    ).reshape(head_shape)
    again = jnp.exp(masked_scores() - log_total)
    d_probs = jnp.einsum(
        "nphe,nqhe->nhpq", d_attended, value_rows, preferred_element_type=jnp.float32
    )
    d_scores = (again * (d_probs - jnp.sum(again * d_probs, axis=-1, keepdims=True))).astype(
        jnp.bfloat16
    )
    d_table = jnp.sum(d_scores, axis=0, dtype=jnp.float32).reshape(head_count, 2401)
    grad_rel = jnp.dot(d_table, one_hot, precision=lax.Precision.HIGHEST).T
    d_query = (
        jnp.einsum("nhpq,nqhe->nphe", d_scores, key_rows, preferred_element_type=jnp.float32)
        * score_scale
    ).astype(jnp.bfloat16)
    d_key = (
        jnp.einsum("nhpq,nphe->nqhe", d_scores, query_rows, preferred_element_type=jnp.float32)
        * score_scale
    ).astype(jnp.bfloat16)
    d_value = jnp.einsum(
        "nhpq,nphe->nqhe", probs_low, d_attended, preferred_element_type=jnp.float32
    ).astype(jnp.bfloat16)
    d_projected = jnp.concatenate(
        [
            d_query.reshape(rows_all, model_width),
            d_key.reshape(rows_all, model_width),
            d_value.reshape(rows_all, model_width),
        ],
        axis=1,
    )
    grad_qkv = jnp.dot(windows.T, d_projected, preferred_element_type=jnp.float32)
    d_windows = jnp.dot(d_projected, w_qkv.T, preferred_element_type=jnp.float32).astype(
        jnp.bfloat16
    )
    d_normed = out_of_window(
        d_windows.reshape(images, 7, 7, model_width),
        lambda strip: from_partner(strip, "narrow", 1),
        lambda strip: from_partner(strip, "narrow", 0),
    ).reshape(images, 49, model_width)
    d_inputs_norm, d_gain_one, d_shift_one = ln1_back(d_normed.astype(jnp.float32))
    grad_tokens = (
        (d_middle.reshape(images, 49, model_width) + d_inputs_norm)
        .astype(jnp.bfloat16)
        .reshape(images, 1, 49, model_width)
    )
    grad_biases = jnp.stack(
        [
            column_sum(d_query.reshape(rows_all, model_width)),
            column_sum(d_value.reshape(rows_all, model_width)),
            column_sum(d_branch),
            column_sum(cot_rows),
            d_shift_one,
            d_shift_two,
        ]
    )
    grad_gains = jnp.stack([d_gain_one, d_gain_two])
    valid_weight = valid_own.astype(jnp.float32).reshape(rows_all)
    flat_inputs = inputs.reshape(rows_all, model_width)
    stat_sums = jnp.stack(
        [
            jnp.sum(valid_weight),
            jnp.sum(valid_weight * jnp.sum(flat_inputs * flat_inputs, axis=-1)),
            jnp.sum(valid_weight * jnp.sum(branch_attn * branch_attn, axis=-1)),
            jnp.sum(valid_weight * jnp.sum(branch_mlp * branch_mlp, axis=-1)),
        ]
    )
    grad_biases, grad_gains, grad_fc1_bias, grad_rel, stat_sums = lax.psum(
        (grad_biases, grad_gains, grad_fc1_bias, grad_rel, stat_sums), ("wide", "narrow")
    )
    stats = jnp.sqrt(stat_sums[1:] / (model_width * stat_sums[0]))
    matrices = (grad_qkv, grad_proj, grad_fc1, grad_fc2)
    partial_sums = (
        lax.psum_scatter(matrices[0], "wide", scatter_dimension=1, tiled=True),
        lax.psum_scatter(matrices[1], "wide", scatter_dimension=1, tiled=True),
        lax.psum_scatter(matrices[2], "wide", scatter_dimension=1, tiled=True),
        lax.psum_scatter(matrices[3], "wide", scatter_dimension=1, tiled=True),
    )
    reduced = (
        lax.psum_scatter(
            partial_sums[0].astype(jnp.bfloat16), "narrow", scatter_dimension=0, tiled=True
        ).astype(jnp.float32),
        lax.psum_scatter(
            partial_sums[1].astype(jnp.bfloat16), "narrow", scatter_dimension=0, tiled=True
        ).astype(jnp.float32),
        lax.psum_scatter(
            partial_sums[2].astype(jnp.bfloat16), "narrow", scatter_dimension=0, tiled=True
        ).astype(jnp.float32),
        lax.psum_scatter(
            partial_sums[3].astype(jnp.bfloat16), "narrow", scatter_dimension=0, tiled=True
        ).astype(jnp.float32),
    )
    grad_qkv, grad_proj, grad_fc1, grad_fc2 = reduced
    return (
        result,
        grad_tokens,
        grad_qkv,
        grad_proj,
        grad_fc1,
        grad_fc2,
        grad_gains,
        grad_biases,
        grad_fc1_bias,
        grad_rel,
        stats,
    )


def plain(mesh):
    return jax.shard_map(
        on_device,
        mesh=mesh,
        in_specs=(
            P("wide", "narrow", None, None),
            P("wide", "narrow", None, None),
            P("wide", None),
            P("wide", "narrow", None),
            P(),
            P(),
            P(),
            P(),
            P(),
            P(),
            P(),
            P(),
        ),
        out_specs=(
            P("wide", "narrow", None, None),
            P("wide", "narrow", None, None),
            P("narrow", "wide"),
            P("narrow", "wide"),
            P("narrow", "wide"),
            P("narrow", "wide"),
            P(),
            P(),
            P(),
            P(),
            P(),
        ),
        check_vma=False,
    )


ROWS = 208
KEYS = 256
T_OWN, T_BACK, T_PICK, T_SPREAD, T_OFFSETS, T_GATHER, T_REPEAT = 0, 208, 464, 720, 928, 1184, 1248
TABLE_ROWS = 1504
MESH = pl.DeviceIdType.MESH
LOW = jnp.bfloat16
FULL = jnp.float32


def place_tables():
    places = []
    for tall, broad in ((0, 0), (1, 0), (0, 1), (1, 1)):
        for image in range(4):
            for i in range(4, 7) if tall else range(4):
                for j in range(4, 7) if broad else range(4):
                    places.append((image, i, j, i - 4 if tall else i + 3, j - 4 if broad else j + 3))
    own = np.zeros((ROWS, 256), np.float32)
    spread = np.zeros((ROWS, 128), np.float32)
    pick = np.zeros((256, 128), np.float32)
    repeat = np.zeros((KEYS, 64), np.float32)
    for spot in range(49):
        for lane in (spot, 64 + spot):
            pick[13 * (spot // 7) + spot % 7, lane] = 1
            pick[128 + 13 * (spot // 7) + spot % 7, lane] = 1
    gather = np.zeros((64, ROWS), np.float32)
    offsets = np.zeros((KEYS, 128), np.float32)
    info = np.zeros((ROWS, 8), np.int32)
    info[:, 3] = -1
    for row in range(ROWS):
        if row >= len(places):
            info[row, 0] = 4 + row - len(places)
            continue
        image, i, j, a, b = places[row]
        own[row, 4 * (7 * a + b) + image] = 1
        spread[row, 7 * i + j] = 1
        spread[row, 64 + 7 * i + j] = 1
        shift = (6 - i) * 13 + 6 - j
        repeat[row, 7 * i + j] = 1
        gather[7 * i + j, row] = 1
        offsets[row, shift] = 1
        info[row, :6] = (image, i, j, 7 * i + j, a, b)
    table = np.zeros((TABLE_ROWS, 256), np.float32)
    table[T_OWN : T_OWN + ROWS] = own
    table[T_BACK : T_BACK + 256, :ROWS] = own.T
    table[T_PICK : T_PICK + 256, :128] = pick
    table[T_REPEAT : T_REPEAT + KEYS, :64] = repeat
    table[T_SPREAD : T_SPREAD + ROWS, :128] = spread
    table[T_OFFSETS : T_OFFSETS + KEYS, :128] = offsets
    table[T_GATHER : T_GATHER + 64, :ROWS] = gather
    return table.astype(jnp.bfloat16), info


def dot(left, right):
    return jnp.dot(left, right, preferred_element_type=FULL)


def dot_t(left, right):
    return lax.dot_general(left, right, (((1,), (1,)), ((), ())), preferred_element_type=FULL)


def lanes(index, width):
    return pl.ds(pl.multiple_of(index * width, width), width)


def normed(values):
    centred = values - jnp.mean(values, axis=-1, keepdims=True)
    scale = lax.rsqrt(jnp.mean(centred * centred, axis=-1, keepdims=True) + 1e-05)
    return centred * scale, scale


def normed_back(grad, gain, unit, scale):
    inner = grad * gain
    along = jnp.mean(inner, axis=-1, keepdims=True)
    across = jnp.mean(inner * unit, axis=-1, keepdims=True)
    return scale * (inner - along - unit * across)


def sum_rows(values):
    return jnp.sum(values, axis=0, keepdims=True)


GROUPS = ((64, 48), (112, 48), (160, 48))

S_TOK = 0
S_COT = 3
S_RES = 6
S_GRAD = 9
S_GT = 12
S_XWT = 13
S_AOT = 14
S_H2T = 15
S_ACT = 16
S_DH = 20
S_DBK = 24
S_DYK = 25
S_AR = 26
S_F1 = 33
S_F2 = 51
S_Q = 69
S_COUNT = 87
OUTPUTS = 11
ROUTES = ((0, 0), (1, 0), (0, 1), (1, 1))


def block_kernel(
    tokens_hbm,
    cotangent_hbm,
    crops_hbm,
    labels_hbm,
    gains_hbm,
    biases_hbm,
    rel_hbm,
    wq_hbm,
    wp_hbm,
    w1_hbm,
    fc1_bias_hbm,
    w2_hbm,
    table_hbm,
    info_hbm,
    to_result,
    to_tokens,
    to_qkv,
    to_proj,
    to_f1,
    to_f2,
    to_gains,
    to_biases,
    to_fc1_bias,
    to_rel,
    to_stats,
    tokens,
    cotangent,
    crops,
    labels,
    gains,
    biases,
    rel_table,
    fc1_bias,
    table,
    info,
    out_result,
    out_tokens,
    out_qkv,
    out_proj,
    out_f1,
    out_f2,
    out_gains,
    out_biases,
    out_fc1_bias,
    out_rel,
    out_stats,
    wq,
    wp,
    w1,
    w2,
    stack,
    result_low,
    x_own,
    g_low,
    g_t,
    g_both,
    tok_own,
    tok_win,
    g_own,
    result_own,
    xw,
    xw_t,
    query,
    key,
    value,
    key_bias,
    row_scale,
    probs,
    att,
    att_t,
    middle,
    h2,
    h2_t,
    act,
    dh,
    gf1,
    gf2,
    gq,
    r1f1,
    r1f2,
    r1q,
    r2f1,
    r2f2,
    r2q,
    r3f1,
    r3f2,
    r3q,
    r4f1,
    r4f2,
    r4q,
    d_mid,
    d_branch,
    db_pack,
    d_att,
    d_proj,
    dy_pack,
    d_win,
    d_own,
    rel_rows,
    rel_grads,
    mask_add,
    valid_col,
    sums,
    sums_one,
    sums_two,
    got_core,
    got_wide,
    got_narrow,
    local_sem,
    send_sem,
    recv_sem,
):
    model = x_own.shape[1]
    width = lax.axis_index("wide")
    depth = lax.axis_index("narrow")
    core = width % 2
    mine = width // 2
    mate = {"wide": width ^ 1, "narrow": depth}
    beside = [None] + [{"wide": width ^ (2 * k), "narrow": depth} for k in (1, 2, 3)]
    along = [None] + [{"wide": width, "narrow": depth ^ k} for k in (1, 2, 3)]
    partners = [mate] + beside[1:] + along[1:]
    quadrant = (along[2], along[1], along[3])

    started = {}

    def copy_of(src, dst, index, device):
        return pltpu.make_async_remote_copy(
            src_ref=src,
            dst_ref=dst,
            send_sem=send_sem.at[index],
            recv_sem=recv_sem.at[index],
            device_id=device,
            device_id_type=MESH,
        )

    def send(*args):
        copy_of(*args).start()
        started[args[2]] = [lambda n: [args], 1, False]

    def got(*args):
        copy_of(*args).wait_recv()
        started[args[2]][2] = True

    def each(copies, count, act):
        def step(n, carry):
            for args in copies(n):
                act(copy_of(*args))
            return carry

        if count == 1:
            step(0, 0)
        else:
            lax.fori_loop(0, count, step, 0)

    def got_all(name):
        copies, count, _ = started[name]
        each(copies, count, lambda copy: copy.wait_recv())
        started[name][2] = True

    def leave():
        for copies, count, arrived in started.values():
            if not arrived:
                each(copies, count, lambda copy: copy.wait_recv())
        for copies, count, _ in started.values():
            each(copies, count, lambda copy: copy.wait_send())
        for copy in stores:
            copy.wait()

    barrier = pltpu.get_barrier_semaphore()
    for partner in partners:
        pl.semaphore_signal(barrier, inc=1, device_id=partner, device_id_type=MESH)
    pairs = ((wq_hbm, wq), (wp_hbm, wp), (w1_hbm, w1), (w2_hbm, w2))
    pairs += ((tokens_hbm, tokens), (table_hbm, table), (gains_hbm, gains), (biases_hbm, biases))
    pairs += ((cotangent_hbm, cotangent), (info_hbm, info), (crops_hbm, crops), (labels_hbm, labels))
    pairs += ((rel_hbm, rel_table), (fc1_bias_hbm, fc1_bias))
    loads = [pltpu.make_async_copy(src, dst, local_sem.at[k]) for k, (src, dst) in enumerate(pairs)]
    for load in loads[4:] + loads[:4]:
        load.start()
    own_t = table.at[pl.ds(T_OWN, ROWS), :]
    back_t = table.at[pl.ds(T_BACK, 256), pl.ds(0, ROWS)]
    pick_t = table.at[pl.ds(T_PICK, 256), pl.ds(0, 128)]
    repeat_t = table.at[pl.ds(T_REPEAT, KEYS), pl.ds(0, 64)]
    spread_t = table.at[pl.ds(T_SPREAD, ROWS), pl.ds(0, 128)]
    offsets_t = table.at[pl.ds(T_OFFSETS, KEYS), pl.ds(0, 128)]
    gather_t = table.at[pl.ds(T_GATHER, 64), pl.ds(0, ROWS)]

    def store(k, src, dst):
        copy = pltpu.make_async_copy(src, dst, local_sem.at[len(pairs) + k])
        copy.start()
        stores.append(copy)

    stores = []

    def in_places(source):
        stack[192:256, :] = jnp.zeros((64, model), FULL)
        for patch in range(49):
            stack[4 * patch : 4 * patch + 4, :] = source[patch].astype(FULL)
        return dot(own_t[...], stack[...].astype(LOW))

    def in_order(values, out):
        stack[...] = dot(back_t[...], values)
        for patch in range(49):
            out[patch] = stack[4 * patch : 4 * patch + 4, :].astype(LOW)

    def swap(src, dst, base):
        dst[0:64, :] = src[0:64, :]
        for k, (row, count) in enumerate(GROUPS):
            rows = pl.ds(row, count)
            send(src.at[rows], dst.at[rows], base + k, quadrant[k])

    def swapped(src, dst, base):
        for k, (row, count) in enumerate(GROUPS):
            rows = pl.ds(row, count)
            got(src.at[rows], dst.at[rows], base + k, quadrant[k])

    for load in loads[4:8]:
        load.wait()
    tok_own[...] = in_places(tokens).astype(LOW)
    pl.semaphore_wait(barrier, len(partners))
    swap(tok_own, tok_win, S_TOK)

    for load in loads[8:]:
        load.wait()
    g_value = in_places(cotangent)
    g_own[...] = g_value.astype(LOW)
    swap(g_own, g_low, S_COT)
    for buffer in (xw_t, att_t, h2_t):
        buffer[:, 128:256] = jnp.zeros((model, 128), LOW)
    for buffer in (act, dh, dy_pack.at[0], dy_pack.at[1], db_pack.at[0], db_pack.at[1]):
        for row in (ROWS, 256 + ROWS):
            buffer[row : row + 48, :] = jnp.zeros((48, buffer.shape[1]), LOW)
    g_t[...] = jnp.zeros_like(g_t)

    sums[...] = jnp.zeros_like(sums)
    sums[5:6, :] = sum_rows(g_value)

    row_half = depth // 2
    col_half = depth % 2
    image_col = info[:, 0:1]
    i_col = info[:, 1:2]
    j_col = info[:, 2:3]
    place_col = info[:, 3:4]
    zero_col = jnp.zeros((ROWS, 1), jnp.int32)
    crop_row = zero_col
    crop_col = zero_col
    label = jnp.zeros((ROWS, 1), FULL)
    lane49 = lax.broadcasted_iota(jnp.int32, (ROWS, 49), 1)
    for image in range(4):
        is_image = image_col == image
        crop_row = jnp.where(is_image, crops[0:1, image : image + 1], crop_row)
        crop_col = jnp.where(is_image, crops[1:2, image : image + 1], crop_col)
        picked = jnp.where(
            lane49 == place_col, labels[image : image + 1, :].astype(FULL), jnp.zeros((ROWS, 49), FULL)
        )
        label = jnp.where(is_image, jnp.sum(picked, axis=1, keepdims=True), label)
    shift_row = 7 * row_half + i_col + 3
    shift_row = jnp.where(shift_row >= 14, shift_row - 14, shift_row)
    shift_col = 7 * col_half + j_col + 3
    shift_col = jnp.where(shift_col >= 14, shift_col - 14, shift_col)
    valid_key = (shift_row < crop_row) & (shift_col < crop_col)
    valid_value = jnp.where(valid_key, 1.0, 0.0).astype(FULL)
    valid_col[...] = valid_value
    code = label + 8.0 * image_col.astype(FULL)
    key_code = jnp.where(valid_key, code, -1.0)
    diagonal = lax.broadcasted_iota(jnp.int32, (ROWS, KEYS), 0) == lax.broadcasted_iota(
        jnp.int32, (ROWS, KEYS), 1
    )
    key_row = jnp.sum(jnp.where(diagonal, key_code + 2.0, 0.0), axis=0, keepdims=True) - 2.0
    mask_add[...] = jnp.where((code == key_row) | diagonal, 0.0, -1000000000.0)

    rel_wide = jnp.concatenate([rel_table[...] * 32**0.5, jnp.zeros((24, 87), FULL)], axis=1)
    rel_rows[1176:1536, :] = jnp.zeros((360, 128), FULL)

    def shifted(spot, carry):
        start = 84 - 13 * (spot // 7) - spot % 7
        rel_rows[pl.ds(pl.multiple_of(24 * spot, 8), 24), :] = pltpu.roll(rel_wide, 256 - start, 1)[:, 0:128]
        return carry

    lax.fori_loop(0, 49, shifted, 0, unroll=7)

    def picked_rows(n, carry):
        rows = pl.ds(pl.multiple_of(168 * n, 8), 168)
        values = rel_rows[rows, :]
        high = values.astype(LOW)
        below = (values - high.astype(FULL)).astype(LOW)
        rel_rows[rows, :] = dot(jnp.concatenate([high, below], axis=1), pick_t[...])
        return carry

    lax.fori_loop(0, 7, picked_rows, 0)
    is_high = lax.broadcasted_iota(jnp.int32, (64, 128), 1) < 64

    def head_bias(head, carry):
        values = rel_rows[pl.ds(head, 64, stride=24), :]
        high = values.astype(LOW).astype(FULL)
        parts = jnp.where(is_high, high, values - high).astype(LOW)
        key_bias[head] = dot(repeat_t[...], parts).astype(LOW)
        return carry

    lax.fori_loop(0, 24, head_bias, 0, unroll=4)

    key[ROWS:KEYS, :] = jnp.zeros((KEYS - ROWS, model), LOW)
    value[ROWS:KEYS, :] = jnp.zeros((KEYS - ROWS, model), LOW)
    swapped(tok_own, tok_win, S_TOK)
    flat = tok_win[...].astype(FULL)
    x_own[...] = flat
    unit, _ = normed(flat)
    xw[...] = (unit * gains[0:1, :] + biases[4:5, :]).astype(LOW)
    stat_total = jnp.sum(valid_value, axis=0, keepdims=True)
    stat_input = sum_rows(valid_value * jnp.sum(flat * flat, axis=-1, keepdims=True))

    loads[0].wait()

    def project(n, carry):
        at = lanes(n, 256)
        window = xw[...]
        query[:, at] = (dot(window, wq[:, at]) + biases[0:1, at]).astype(LOW)
        key[0:ROWS, at] = dot(window, wq[:, lanes(n + 3, 256)]).astype(LOW)
        value[0:ROWS, at] = (dot(window, wq[:, lanes(n + 6, 256)]) + biases[1:2, at]).astype(LOW)
        return carry

    lax.fori_loop(0, 3, project, 0)

    lane_head = lax.broadcasted_iota(jnp.int32, (1, 128), 1) // 32
    only = [(lane_head == h).astype(FULL).astype(LOW) for h in range(4)]
    row_head = lax.broadcasted_iota(jnp.int32, (128, 1), 0) // 32
    only_row = [(row_head == h).astype(FULL).astype(LOW) for h in range(4)]
    scale = 32 ** (-0.5)

    def attend(t, carry):
        at = lanes(t, 128)
        q = query[:, at]
        k = key[:, at]
        v = value[:, at]
        powers = []
        right = []
        for h in range(4):
            left = jnp.concatenate([q * only[h], spread_t[...]], axis=1)
            scores = dot_t(left, jnp.concatenate([k, key_bias[4 * t + h]], axis=1)) + mask_add[...]
            top = jnp.max(scores, axis=-1, keepdims=True)
            power = jnp.exp2((scores - top) * (scale * 1.4426950408889634)).astype(LOW)
            probs[4 * t + h, 0:ROWS] = power
            probs[4 * t + h, ROWS:KEYS] = jnp.zeros((KEYS - ROWS, KEYS), LOW)
            powers.append(power)
            right.append(jnp.concatenate([v * only[h], jnp.ones((KEYS, 128), LOW) * only[h]], axis=1))
        both = dot(jnp.concatenate(powers, axis=1), jnp.concatenate(right, axis=0))
        total = both[:, 0:128]
        below = 1.0 / both[:, 128:256]
        row_scale[:, at] = below
        total = (total * below).astype(LOW)
        att[:, at] = total
        return carry

    lax.fori_loop(0, 6, attend, 0)

    def share(buffer, index):
        return buffer.at[:, pl.ds(0, 256)], buffer.at[:, pl.ds(256, 256)], index, mate

    xw_t[:, 0:ROWS] = xw[...].T
    send(*share(xw_t, S_XWT))

    swapped(g_own, g_low, S_COT)
    turned = g_low[...].T
    for j in range(8):
        g_t[j // 2, j % 2, :, 0:ROWS] = turned[96 * j : 96 * j + 96]
    g_both[:, :, 0:256] = g_t[:, core]
    send(g_t.at[:, 1 - core], g_both.at[:, :, pl.ds(256, 256)], S_GT, mate)
    att_t[:, 0:ROWS] = att[...].T
    send(*share(att_t, S_AOT))
    loads[1].wait()

    def attn_branch(n, carry):
        at = lanes(n, 256)
        branch = dot(att[...], wp[:, at]) + biases[2:3, at]
        middle[:, at] = x_own[:, at] + branch
        return carry + jnp.sum(branch * branch, axis=-1, keepdims=True)

    branch_square = lax.fori_loop(0, 3, attn_branch, jnp.zeros((ROWS, 1), FULL))
    stat_attn = sum_rows(valid_col[...] * branch_square)

    unit, _ = normed(middle[...])
    h2[...] = (unit * gains[1:2, :] + biases[5:6, :]).astype(LOW)
    h2_t[:, 0:ROWS] = h2[...].T
    send(*share(h2_t, S_H2T))
    loads[2].wait()
    loads[3].wait()

    def turn(r):
        return mine ^ jnp.where(r == 0, 3, jnp.where(r == 3, 0, r))

    def mlp_copies(r):
        at = lanes(turn(r), 768)
        return [
            (act.at[pl.ds(0, ROWS), at], act.at[pl.ds(256, ROWS), at], S_ACT + r, mate),
            (dh.at[pl.ds(0, ROWS), at], dh.at[pl.ds(256, ROWS), at], S_DH + r, mate),
        ]

    def hidden_quarter(r):
        quarter = turn(r)

        def hidden_part(n, carry):
            at = lanes(quarter * 3 + n, 256)
            hidden = dot(h2[...], w1[:, at]) + fc1_bias[:, at]
            d_act = dot_t(g_low[...], w2[at, :])
            below = 0.5 + 0.5 * lax.erf(hidden * 0.7071067811865476)
            act[0:ROWS, at] = (hidden * below).astype(LOW)
            slope = below + hidden * (0.3989422804014327 * jnp.exp(-0.5 * hidden * hidden))
            d_hidden = (slope * d_act).astype(LOW)
            dh[0:ROWS, at] = d_hidden
            sums[pl.ds(8 + quarter, 1), lanes(n, 256)] = sum_rows(d_hidden.astype(FULL))
            return carry

        lax.fori_loop(0, 3, hidden_part, 0, unroll=3)
        for args in mlp_copies(r):
            copy_of(*args).start()

    first = (beside[1], beside[2])
    second = (beside[2], beside[1])
    second_block = (mine ^ 2, mine ^ 1)
    groups = {"f1": (gf1, r1f1, r2f1, r3f1, r4f1, S_F1), "f2": (gf2, r1f2, r2f2, r3f2, r4f2, S_F2)}
    groups["q"] = (gq, r1q, r2q, r3q, r4q, S_Q)
    places = (depth ^ 3, depth ^ 1, depth ^ 2, depth)

    def step_one(name, route, slot):
        grads, landing, _, _, _, base = groups[name]
        block = mine ^ 3 if slot == 0 else mine ^ (1 + route)
        return grads.at[block, route], landing.at[route, slot], base + 2 * route + slot, first[route]

    def step_two(name, route, slot):
        grads, _, landing, _, _, base = groups[name]
        place = places[slot]
        return (
            grads.at[second_block[route], route, place],
            landing.at[route, place],
            base + 4 + 4 * route + slot,
            second[route],
        )

    def step_three(name, route, slot):
        grads, _, _, landing, _, base = groups[name]
        return (
            grads.at[mine, route, places[slot]],
            landing.at[route, slot],
            base + 12 + 2 * route + slot,
            along[1],
        )

    def step_four(name, route):
        grads, _, _, _, landing, base = groups[name]
        return grads.at[mine, route, depth ^ 2], landing.at[route], base + 16 + route, along[2]

    def begin(name):
        for route, slot in ROUTES:
            send(*step_one(name, route, slot))

    def grads_quarter(r):
        quarter = turn(r)
        for args in mlp_copies(r):
            copy_of(*args).wait_recv()
        at = lanes(2 * quarter + core, 384)

        total = dot(h2_t[...], dh[:, at])
        for n in range(4):
            for half in range(2):
                row = 192 * n + 96 * half
                gf1[quarter, half, n] = total[row : row + 96].astype(LOW)

        @pl.when(r == 0)
        def _():
            copy_of(*step_one("f1", 0, 0)).start()
            copy_of(*step_one("f1", 1, 0)).start()

        @pl.when(r == 1)
        def _():
            copy_of(*step_one("f1", 0, 1)).start()

        @pl.when(r == 2)
        def _():
            copy_of(*step_one("f1", 1, 1)).start()

        total = dot(g_both[...].reshape(384, 512), act[:, lanes(quarter, 768)])
        for n in range(4):
            for half in range(2):
                row = 96 * n + 48 * half
                gf2[n, half, quarter] = total[row : row + 48].astype(LOW)

    got(g_t.at[:, 1 - core], g_both.at[:, :, pl.ds(256, 256)], S_GT, mate)
    got(*share(h2_t, S_H2T))
    hidden_quarter(jnp.int32(0))

    def quarters(r, carry):
        hidden_quarter(r)
        grads_quarter(r - 1)
        return carry

    lax.fori_loop(1, 4, quarters, 0)
    grads_quarter(jnp.int32(3))
    started["mlp"] = [mlp_copies, 4, True]
    for route, slot in ROUTES:
        args = step_one("f1", route, slot)
        started[args[2]] = [lambda n, args=args: [args], 1, False]
    begin("f2")

    def d_normed_part(n, carry):
        at = lanes(n, 256)
        d_mid[:, at] = dot_t(dh[0:ROWS, :], w1[at, :])
        return carry

    lax.fori_loop(0, 3, d_normed_part, 0)
    unit, spread_two = normed(middle[...])
    d_normed = d_mid[...]
    sums[1:2, :] = sum_rows(d_normed * unit)
    sums[7:8, :] = sum_rows(d_normed)
    d_middle = g_low[...].astype(FULL) + normed_back(d_normed, gains[1:2, :], unit, spread_two)
    d_mid[...] = d_middle
    d_low = d_middle.astype(LOW)
    d_branch[...] = d_low
    sums[4:5, :] = sum_rows(d_low.astype(FULL))

    def d_res_part(n, carry):
        at = lanes(n, 256)
        d_att[:, at] = dot_t(d_branch[...], wp[at, :]).astype(LOW)
        return carry

    lax.fori_loop(0, 3, d_res_part, 0)

    for j in range(8):
        db_pack[j % 2, 0:ROWS, 128 * (j // 2) : 128 * (j // 2) + 128] = jnp.concatenate(
            [jnp.zeros((ROWS, 32), LOW), d_branch[:, 96 * j : 96 * j + 96]], axis=1
        )

    def share_pack(buffer, index):
        return buffer.at[1 - core, pl.ds(0, ROWS)], buffer.at[1 - core, pl.ds(256, ROWS)], index, mate

    send(*share_pack(db_pack, S_DBK))

    def add_in(grads, index, landing):
        grads[index] = (grads[index].astype(FULL) + landing[...].astype(FULL)).astype(LOW)

    def run_two(name):
        grads, landing, _, _, _, _ = groups[name]
        for route in range(2):
            got(*step_one(name, route, 0))
            for slot in range(4):
                place = places[slot]
                add_in(grads, (second_block[route], route, place), landing.at[route, 0, place])
                send(*step_two(name, route, slot))
        for route in range(2):
            got(*step_one(name, route, 1))

            def add(n, carry):
                add_in(grads, (mine, route, n), landing.at[route, 1, n])
                return carry

            lax.fori_loop(0, 4, add, 0)

    def run_three(name):
        grads, _, landing, _, _, _ = groups[name]
        for slot in range(4):
            for route in range(2):
                got(*step_two(name, route, slot))
                add_in(grads, (mine, route, places[slot]), landing.at[route, places[slot]])
                if slot < 2:
                    send(*step_three(name, route, slot))

    def run_four(name):
        grads, _, _, landing, _, _ = groups[name]
        for slot in range(2):
            for route in range(2):
                got(*step_three(name, route, slot))
                add_in(grads, (mine, route, places[2 + slot]), landing.at[route, slot])
                if slot == 0:
                    send(*step_four(name, route))

    def finish(name):
        grads, _, _, _, landing, _ = groups[name]
        for route in range(2):
            got(*step_four(name, route))
            total = grads[mine, route, depth].astype(FULL) + landing[route].astype(FULL)
            if name == "q":
                out_qkv[96 * route : 96 * route + 96, :] = total[:, 0:288]
                out_proj[96 * route : 96 * route + 96, :] = total[:, 288:384]
            elif name == "f1":
                out_f1[96 * route : 96 * route + 96, :] = total
            else:
                out_f2[48 * route : 48 * route + 48, :] = total

    def attend_back(t, carry):
        at = lanes(t, 128)
        q = query[:, at]
        k = key[:, at]
        v = value[:, at]
        d_out = d_att[:, at].astype(FULL) * row_scale[:, at]
        common = (d_out * att[:, at].astype(FULL)).astype(LOW)
        d_out = d_out.astype(LOW)
        rest = jnp.zeros((KEYS - ROWS, 128), LOW)
        q_t = jnp.concatenate([q, rest], axis=0).T
        d_out_t = jnp.concatenate([d_out, rest], axis=0).T
        all_scores = []
        right = jnp.concatenate([v, jnp.full((KEYS, 128), -1.0, LOW)], axis=1)
        for h in range(4):
            d_probs = dot_t(jnp.concatenate([d_out * only[h], common * only[h]], axis=1), right)
            low_probs = probs[4 * t + h, 0:ROWS]
            d_scores = (low_probs.astype(FULL) * d_probs).astype(LOW)
            all_scores.append(d_scores)
        d_query = dot(
            jnp.concatenate(all_scores, axis=1), jnp.concatenate([k * only[h] for h in range(4)], axis=0)
        )
        four = pl.ds(4 * t, 4)
        d_value = dot(
            jnp.concatenate([d_out_t * only_row[h] for h in range(4)], axis=1),
            probs[four].reshape(4 * KEYS, KEYS),
        )
        for h in range(4):
            probs[4 * t + h, 0:ROWS] = all_scores[h]
        d_key = dot(
            jnp.concatenate([q_t * only_row[h] for h in range(4)], axis=1),
            probs[four].reshape(4 * KEYS, KEYS),
        )
        d_query = (d_query * scale).astype(LOW)
        d_key = (d_key * scale).astype(LOW).T[0:ROWS]
        d_value = d_value.astype(LOW).T[0:ROWS]
        d_proj[:, at] = d_query
        d_proj[:, lanes(6 + t, 128)] = d_key
        d_proj[:, lanes(12 + t, 128)] = d_value
        sums[2:3, at] = sum_rows(d_query.astype(FULL))
        sums[3:4, at] = sum_rows(d_value.astype(FULL))
        return carry

    lax.fori_loop(0, 6, attend_back, 0)

    for j in range(8):
        dy_pack[j % 2, 0:ROWS, 384 * (j // 2) : 384 * (j // 2) + 384] = jnp.concatenate(
            [d_proj[:, 288 * j : 288 * j + 288], jnp.zeros((ROWS, 96), LOW)], axis=1
        )
    send(*share_pack(dy_pack, S_DYK))

    run_two("f1")

    def mlp_branch(n, carry):
        at = lanes(n, 256)
        branch = dot(act[0:ROWS, :], w2[:, at]) + biases[3:4, at]
        result_low[:, at] = (middle[:, at] + branch).astype(LOW)
        return carry + jnp.sum(branch * branch, axis=-1, keepdims=True)

    branch_square = lax.fori_loop(0, 3, mlp_branch, jnp.zeros((ROWS, 1), FULL))
    stat_mlp = sum_rows(valid_col[...] * branch_square)
    swap(result_low, result_own, S_RES)
    lane = lax.broadcasted_iota(jnp.int32, (1, 128), 1)
    stat_row = jnp.zeros((1, 128), FULL)
    for k, total in enumerate((stat_total, stat_input, stat_attn, stat_mlp)):
        stat_row = jnp.where(lane == k, total, stat_row)
    sums[12:13, 0:128] = stat_row

    def d_win_part(n, carry):
        at = lanes(n, 256)
        d_win[:, at] = dot_t(d_proj[...], wq[at, :]).astype(LOW)
        return carry

    lax.fori_loop(0, 3, d_win_part, 0)
    unit, spread_one = normed(x_own[...])
    d_normed = d_win[...].astype(FULL)
    sums[0:1, :] = sum_rows(d_normed * unit)
    sums[6:7, :] = sum_rows(d_normed)
    d_win[...] = (d_mid[...] + normed_back(d_normed, gains[0:1, :], unit, spread_one)).astype(LOW)
    swap(d_win, d_own, S_GRAD)

    got(*share(xw_t, S_XWT))
    got(*share(att_t, S_AOT))
    got(*share_pack(db_pack, S_DBK))
    got(*share_pack(dy_pack, S_DYK))

    def qp_block(block):
        total = dot(xw_t[...], dy_pack[core, :, lanes(block, 384)])
        more = dot(att_t[...], db_pack[core, :, lanes(block, 128)])
        for n in range(4):
            for half in range(2):
                row = 192 * n + 96 * half
                cut = slice(row, row + 96)
                gq[block, half, n, :, 0:256] = total[cut, 0:256].astype(LOW)
                gq[block, half, n, :, 256:384] = (total[cut, 256:384] + more[cut]).astype(LOW)

    for block in range(4):
        qp_block(block)

    run_two("f2")
    begin("q")
    def spread_rel(head, carry):
        rows = dot(gather_t[...], probs[head, 0:ROWS]).astype(LOW)
        rel_grads[pl.ds(pl.multiple_of(64 * head, 64), 64), :] = dot(rows, offsets_t[...])
        return carry

    lax.fori_loop(0, 24, spread_rel, 0, unroll=4)

    def gather_rel(i, carry):
        start = 13 * (i // 7) + i % 7
        rows = rel_grads[pl.ds(i, 24, stride=64), :]
        return carry + pltpu.roll(jnp.concatenate([rows, jnp.zeros((24, 128), FULL)], axis=1), start, 1)

    rel_sum = lax.fori_loop(0, 49, gather_rel, jnp.zeros((24, 256), FULL), unroll=7)
    for k in range(3):
        sums[16:24, 256 * k : 256 * k + 256] = rel_sum[8 * k : 8 * k + 8, :]

    send(sums, got_core, S_AR, mate)
    run_three("f1")
    swapped(result_low, result_own, S_RES)
    in_order(result_own[...], out_result)
    store(0, out_result, to_result)
    got(sums, got_core, S_AR, mate)
    sums_one[...] = sums[...] + got_core[...]
    for k in (1, 2, 3):
        send(sums_one, got_wide.at[k - 1], S_AR + k, beside[k])
    run_three("f2")
    swapped(d_win, d_own, S_GRAD)
    in_order(d_own[...], out_tokens)
    store(1, out_tokens, to_tokens)
    run_four("f1")
    finish("f1")
    store(2, out_f1, to_f1)
    run_two("q")
    run_four("f2")
    for k in (1, 2, 3):
        got(sums_one, got_wide.at[k - 1], S_AR + k, beside[k])
    sums_two[...] = (sums_one[...] + got_wide[0]) + (got_wide[1] + got_wide[2])
    for k in (1, 2, 3):
        send(sums_two, got_narrow.at[k - 1], S_AR + 3 + k, along[k])
    finish("f2")
    store(3, out_f2, to_f2)
    run_three("q")
    for k in (1, 2, 3):
        got(sums_two, got_narrow.at[k - 1], S_AR + 3 + k, along[k])
    small = (sums_two[...] + got_narrow[0]) + (got_narrow[1] + got_narrow[2])
    out_gains[...] = small[0:2]
    out_biases[...] = small[2:8]
    for k in range(4):
        out_fc1_bias[:, 768 * k : 768 * k + 768] = small[8 + k : 9 + k]
    for k in range(3):
        out_rel[8 * k : 8 * k + 8, :] = small[16:24, 256 * k : 256 * k + 169]
    out_stats[...] = jnp.sqrt(small[12:13, 1:4] / (model * small[12:13, 0:1]))
    for k, (src, dst) in enumerate(
        (
            (out_gains, to_gains),
            (out_biases, to_biases),
            (out_fc1_bias, to_fc1_bias),
            (out_rel, to_rel),
            (out_stats, to_stats),
        )
    ):
        store(4 + k, src, dst)
    run_four("q")
    finish("q")
    store(9, out_qkv, to_qkv)
    store(10, out_proj, to_proj)

    leave()


def fused_on_device(
    tokens, cotangent, crops, labels, norm_gains, biases, rel_table, w_qkv, w_proj, w_fc1, fc1_bias, w_fc2
):
    images, _, patches, model = tokens.shape
    hidden = w_fc1.shape[1]
    heads = rel_table.shape[1]
    vmem = pl.BlockSpec(memory_space=pltpu.VMEM)
    hbm = pl.BlockSpec(memory_space=pl.ANY)

    def low(*shape):
        return pltpu.VMEM(shape, LOW)

    def full(*shape):
        return pltpu.VMEM(shape, FULL)

    one_low = low(ROWS, model)
    one_t = low(model, ROWS)
    scratch = dict(
        wq=low(*w_qkv.shape),
        wp=low(*w_proj.shape),
        w1=low(*w_fc1.shape),
        w2=low(*w_fc2.shape),
        stack=full(256, model),
        result_low=one_low,
        x_own=full(ROWS, model),
        g_low=one_low,
        g_t=low(4, 2, 96, 256),
        g_both=low(4, 96, 512),
        tok_own=one_low,
        tok_win=one_low,
        g_own=one_low,
        result_own=one_low,
        xw=one_low,
        xw_t=low(model, 512),
        query=one_low,
        key=low(KEYS, model),
        value=low(KEYS, model),
        key_bias=low(heads, KEYS, 128),
        row_scale=full(ROWS, model),
        probs=low(heads, KEYS, KEYS),
        att=one_low,
        att_t=low(model, 512),
        middle=full(ROWS, model),
        h2=one_low,
        h2_t=low(model, 512),
        act=low(512, hidden),
        dh=low(512, hidden),
        gf1=low(4, 2, 4, 96, 384),
        gf2=low(4, 2, 4, 48, 768),
        gq=low(4, 2, 4, 96, 384),
        r1f1=low(2, 2, 4, 96, 384),
        r1f2=low(2, 2, 4, 48, 768),
        r1q=low(2, 2, 4, 96, 384),
        r2f1=low(2, 4, 96, 384),
        r2f2=low(2, 4, 48, 768),
        r2q=low(2, 4, 96, 384),
        r3f1=low(2, 2, 96, 384),
        r3f2=low(2, 2, 48, 768),
        r3q=low(2, 2, 96, 384),
        r4f1=low(2, 96, 384),
        r4f2=low(2, 48, 768),
        r4q=low(2, 96, 384),
        d_mid=full(ROWS, model),
        d_branch=one_low,
        db_pack=low(2, 512, 512),
        d_att=one_low,
        d_proj=low(ROWS, 3 * model),
        dy_pack=low(2, 512, 1536),
        d_win=one_low,
        d_own=one_low,
        rel_rows=full(64 * 24, 128),
        rel_grads=full(64 * 24, 128),
        mask_add=full(ROWS, KEYS),
        valid_col=full(ROWS, 1),
        sums=full(24, 768),
        sums_one=full(24, 768),
        sums_two=full(24, 768),
        got_core=full(24, 768),
        got_wide=full(3, 24, 768),
        got_narrow=full(3, 24, 768),
        local_sem=pltpu.SemaphoreType.DMA((32,)),
        send_sem=pltpu.SemaphoreType.DMA((S_COUNT,)),
        recv_sem=pltpu.SemaphoreType.DMA((S_COUNT,)),
    )
    shapes = (
        ((patches, images, model), LOW),
        ((patches, images, model), LOW),
        ((192, 288), FULL),
        ((192, 96), FULL),
        ((192, 384), FULL),
        ((96, 768), FULL),
        ((2, model), FULL),
        ((6, model), FULL),
        ((1, hidden), FULL),
        ((heads, 169), FULL),
        ((1, 3), FULL),
    )
    inputs = (
        ((patches, images, model), LOW),
        ((patches, images, model), LOW),
        ((2, images), jnp.int32),
        ((images, patches), jnp.int32),
        ((2, model), FULL),
        ((6, model), FULL),
        ((heads, 169), FULL),
        ((1, hidden), FULL),
        ((TABLE_ROWS, 256), LOW),
        ((ROWS, 8), jnp.int32),
    )
    outs = pl.pallas_call(
        block_kernel,
        out_shape=tuple(jax.ShapeDtypeStruct(*shape) for shape in shapes),
        in_specs=[hbm] * 14,
        out_specs=[hbm] * OUTPUTS,
        scratch_shapes=[pltpu.VMEM(*shape) for shape in inputs + shapes] + list(scratch.values()),
        compiler_params=pltpu.CompilerParams(
            collective_id=0, has_side_effects=True, vmem_limit_bytes=VMEM_LIMIT
        ),
    )(
        tokens[:, 0].transpose(1, 0, 2),
        cotangent[:, 0].transpose(1, 0, 2),
        crops.T,
        labels[:, 0],
        norm_gains,
        biases,
        rel_table.T,
        w_qkv,
        w_proj,
        w_fc1,
        fc1_bias.reshape(1, hidden),
        w_fc2,
        *[jnp.asarray(table) for table in place_tables()],
    )
    outs = pl.pallas_call(
        hand_over,
        out_shape=tuple(jax.ShapeDtypeStruct(*shape) for shape in shapes),
        in_specs=[hbm] * OUTPUTS,
        out_specs=[hbm] * OUTPUTS,
        scratch_shapes=[pltpu.VMEM(*shape) for shape in shapes]
        + [pltpu.SemaphoreType.DMA((2, OUTPUTS))],
    )(*outs)
    return (
        outs[0].transpose(1, 0, 2)[:, None],
        outs[1].transpose(1, 0, 2)[:, None],
        outs[2],
        outs[3],
        outs[4],
        outs[5].T,
        outs[6],
        outs[7],
        outs[8].reshape(hidden),
        outs[9].T,
        outs[10].reshape(3),
    )


def hand_over(*refs):
    sems = refs[-1]
    held = refs[2 * OUTPUTS : 3 * OUTPUTS]
    loads = [pltpu.make_async_copy(refs[k], held[k], sems.at[0, k]) for k in range(OUTPUTS)]
    stores = [pltpu.make_async_copy(held[k], refs[OUTPUTS + k], sems.at[1, k]) for k in range(OUTPUTS)]
    for load in loads:
        load.start()
    for load, store in zip(loads, stores):
        load.wait()
        store.start()
    for store in stores:
        store.wait()


VMEM_LIMIT = 62 * 1024 * 1024


def fused(mesh):
    each = P("wide", "narrow", None, None)
    cut = P("narrow", "wide")
    return jax.shard_map(
        fused_on_device,
        mesh=mesh,
        in_specs=(each, each, P("wide", None), P("wide", "narrow", None)) + (P(),) * 8,
        out_specs=(each, each) + (cut,) * 4 + (P(),) * 5,
        check_vma=False,
    )


def solution(mesh):
    if mesh.shape["wide"] == 8 and mesh.shape["narrow"] == 4:
        return fused(mesh)
    return plain(mesh)
```

```python
from functools import partial

import jax
import jax.numpy as jnp
import numpy as np
from jax import lax
from jax.experimental import pallas as pl
from jax.experimental.pallas import tpu as pltpu
from jax.sharding import PartitionSpec as P


def from_partner(shard, axis, stride):
    return lax.ppermute(shard, axis, [(i, i ^ 1 << stride) for i in range(lax.axis_size(axis))])


def layer_norm(values, gain, shift):
    centre = jnp.mean(values, axis=-1, keepdims=True)
    centred = values - centre
    spread = jnp.mean(centred * centred, axis=-1, keepdims=True)
    return centred * lax.rsqrt(spread + 1e-05) * gain + shift


def into_window(field, swap_rows, swap_cols):
    tall = jnp.concatenate([field[:, 3:], swap_rows(field[:, :3])], axis=1)
    return jnp.concatenate([tall[:, :, 3:], swap_cols(tall[:, :, :3])], axis=2)


def out_of_window(field, swap_rows, swap_cols):
    broad = jnp.concatenate([swap_cols(field[:, :, 4:]), field[:, :, :4]], axis=2)
    return jnp.concatenate([swap_rows(broad[:, 4:]), broad[:, :4]], axis=1)


def relative_index():
    positions = jnp.arange(49, dtype=jnp.int32)
    inner_rows = positions // 7
    inner_cols = positions % 7
    return (
        (inner_rows[:, None] - inner_rows[None, :] + 6) * 13
        + inner_cols[:, None]
        - inner_cols[None, :]
        + 6
    )


def column_sum(values):
    return jnp.sum(values, axis=0, dtype=jnp.float32)


def on_device(
    tokens,
    cotangent,
    crops,
    labels,
    norm_gains,
    biases,
    rel_table,
    w_qkv,
    w_proj,
    w_fc1,
    fc1_bias,
    w_fc2,
):
    images = tokens.shape[0]
    model_width = tokens.shape[-1]
    head_count = rel_table.shape[1]
    head_size = model_width // head_count
    rows_all = images * 49
    score_scale = head_size ** (-0.5)
    where_narrow = lax.axis_index("narrow")
    row_half = where_narrow // 2
    col_half = where_narrow % 2
    positions = jnp.arange(49, dtype=jnp.int32)
    own_row = 7 * row_half + positions // 7
    own_col = 7 * col_half + positions % 7
    shift_row = (own_row + 3) % 14
    shift_col = (own_col + 3) % 14
    valid_own = (own_row[None] < crops[:, 0:1]) & (own_col[None] < crops[:, 1:2])
    valid_shift = (shift_row[None] < crops[:, 0:1]) & (shift_col[None] < crops[:, 1:2])
    label_rows = labels[:, 0]
    allowed = (label_rows[:, :, None] == label_rows[:, None, :]) & valid_shift[
        :, None, :
    ] | jnp.eye(49, dtype=bool)[None]
    allowed_heads = allowed[:, None]
    inputs = tokens[:, 0].astype(jnp.float32)
    normed, ln1_back = jax.vjp(layer_norm, inputs, norm_gains[0], biases[4])
    normed_low = normed.astype(jnp.bfloat16).reshape(images, 7, 7, model_width)
    windows = into_window(
        normed_low,
        lambda strip: from_partner(strip, "narrow", 1),
        lambda strip: from_partner(strip, "narrow", 0),
    ).reshape(rows_all, model_width)
    projected = jnp.dot(windows, w_qkv, preferred_element_type=jnp.float32)
    head_shape = (images, 49, head_count, head_size)
    query_rows = (projected[:, :model_width] + biases[0]).astype(jnp.bfloat16).reshape(head_shape)
    key_rows = projected[:, model_width : 2 * model_width].astype(jnp.bfloat16).reshape(head_shape)
    value_rows = (
        (projected[:, 2 * model_width :] + biases[1]).astype(jnp.bfloat16).reshape(head_shape)
    )
    one_hot = (
        (relative_index()[:, :, None] == jnp.arange(169, dtype=jnp.int32))
        .reshape(2401, 169)
        .astype(jnp.float32)
    )
    bias_table = (
        jnp.dot(one_hot, rel_table, precision=lax.Precision.HIGHEST)
        .reshape(49, 49, head_count)
        .transpose(2, 0, 1)
    )

    def masked_scores():
        raw = jnp.einsum(
            "nphe,nqhe->nhpq", query_rows, key_rows, preferred_element_type=jnp.float32
        )
        return jnp.where(allowed_heads, raw * score_scale + bias_table[None], -1000000000.0)

    masked = masked_scores()
    row_top = jnp.max(masked, axis=-1, keepdims=True)
    log_total = row_top + jnp.log(jnp.sum(jnp.exp(masked - row_top), axis=-1, keepdims=True))
    attn_probs = jnp.exp(masked - log_total)
    probs_low = attn_probs.astype(jnp.bfloat16)
    attended = jnp.einsum(
        "nhpq,nqhe->nphe", probs_low, value_rows, preferred_element_type=jnp.float32
    ).astype(jnp.bfloat16)
    restored = out_of_window(
        attended.reshape(images, 7, 7, model_width),
        lambda strip: from_partner(strip, "narrow", 1),
        lambda strip: from_partner(strip, "narrow", 0),
    ).reshape(rows_all, model_width)
    branch_attn = jnp.dot(restored, w_proj, preferred_element_type=jnp.float32) + biases[2]
    middle = inputs.reshape(rows_all, model_width) + branch_attn
    normed_two, ln2_back = jax.vjp(layer_norm, middle, norm_gains[1], biases[5])
    normed_two_low = normed_two.astype(jnp.bfloat16)
    hidden = jnp.dot(normed_two_low, w_fc1, preferred_element_type=jnp.float32) + fc1_bias
    activated, gelu_back = jax.vjp(partial(jax.nn.gelu, approximate=False), hidden)
    activated_low = activated.astype(jnp.bfloat16)
    branch_mlp = jnp.dot(activated_low, w_fc2, preferred_element_type=jnp.float32) + biases[3]
    result = (middle + branch_mlp).astype(jnp.bfloat16).reshape(images, 1, 49, model_width)
    cot_rows = cotangent.reshape(rows_all, model_width)
    grad_fc2 = jnp.dot(activated_low.T, cot_rows, preferred_element_type=jnp.float32)
    d_activated = jnp.dot(cot_rows, w_fc2.T, preferred_element_type=jnp.float32)
    (d_hidden,) = gelu_back(d_activated)
    d_hidden_low = d_hidden.astype(jnp.bfloat16)
    grad_fc1 = jnp.dot(normed_two_low.T, d_hidden_low, preferred_element_type=jnp.float32)
    grad_fc1_bias = column_sum(d_hidden_low)
    d_normed_two = jnp.dot(d_hidden_low, w_fc1.T, preferred_element_type=jnp.float32)
    d_middle_norm, d_gain_two, d_shift_two = ln2_back(d_normed_two)
    d_middle = cot_rows.astype(jnp.float32) + d_middle_norm
    d_branch = d_middle.astype(jnp.bfloat16)
    grad_proj = jnp.dot(restored.T, d_branch, preferred_element_type=jnp.float32)
    d_restored = jnp.dot(d_branch, w_proj.T, preferred_element_type=jnp.float32).astype(
        jnp.bfloat16
    )
    d_attended = into_window(
        d_restored.reshape(images, 7, 7, model_width),
        lambda strip: from_partner(strip, "narrow", 1),
        lambda strip: from_partner(strip, "narrow", 0),
    ).reshape(head_shape)
    again = jnp.exp(masked_scores() - log_total)
    d_probs = jnp.einsum(
        "nphe,nqhe->nhpq", d_attended, value_rows, preferred_element_type=jnp.float32
    )
    d_scores = (again * (d_probs - jnp.sum(again * d_probs, axis=-1, keepdims=True))).astype(
        jnp.bfloat16
    )
    d_table = jnp.sum(d_scores, axis=0, dtype=jnp.float32).reshape(head_count, 2401)
    grad_rel = jnp.dot(d_table, one_hot, precision=lax.Precision.HIGHEST).T
    d_query = (
        jnp.einsum("nhpq,nqhe->nphe", d_scores, key_rows, preferred_element_type=jnp.float32)
        * score_scale
    ).astype(jnp.bfloat16)
    d_key = (
        jnp.einsum("nhpq,nphe->nqhe", d_scores, query_rows, preferred_element_type=jnp.float32)
        * score_scale
    ).astype(jnp.bfloat16)
    d_value = jnp.einsum(
        "nhpq,nphe->nqhe", probs_low, d_attended, preferred_element_type=jnp.float32
    ).astype(jnp.bfloat16)
    d_projected = jnp.concatenate(
        [
            d_query.reshape(rows_all, model_width),
            d_key.reshape(rows_all, model_width),
            d_value.reshape(rows_all, model_width),
        ],
        axis=1,
    )
    grad_qkv = jnp.dot(windows.T, d_projected, preferred_element_type=jnp.float32)
    d_windows = jnp.dot(d_projected, w_qkv.T, preferred_element_type=jnp.float32).astype(
        jnp.bfloat16
    )
    d_normed = out_of_window(
        d_windows.reshape(images, 7, 7, model_width),
        lambda strip: from_partner(strip, "narrow", 1),
        lambda strip: from_partner(strip, "narrow", 0),
    ).reshape(images, 49, model_width)
    d_inputs_norm, d_gain_one, d_shift_one = ln1_back(d_normed.astype(jnp.float32))
    grad_tokens = (
        (d_middle.reshape(images, 49, model_width) + d_inputs_norm)
        .astype(jnp.bfloat16)
        .reshape(images, 1, 49, model_width)
    )
    grad_biases = jnp.stack(
        [
            column_sum(d_query.reshape(rows_all, model_width)),
            column_sum(d_value.reshape(rows_all, model_width)),
            column_sum(d_branch),
            column_sum(cot_rows),
            d_shift_one,
            d_shift_two,
        ]
    )
    grad_gains = jnp.stack([d_gain_one, d_gain_two])
    valid_weight = valid_own.astype(jnp.float32).reshape(rows_all)
    flat_inputs = inputs.reshape(rows_all, model_width)
    stat_sums = jnp.stack(
        [
            jnp.sum(valid_weight),
            jnp.sum(valid_weight * jnp.sum(flat_inputs * flat_inputs, axis=-1)),
            jnp.sum(valid_weight * jnp.sum(branch_attn * branch_attn, axis=-1)),
            jnp.sum(valid_weight * jnp.sum(branch_mlp * branch_mlp, axis=-1)),
        ]
    )
    grad_biases, grad_gains, grad_fc1_bias, grad_rel, stat_sums = lax.psum(
        (grad_biases, grad_gains, grad_fc1_bias, grad_rel, stat_sums), ("wide", "narrow")
    )
    stats = jnp.sqrt(stat_sums[1:] / (model_width * stat_sums[0]))
    matrices = (grad_qkv, grad_proj, grad_fc1, grad_fc2)
    partial_sums = (
        lax.psum_scatter(matrices[0], "wide", scatter_dimension=1, tiled=True),
        lax.psum_scatter(matrices[1], "wide", scatter_dimension=1, tiled=True),
        lax.psum_scatter(matrices[2], "wide", scatter_dimension=1, tiled=True),
        lax.psum_scatter(matrices[3], "wide", scatter_dimension=1, tiled=True),
    )
    reduced = (
        lax.psum_scatter(
            partial_sums[0].astype(jnp.bfloat16), "narrow", scatter_dimension=0, tiled=True
        ).astype(jnp.float32),
        lax.psum_scatter(
            partial_sums[1].astype(jnp.bfloat16), "narrow", scatter_dimension=0, tiled=True
        ).astype(jnp.float32),
        lax.psum_scatter(
            partial_sums[2].astype(jnp.bfloat16), "narrow", scatter_dimension=0, tiled=True
        ).astype(jnp.float32),
        lax.psum_scatter(
            partial_sums[3].astype(jnp.bfloat16), "narrow", scatter_dimension=0, tiled=True
        ).astype(jnp.float32),
    )
    grad_qkv, grad_proj, grad_fc1, grad_fc2 = reduced
    return (
        result,
        grad_tokens,
        grad_qkv,
        grad_proj,
        grad_fc1,
        grad_fc2,
        grad_gains,
        grad_biases,
        grad_fc1_bias,
        grad_rel,
        stats,
    )


def plain(mesh):
    return jax.shard_map(
        on_device,
        mesh=mesh,
        in_specs=(
            P("wide", "narrow", None, None),
            P("wide", "narrow", None, None),
            P("wide", None),
            P("wide", "narrow", None),
            P(),
            P(),
            P(),
            P(),
            P(),
            P(),
            P(),
            P(),
        ),
        out_specs=(
            P("wide", "narrow", None, None),
            P("wide", "narrow", None, None),
            P("narrow", "wide"),
            P("narrow", "wide"),
            P("narrow", "wide"),
            P("narrow", "wide"),
            P(),
            P(),
            P(),
            P(),
            P(),
        ),
        check_vma=False,
    )


ROWS = 208
KEYS = 256
T_OWN, T_BACK, T_PICK, T_SPREAD, T_OFFSETS, T_GATHER, T_REPEAT = 0, 208, 464, 720, 928, 1184, 1248
TABLE_ROWS = 1504
MESH = pl.DeviceIdType.MESH
LOW = jnp.bfloat16
FULL = jnp.float32


def place_tables():
    places = []
    for tall, broad in ((0, 0), (1, 0), (0, 1), (1, 1)):
        for image in range(4):
            for i in range(4, 7) if tall else range(4):
                for j in range(4, 7) if broad else range(4):
                    places.append((image, i, j, i - 4 if tall else i + 3, j - 4 if broad else j + 3))
    own = np.zeros((ROWS, 256), np.float32)
    spread = np.zeros((ROWS, 128), np.float32)
    pick = np.zeros((256, 128), np.float32)
    repeat = np.zeros((KEYS, 64), np.float32)
    for spot in range(49):
        for lane in (spot, 64 + spot):
            pick[13 * (spot // 7) + spot % 7, lane] = 1
            pick[128 + 13 * (spot // 7) + spot % 7, lane] = 1
    gather = np.zeros((64, ROWS), np.float32)
    offsets = np.zeros((KEYS, 128), np.float32)
    info = np.zeros((ROWS, 8), np.int32)
    info[:, 3] = -1
    for row in range(ROWS):
        if row >= len(places):
            info[row, 0] = 4 + row - len(places)
            continue
        image, i, j, a, b = places[row]
        own[row, 4 * (7 * a + b) + image] = 1
        spread[row, 7 * i + j] = 1
        spread[row, 64 + 7 * i + j] = 1
        shift = (6 - i) * 13 + 6 - j
        repeat[row, 7 * i + j] = 1
        gather[7 * i + j, row] = 1
        offsets[row, shift] = 1
        info[row, :6] = (image, i, j, 7 * i + j, a, b)
    table = np.zeros((TABLE_ROWS, 256), np.float32)
    table[T_OWN : T_OWN + ROWS] = own
    table[T_BACK : T_BACK + 256, :ROWS] = own.T
    table[T_PICK : T_PICK + 256, :128] = pick
    table[T_REPEAT : T_REPEAT + KEYS, :64] = repeat
    table[T_SPREAD : T_SPREAD + ROWS, :128] = spread
    table[T_OFFSETS : T_OFFSETS + KEYS, :128] = offsets
    table[T_GATHER : T_GATHER + 64, :ROWS] = gather
    return table.astype(jnp.bfloat16), info


def dot(left, right):
    return jnp.dot(left, right, preferred_element_type=FULL)


def dot_t(left, right):
    return lax.dot_general(left, right, (((1,), (1,)), ((), ())), preferred_element_type=FULL)


def lanes(index, width):
    return pl.ds(pl.multiple_of(index * width, width), width)


def normed(values):
    centred = values - jnp.mean(values, axis=-1, keepdims=True)
    scale = lax.rsqrt(jnp.mean(centred * centred, axis=-1, keepdims=True) + 1e-05)
    return centred * scale, scale


def normed_back(grad, gain, unit, scale):
    inner = grad * gain
    along = jnp.mean(inner, axis=-1, keepdims=True)
    across = jnp.mean(inner * unit, axis=-1, keepdims=True)
    return scale * (inner - along - unit * across)


def sum_rows(values):
    return jnp.sum(values, axis=0, keepdims=True)


GROUPS = ((64, 48), (112, 48), (160, 48))

S_TOK = 0
S_COT = 3
S_RES = 6
S_GRAD = 9
S_GT = 12
S_XWT = 13
S_AOT = 14
S_H2T = 15
S_ACT = 16
S_DH = 20
S_DBK = 24
S_DYK = 25
S_AR = 26
S_F1 = 33
S_F2 = 51
S_Q = 75
S_COUNT = 93
OUTPUTS = 11
ROUTES = ((0, 0), (1, 0), (0, 1), (1, 1))


def block_kernel(
    tokens_hbm,
    cotangent_hbm,
    crops_hbm,
    labels_hbm,
    gains_hbm,
    biases_hbm,
    rel_hbm,
    wq_hbm,
    wp_hbm,
    w1_hbm,
    fc1_bias_hbm,
    w2_hbm,
    table_hbm,
    info_hbm,
    to_result,
    to_tokens,
    to_qkv,
    to_proj,
    to_f1,
    to_f2,
    to_gains,
    to_biases,
    to_fc1_bias,
    to_rel,
    to_stats,
    tokens,
    cotangent,
    crops,
    labels,
    gains,
    biases,
    rel_table,
    fc1_bias,
    table,
    info,
    out_result,
    out_tokens,
    out_qkv,
    out_proj,
    out_f1,
    out_f2,
    out_gains,
    out_biases,
    out_fc1_bias,
    out_rel,
    out_stats,
    wq,
    wp,
    w1,
    w2,
    stack,
    result_low,
    x_own,
    g_low,
    g_t,
    g_both,
    tok_own,
    tok_win,
    g_own,
    result_own,
    xw,
    xw_t,
    query,
    key,
    value,
    key_bias,
    row_scale,
    probs,
    att,
    att_t,
    middle,
    h2,
    h2_t,
    act,
    dh,
    gf1,
    gf2,
    rzf2,
    gq,
    r1f1,
    r1f2,
    r1q,
    r2f1,
    r2f2,
    r3f2,
    r2q,
    r3f1,
    r3q,
    r4f1,
    r4f2,
    r4q,
    d_mid,
    d_branch,
    db_pack,
    d_att,
    d_proj,
    dy_pack,
    d_win,
    d_own,
    rel_rows,
    rel_grads,
    mask_add,
    valid_col,
    sums,
    sums_one,
    sums_two,
    sums_three,
    got_core,
    got_wide,
    got_narrow,
    local_sem,
    send_sem,
    recv_sem,
):
    model = x_own.shape[1]
    width = lax.axis_index("wide")
    depth = lax.axis_index("narrow")
    core = width % 2
    mine = width // 2
    mate = {"wide": width ^ 1, "narrow": depth}
    beside = [None] + [{"wide": width ^ (2 * k), "narrow": depth} for k in (1, 2, 3)]
    along = [None] + [{"wide": width, "narrow": depth ^ k} for k in (1, 2, 3)]
    partners = [mate] + beside[1:] + along[1:]
    quadrant = (along[2], along[1], along[3])

    started = {}

    def copy_of(src, dst, index, device):
        return pltpu.make_async_remote_copy(
            src_ref=src,
            dst_ref=dst,
            send_sem=send_sem.at[index],
            recv_sem=recv_sem.at[index],
            device_id=device,
            device_id_type=MESH,
        )

    def send(*args):
        copy_of(*args).start()
        started[args[2]] = [lambda n: [args], 1, False]

    def got(*args):
        copy_of(*args).wait_recv()
        started[args[2]][2] = True

    def each(copies, count, act):
        def step(n, carry):
            for args in copies(n):
                act(copy_of(*args))
            return carry

        if count == 1:
            step(0, 0)
        else:
            lax.fori_loop(0, count, step, 0)

    def got_all(name):
        copies, count, _ = started[name]
        each(copies, count, lambda copy: copy.wait_recv())
        started[name][2] = True

    def leave():
        for copies, count, arrived in started.values():
            if not arrived:
                each(copies, count, lambda copy: copy.wait_recv())
        for copies, count, _ in started.values():
            each(copies, count, lambda copy: copy.wait_send())
        for copy in stores:
            copy.wait()

    barrier = pltpu.get_barrier_semaphore()
    for partner in partners:
        pl.semaphore_signal(barrier, inc=1, device_id=partner, device_id_type=MESH)
    pairs = ((wq_hbm, wq), (wp_hbm, wp), (w1_hbm, w1), (w2_hbm, w2))
    pairs += ((tokens_hbm, tokens), (table_hbm, table), (gains_hbm, gains), (biases_hbm, biases))
    pairs += ((cotangent_hbm, cotangent), (info_hbm, info), (crops_hbm, crops), (labels_hbm, labels))
    pairs += ((rel_hbm, rel_table), (fc1_bias_hbm, fc1_bias))
    loads = [pltpu.make_async_copy(src, dst, local_sem.at[k]) for k, (src, dst) in enumerate(pairs)]
    for load in loads[4:] + loads[:4]:
        load.start()
    own_t = table.at[pl.ds(T_OWN, ROWS), :]
    back_t = table.at[pl.ds(T_BACK, 256), pl.ds(0, ROWS)]
    pick_t = table.at[pl.ds(T_PICK, 256), pl.ds(0, 128)]
    repeat_t = table.at[pl.ds(T_REPEAT, KEYS), pl.ds(0, 64)]
    spread_t = table.at[pl.ds(T_SPREAD, ROWS), pl.ds(0, 128)]
    offsets_t = table.at[pl.ds(T_OFFSETS, KEYS), pl.ds(0, 128)]
    gather_t = table.at[pl.ds(T_GATHER, 64), pl.ds(0, ROWS)]

    def store(k, src, dst):
        copy = pltpu.make_async_copy(src, dst, local_sem.at[len(pairs) + k])
        copy.start()
        stores.append(copy)

    stores = []

    def in_places(source):
        stack[192:256, :] = jnp.zeros((64, model), FULL)
        for patch in range(49):
            stack[4 * patch : 4 * patch + 4, :] = source[patch].astype(FULL)
        return dot(own_t[...], stack[...].astype(LOW))

    def in_order(values, out):
        stack[...] = dot(back_t[...], values)
        for patch in range(49):
            out[patch] = stack[4 * patch : 4 * patch + 4, :].astype(LOW)

    def swap(src, dst, base):
        dst[0:64, :] = src[0:64, :]
        for k, (row, count) in enumerate(GROUPS):
            rows = pl.ds(row, count)
            send(src.at[rows], dst.at[rows], base + k, quadrant[k])

    def swapped(src, dst, base):
        for k, (row, count) in enumerate(GROUPS):
            rows = pl.ds(row, count)
            got(src.at[rows], dst.at[rows], base + k, quadrant[k])

    for load in loads[4:8]:
        load.wait()
    tok_own[...] = in_places(tokens).astype(LOW)
    pl.semaphore_wait(barrier, len(partners))
    swap(tok_own, tok_win, S_TOK)

    for load in loads[8:]:
        load.wait()
    g_value = in_places(cotangent)
    g_own[...] = g_value.astype(LOW)
    for buffer in (xw_t, att_t, h2_t):
        buffer[:, 128:256] = jnp.zeros((model, 128), LOW)
    for buffer in (act, dh, dy_pack.at[0], dy_pack.at[1], db_pack.at[0], db_pack.at[1]):
        for row in (ROWS, 256 + ROWS):
            buffer[row : row + 48, :] = jnp.zeros((48, buffer.shape[1]), LOW)
    g_t[...] = jnp.zeros_like(g_t)

    sums[...] = jnp.zeros_like(sums)
    sums[5:6, :] = sum_rows(g_value)

    row_half = depth // 2
    col_half = depth % 2
    image_col = info[:, 0:1]
    i_col = info[:, 1:2]
    j_col = info[:, 2:3]
    place_col = info[:, 3:4]
    zero_col = jnp.zeros((ROWS, 1), jnp.int32)
    crop_row = zero_col
    crop_col = zero_col
    label = jnp.zeros((ROWS, 1), FULL)
    lane49 = lax.broadcasted_iota(jnp.int32, (ROWS, 49), 1)
    for image in range(4):
        is_image = image_col == image
        crop_row = jnp.where(is_image, crops[0:1, image : image + 1], crop_row)
        crop_col = jnp.where(is_image, crops[1:2, image : image + 1], crop_col)
        picked = jnp.where(
            lane49 == place_col, labels[image : image + 1, :].astype(FULL), jnp.zeros((ROWS, 49), FULL)
        )
        label = jnp.where(is_image, jnp.sum(picked, axis=1, keepdims=True), label)
    shift_row = 7 * row_half + i_col + 3
    shift_row = jnp.where(shift_row >= 14, shift_row - 14, shift_row)
    shift_col = 7 * col_half + j_col + 3
    shift_col = jnp.where(shift_col >= 14, shift_col - 14, shift_col)
    valid_key = (shift_row < crop_row) & (shift_col < crop_col)
    valid_value = jnp.where(valid_key, 1.0, 0.0).astype(FULL)
    valid_col[...] = valid_value
    code = label + 8.0 * image_col.astype(FULL)
    key_code = jnp.where(valid_key, code, -1.0)
    diagonal = lax.broadcasted_iota(jnp.int32, (ROWS, KEYS), 0) == lax.broadcasted_iota(
        jnp.int32, (ROWS, KEYS), 1
    )
    key_row = jnp.sum(jnp.where(diagonal, key_code + 2.0, 0.0), axis=0, keepdims=True) - 2.0
    mask_add[...] = jnp.where((code == key_row) | diagonal, 0.0, -1000000000.0)

    rel_wide = jnp.concatenate([rel_table[...] * 32**0.5, jnp.zeros((24, 87), FULL)], axis=1)
    rel_rows[1176:1536, :] = jnp.zeros((360, 128), FULL)

    def shifted(spot, carry):
        start = 84 - 13 * (spot // 7) - spot % 7
        rel_rows[pl.ds(pl.multiple_of(24 * spot, 8), 24), :] = pltpu.roll(rel_wide, 256 - start, 1)[:, 0:128]
        return carry

    lax.fori_loop(0, 49, shifted, 0, unroll=7)

    def picked_rows(n, carry):
        rows = pl.ds(pl.multiple_of(168 * n, 8), 168)
        values = rel_rows[rows, :]
        high = values.astype(LOW)
        below = (values - high.astype(FULL)).astype(LOW)
        rel_rows[rows, :] = dot(jnp.concatenate([high, below], axis=1), pick_t[...])
        return carry

    lax.fori_loop(0, 7, picked_rows, 0)
    is_high = lax.broadcasted_iota(jnp.int32, (64, 128), 1) < 64

    def head_bias(head, carry):
        values = rel_rows[pl.ds(head, 64, stride=24), :]
        high = values.astype(LOW).astype(FULL)
        parts = jnp.where(is_high, high, values - high).astype(LOW)
        key_bias[head] = dot(repeat_t[...], parts).astype(LOW)
        return carry

    lax.fori_loop(0, 24, head_bias, 0, unroll=4)

    key[ROWS:KEYS, :] = jnp.zeros((KEYS - ROWS, model), LOW)
    value[ROWS:KEYS, :] = jnp.zeros((KEYS - ROWS, model), LOW)
    swapped(tok_own, tok_win, S_TOK)
    swap(g_own, g_low, S_COT)
    flat = tok_win[...].astype(FULL)
    x_own[...] = flat
    unit, _ = normed(flat)
    xw[...] = (unit * gains[0:1, :] + biases[4:5, :]).astype(LOW)
    stat_total = jnp.sum(valid_value, axis=0, keepdims=True)
    stat_input = sum_rows(valid_value * jnp.sum(flat * flat, axis=-1, keepdims=True))

    loads[0].wait()

    def project(n, carry):
        at = lanes(n, 256)
        window = xw[...]
        query[:, at] = (dot(window, wq[:, at]) + biases[0:1, at]).astype(LOW)
        key[0:ROWS, at] = dot(window, wq[:, lanes(n + 3, 256)]).astype(LOW)
        value[0:ROWS, at] = (dot(window, wq[:, lanes(n + 6, 256)]) + biases[1:2, at]).astype(LOW)
        return carry

    lax.fori_loop(0, 3, project, 0)

    lane_head = lax.broadcasted_iota(jnp.int32, (1, 128), 1) // 32
    only = [(lane_head == h).astype(FULL).astype(LOW) for h in range(4)]
    row_head = lax.broadcasted_iota(jnp.int32, (128, 1), 0) // 32
    only_row = [(row_head == h).astype(FULL).astype(LOW) for h in range(4)]
    scale = 32 ** (-0.5)

    def attend(t, carry):
        at = lanes(t, 128)
        q = query[:, at]
        k = key[:, at]
        v = value[:, at]
        powers = []
        right = []
        for h in range(4):
            left = jnp.concatenate([q * only[h], spread_t[...]], axis=1)
            scores = dot_t(left, jnp.concatenate([k, key_bias[4 * t + h]], axis=1)) + mask_add[...]
            top = jnp.max(scores, axis=-1, keepdims=True)
            power = jnp.exp2((scores - top) * (scale * 1.4426950408889634)).astype(LOW)
            probs[4 * t + h, 0:ROWS] = power
            probs[4 * t + h, ROWS:KEYS] = jnp.zeros((KEYS - ROWS, KEYS), LOW)
            powers.append(power)
            right.append(jnp.concatenate([v * only[h], jnp.ones((KEYS, 128), LOW) * only[h]], axis=1))
        both = dot(jnp.concatenate(powers, axis=1), jnp.concatenate(right, axis=0))
        total = both[:, 0:128]
        below = 1.0 / both[:, 128:256]
        row_scale[:, at] = below
        total = (total * below).astype(LOW)
        att[:, at] = total
        return carry

    lax.fori_loop(0, 6, attend, 0)

    def share(buffer, index):
        return buffer.at[:, pl.ds(0, 256)], buffer.at[:, pl.ds(256, 256)], index, mate

    xw_t[:, 0:ROWS] = xw[...].T
    send(*share(xw_t, S_XWT))

    swapped(g_own, g_low, S_COT)
    turned = g_low[...].T
    for j in range(8):
        g_t[j // 2, j % 2, :, 0:ROWS] = turned[96 * j : 96 * j + 96]
    g_both[:, :, 0:256] = g_t[:, core]
    send(g_t.at[:, 1 - core], g_both.at[:, :, pl.ds(256, 256)], S_GT, mate)
    att_t[:, 0:ROWS] = att[...].T
    send(*share(att_t, S_AOT))
    loads[1].wait()

    def attn_branch(n, carry):
        at = lanes(n, 256)
        branch = dot(att[...], wp[:, at]) + biases[2:3, at]
        middle[:, at] = x_own[:, at] + branch
        return carry + jnp.sum(branch * branch, axis=-1, keepdims=True)

    branch_square = lax.fori_loop(0, 3, attn_branch, jnp.zeros((ROWS, 1), FULL))
    stat_attn = sum_rows(valid_col[...] * branch_square)

    unit, _ = normed(middle[...])
    h2[...] = (unit * gains[1:2, :] + biases[5:6, :]).astype(LOW)
    h2_t[:, 0:ROWS] = h2[...].T
    send(*share(h2_t, S_H2T))
    loads[2].wait()
    loads[3].wait()

    def turn(r):
        return mine ^ jnp.where(r == 0, 3, jnp.where(r == 3, 0, r))

    def mlp_copies(r):
        at = lanes(turn(r), 768)
        return [
            (act.at[pl.ds(0, ROWS), at], act.at[pl.ds(256, ROWS), at], S_ACT + r, mate),
            (dh.at[pl.ds(0, ROWS), at], dh.at[pl.ds(256, ROWS), at], S_DH + r, mate),
        ]

    def hidden_quarter(r):
        quarter = turn(r)

        def hidden_part(n, carry):
            at = lanes(quarter * 3 + n, 256)
            hidden = dot(h2[...], w1[:, at]) + fc1_bias[:, at]
            d_act = dot_t(g_low[...], w2[at, :])
            below = 0.5 + 0.5 * lax.erf(hidden * 0.7071067811865476)
            act[0:ROWS, at] = (hidden * below).astype(LOW)
            slope = below + hidden * (0.3989422804014327 * jnp.exp(-0.5 * hidden * hidden))
            d_hidden = (slope * d_act).astype(LOW)
            dh[0:ROWS, at] = d_hidden
            sums[pl.ds(8 + quarter, 1), lanes(n, 256)] = sum_rows(d_hidden.astype(FULL))
            return carry

        lax.fori_loop(0, 3, hidden_part, 0, unroll=3)
        for args in mlp_copies(r):
            copy_of(*args).start()

    first = (beside[1], beside[2])
    second = (beside[2], beside[1])
    second_block = (mine ^ 2, mine ^ 1)
    groups = {"f1": (gf1, r1f1, r2f1, r3f1, r4f1, S_F1)}
    groups["q"] = (gq, r1q, r2q, r3q, r4q, S_Q)
    places = (depth ^ 3, depth ^ 1, depth ^ 2, depth)

    def step_one(name, route, slot):
        grads, landing, _, _, _, base = groups[name]
        block = mine ^ 3 if slot == 0 else mine ^ (1 + route)
        return grads.at[block, route], landing.at[route, slot], base + 2 * route + slot, first[route]

    def step_two(name, route, slot):
        grads, _, landing, _, _, base = groups[name]
        place = places[slot]
        return (
            grads.at[second_block[route], route, place],
            landing.at[route, place],
            base + 4 + 4 * route + slot,
            second[route],
        )

    def step_three(name, route, slot):
        grads, _, _, landing, _, base = groups[name]
        return (
            grads.at[mine, route, places[slot]],
            landing.at[route, slot],
            base + 12 + 2 * route + slot,
            along[1],
        )

    def step_four(name, route):
        grads, _, _, _, landing, base = groups[name]
        return grads.at[mine, route, depth ^ 2], landing.at[route], base + 16 + route, along[2]

    kept = (depth ^ 3, depth ^ 2, depth)

    def aside():
        return gf2.at[depth ^ 1], rzf2, S_F2, along[1]

    def f2_one(route, slot, k):
        block = mine ^ 3 if slot == 0 else mine ^ (1 + route)
        return (
            gf2.at[kept[k], block, route],
            r1f2.at[route, slot, k],
            S_F2 + 1 + 6 * slot + 3 * route + k,
            first[route],
        )

    def f2_two(route, k):
        return gf2.at[kept[k], second_block[route], route], r2f2.at[route, k], S_F2 + 13 + 3 * route + k, second[route]

    def f2_three(route):
        return gf2.at[kept[0], mine, route], r3f2.at[route], S_F2 + 19 + route, along[1]

    def f2_four(route):
        return gf2.at[kept[1], mine, route], r4f2.at[route], S_F2 + 21 + route, along[2]

    def f2_begin(*which):
        for slot in range(2):
            for k in which:
                for route in range(2):
                    send(*f2_one(route, slot, k))

    def begin(name, slot):
        for route in range(2):
            send(*step_one(name, route, slot))

    def grads_quarter(r):
        quarter = turn(r)
        for args in mlp_copies(r):
            copy_of(*args).wait_recv()
        at = lanes(2 * quarter + core, 384)

        total = dot(h2_t[...], dh[:, at])
        for n in range(4):
            for half in range(2):
                row = 192 * n + 96 * half
                gf1[quarter, half, n] = total[row : row + 96].astype(LOW)

        @pl.when(r == 0)
        def _():
            copy_of(*step_one("f1", 0, 0)).start()
            copy_of(*step_one("f1", 1, 0)).start()

        @pl.when(r == 1)
        def _():
            copy_of(*step_one("f1", 0, 1)).start()

        @pl.when(r == 2)
        def _():
            copy_of(*step_one("f1", 1, 1)).start()

        total = dot(g_both[...].reshape(384, 512), act[:, lanes(quarter, 768)])
        for n in range(4):
            for half in range(2):
                row = 96 * n + 48 * half
                gf2[quarter, n, half] = total[row : row + 48].astype(LOW)

        @pl.when(quarter == depth ^ 1)
        def _():
            copy_of(*aside()).start()


    got(g_t.at[:, 1 - core], g_both.at[:, :, pl.ds(256, 256)], S_GT, mate)
    got(*share(h2_t, S_H2T))
    hidden_quarter(jnp.int32(0))

    def quarters(r, carry):
        hidden_quarter(r)
        grads_quarter(r - 1)
        return carry

    lax.fori_loop(1, 4, quarters, 0)
    grads_quarter(jnp.int32(3))
    started["mlp"] = [mlp_copies, 4, True]
    for route, slot in ROUTES:
        args = step_one("f1", route, slot)
        started[args[2]] = [lambda n, args=args: [args], 1, False]
    started["aside"] = [lambda n: [aside()], 1, False]
    f2_begin(0, 1)

    def mlp_branch(n, carry):
        at = lanes(n, 256)
        branch = dot(act[0:ROWS, :], w2[:, at]) + biases[3:4, at]
        result_low[:, at] = (middle[:, at] + branch).astype(LOW)
        return carry + jnp.sum(branch * branch, axis=-1, keepdims=True)

    branch_square = lax.fori_loop(0, 3, mlp_branch, jnp.zeros((ROWS, 1), FULL))
    stat_mlp = sum_rows(valid_col[...] * branch_square)
    swap(result_low, result_own, S_RES)
    lane = lax.broadcasted_iota(jnp.int32, (1, 128), 1)
    stat_row = jnp.zeros((1, 128), FULL)
    for k, total in enumerate((stat_total, stat_input, stat_attn, stat_mlp)):
        stat_row = jnp.where(lane == k, total, stat_row)
    sums[12:13, 0:128] = stat_row

    def d_normed_part(n, carry):
        at = lanes(n, 256)
        d_mid[:, at] = dot_t(dh[0:ROWS, :], w1[at, :])
        return carry

    lax.fori_loop(0, 3, d_normed_part, 0)
    unit, spread_two = normed(middle[...])
    d_normed = d_mid[...]
    sums[1:2, :] = sum_rows(d_normed * unit)
    sums[7:8, :] = sum_rows(d_normed)
    d_middle = g_low[...].astype(FULL) + normed_back(d_normed, gains[1:2, :], unit, spread_two)
    d_mid[...] = d_middle
    d_low = d_middle.astype(LOW)
    d_branch[...] = d_low
    sums[4:5, :] = sum_rows(d_low.astype(FULL))

    def d_res_part(n, carry):
        at = lanes(n, 256)
        d_att[:, at] = dot_t(d_branch[...], wp[at, :]).astype(LOW)
        return carry

    lax.fori_loop(0, 3, d_res_part, 0)

    for j in range(8):
        db_pack[j % 2, 0:ROWS, 128 * (j // 2) : 128 * (j // 2) + 128] = jnp.concatenate(
            [jnp.zeros((ROWS, 32), LOW), d_branch[:, 96 * j : 96 * j + 96]], axis=1
        )

    def share_pack(buffer, index):
        return buffer.at[1 - core, pl.ds(0, ROWS)], buffer.at[1 - core, pl.ds(256, ROWS)], index, mate

    send(*share_pack(db_pack, S_DBK))

    def add_in(grads, index, landing):
        grads[index] = (grads[index].astype(FULL) + landing[...].astype(FULL)).astype(LOW)

    def run_two(name):
        grads, landing, _, _, _, _ = groups[name]
        for route in range(2):
            got(*step_one(name, route, 0))
            for slot in range(4):
                place = places[slot]
                add_in(grads, (second_block[route], route, place), landing.at[route, 0, place])
                send(*step_two(name, route, slot))

    def run_two_own(name):
        grads, landing, _, _, _, _ = groups[name]
        for route in range(2):
            got(*step_one(name, route, 1))

            def add(n, carry):
                add_in(grads, (mine, route, n), landing.at[route, 1, n])
                return carry

            lax.fori_loop(0, 4, add, 0)

    def f2_aside():
        got_all("aside")

        def add(block, carry):
            for route in range(2):
                add_in(gf2, (depth, block, route), rzf2.at[block, route])
            return carry

        lax.fori_loop(0, 4, add, 0)
        f2_begin(2)

    def f2_run_two(*which):
        for k in which:
            for route in range(2):
                got(*f2_one(route, 0, k))
                add_in(gf2, (kept[k], second_block[route], route), r1f2.at[route, 0, k])
                send(*f2_two(route, k))
        for k in which:
            for route in range(2):
                got(*f2_one(route, 1, k))
                add_in(gf2, (kept[k], mine, route), r1f2.at[route, 1, k])

    def f2_run_three(*which):
        for k in which:
            for route in range(2):
                got(*f2_two(route, k))
                add_in(gf2, (kept[k], mine, route), r2f2.at[route, k])
                if k == 0:
                    send(*f2_three(route))

    def f2_run_four():
        for route in range(2):
            got(*f2_three(route))
            add_in(gf2, (kept[1], mine, route), r3f2.at[route])
            send(*f2_four(route))

    def f2_finish():
        for route in range(2):
            got(*f2_four(route))
            out_f2[48 * route : 48 * route + 48, :] = gf2[depth, mine, route].astype(FULL) + r4f2[route].astype(FULL)

    def run_three(name):
        grads, _, landing, _, _, _ = groups[name]
        for slot in range(4):
            for route in range(2):
                got(*step_two(name, route, slot))
                add_in(grads, (mine, route, places[slot]), landing.at[route, places[slot]])
                if slot < 2:
                    send(*step_three(name, route, slot))

    def run_four(name):
        grads, _, _, landing, _, _ = groups[name]
        for slot in range(2):
            for route in range(2):
                got(*step_three(name, route, slot))
                add_in(grads, (mine, route, places[2 + slot]), landing.at[route, slot])
                if slot == 0:
                    send(*step_four(name, route))

    def finish(name):
        grads, _, _, _, landing, _ = groups[name]
        for route in range(2):
            got(*step_four(name, route))
            total = grads[mine, route, depth].astype(FULL) + landing[route].astype(FULL)
            if name == "q":
                out_qkv[96 * route : 96 * route + 96, :] = total[:, 0:288]
                out_proj[96 * route : 96 * route + 96, :] = total[:, 288:384]
            else:
                out_f1[96 * route : 96 * route + 96, :] = total

    def attend_back(t, carry):
        at = lanes(t, 128)
        q = query[:, at]
        k = key[:, at]
        v = value[:, at]
        d_out = d_att[:, at].astype(FULL) * row_scale[:, at]
        common = (d_out * att[:, at].astype(FULL)).astype(LOW)
        d_out = d_out.astype(LOW)
        rest = jnp.zeros((KEYS - ROWS, 128), LOW)
        q_t = jnp.concatenate([q, rest], axis=0).T
        d_out_t = jnp.concatenate([d_out, rest], axis=0).T
        all_scores = []
        right = jnp.concatenate([v, jnp.full((KEYS, 128), -1.0, LOW)], axis=1)
        for h in range(4):
            d_probs = dot_t(jnp.concatenate([d_out * only[h], common * only[h]], axis=1), right)
            low_probs = probs[4 * t + h, 0:ROWS]
            d_scores = (low_probs.astype(FULL) * d_probs).astype(LOW)
            all_scores.append(d_scores)
        d_query = dot(
            jnp.concatenate(all_scores, axis=1), jnp.concatenate([k * only[h] for h in range(4)], axis=0)
        )
        four = pl.ds(4 * t, 4)
        d_value = dot(
            jnp.concatenate([d_out_t * only_row[h] for h in range(4)], axis=1),
            probs[four].reshape(4 * KEYS, KEYS),
        )
        for h in range(4):
            probs[4 * t + h, 0:ROWS] = all_scores[h]
        d_key = dot(
            jnp.concatenate([q_t * only_row[h] for h in range(4)], axis=1),
            probs[four].reshape(4 * KEYS, KEYS),
        )
        d_query = (d_query * scale).astype(LOW)
        d_key = (d_key * scale).astype(LOW).T[0:ROWS]
        d_value = d_value.astype(LOW).T[0:ROWS]
        d_proj[:, at] = d_query
        d_proj[:, lanes(6 + t, 128)] = d_key
        d_proj[:, lanes(12 + t, 128)] = d_value
        sums[2:3, at] = sum_rows(d_query.astype(FULL))
        sums[3:4, at] = sum_rows(d_value.astype(FULL))
        return carry

    run_two("f1")
    lax.fori_loop(0, 6, attend_back, 0)

    for j in range(8):
        dy_pack[j % 2, 0:ROWS, 384 * (j // 2) : 384 * (j // 2) + 384] = jnp.concatenate(
            [d_proj[:, 288 * j : 288 * j + 288], jnp.zeros((ROWS, 96), LOW)], axis=1
        )
    send(*share_pack(dy_pack, S_DYK))

    def d_win_part(n, carry):
        at = lanes(n, 256)
        d_win[:, at] = dot_t(d_proj[...], wq[at, :]).astype(LOW)
        return carry

    lax.fori_loop(0, 3, d_win_part, 0)
    unit, spread_one = normed(x_own[...])
    d_normed = d_win[...].astype(FULL)
    sums[0:1, :] = sum_rows(d_normed * unit)
    sums[6:7, :] = sum_rows(d_normed)
    d_win[...] = (d_mid[...] + normed_back(d_normed, gains[0:1, :], unit, spread_one)).astype(LOW)
    swap(d_win, d_own, S_GRAD)

    got(*share(xw_t, S_XWT))
    got(*share(att_t, S_AOT))
    got(*share_pack(db_pack, S_DBK))
    got(*share_pack(dy_pack, S_DYK))

    def qp_block(block):
        total = dot(xw_t[...], dy_pack[core, :, lanes(block, 384)])
        more = dot(att_t[...], db_pack[core, :, lanes(block, 128)])
        for n in range(4):
            for half in range(2):
                row = 192 * n + 96 * half
                cut = slice(row, row + 96)
                gq[block, half, n, :, 0:256] = total[cut, 0:256].astype(LOW)
                gq[block, half, n, :, 256:384] = (total[cut, 256:384] + more[cut]).astype(LOW)

    for block in range(4):
        qp_block(block)

    begin("q", 0)
    f2_run_two(0, 1)
    def spread_rel(head, carry):
        rows = dot(gather_t[...], probs[head, 0:ROWS]).astype(LOW)
        rel_grads[pl.ds(pl.multiple_of(64 * head, 64), 64), :] = dot(rows, offsets_t[...])
        return carry

    lax.fori_loop(0, 24, spread_rel, 0, unroll=4)

    def gather_rel(i, carry):
        start = 13 * (i // 7) + i % 7
        rows = rel_grads[pl.ds(i, 24, stride=64), :]
        return carry + pltpu.roll(jnp.concatenate([rows, jnp.zeros((24, 128), FULL)], axis=1), start, 1)

    rel_sum = lax.fori_loop(0, 49, gather_rel, jnp.zeros((24, 256), FULL), unroll=7)
    for k in range(3):
        sums[16:24, 256 * k : 256 * k + 256] = rel_sum[8 * k : 8 * k + 8, :]

    send(sums, got_core, S_AR, mate)
    run_two_own("f1")
    got(sums, got_core, S_AR, mate)
    sums_one[...] = sums[...] + got_core[...]
    for k in (1, 2, 3):
        send(sums_one, got_wide.at[k - 1], S_AR + k, beside[k])
    begin("q", 1)
    run_three("f1")
    run_two("q")
    f2_aside()
    f2_run_three(0, 1)
    swapped(result_low, result_own, S_RES)
    in_order(result_own[...], out_result)
    store(0, out_result, to_result)
    for k in (1, 2, 3):
        got(sums_one, got_wide.at[k - 1], S_AR + k, beside[k])
    sums_two[...] = (sums_one[...] + got_wide[0]) + (got_wide[1] + got_wide[2])
    send(sums_two, got_narrow.at[0], S_AR + 4, along[1])
    run_four("f1")
    f2_run_four()
    got(sums_two, got_narrow.at[0], S_AR + 4, along[1])
    sums_three[...] = sums_two[...] + got_narrow[0]
    send(sums_three, got_narrow.at[1], S_AR + 5, along[2])
    swapped(d_win, d_own, S_GRAD)
    in_order(d_own[...], out_tokens)
    store(1, out_tokens, to_tokens)
    run_two_own("q")
    run_three("q")
    finish("f1")
    store(2, out_f1, to_f1)
    run_four("q")
    f2_run_two(2)
    got(sums_three, got_narrow.at[1], S_AR + 5, along[2])
    small = sums_three[...] + got_narrow[1]
    out_gains[...] = small[0:2]
    out_biases[...] = small[2:8]
    for k in range(4):
        out_fc1_bias[:, 768 * k : 768 * k + 768] = small[8 + k : 9 + k]
    for k in range(3):
        out_rel[8 * k : 8 * k + 8, :] = small[16:24, 256 * k : 256 * k + 169]
    out_stats[...] = jnp.sqrt(small[12:13, 1:4] / (model * small[12:13, 0:1]))
    for k, (src, dst) in enumerate(
        (
            (out_gains, to_gains),
            (out_biases, to_biases),
            (out_fc1_bias, to_fc1_bias),
            (out_rel, to_rel),
            (out_stats, to_stats),
        )
    ):
        store(4 + k, src, dst)
    f2_run_three(2)
    f2_finish()
    store(3, out_f2, to_f2)
    finish("q")
    store(9, out_qkv, to_qkv)
    store(10, out_proj, to_proj)

    leave()


def fused_on_device(
    tokens, cotangent, crops, labels, norm_gains, biases, rel_table, w_qkv, w_proj, w_fc1, fc1_bias, w_fc2
):
    images, _, patches, model = tokens.shape
    hidden = w_fc1.shape[1]
    heads = rel_table.shape[1]
    vmem = pl.BlockSpec(memory_space=pltpu.VMEM)
    hbm = pl.BlockSpec(memory_space=pl.ANY)

    def low(*shape):
        return pltpu.VMEM(shape, LOW)

    def full(*shape):
        return pltpu.VMEM(shape, FULL)

    one_low = low(ROWS, model)
    one_t = low(model, ROWS)
    scratch = dict(
        wq=low(*w_qkv.shape),
        wp=low(*w_proj.shape),
        w1=low(*w_fc1.shape),
        w2=low(*w_fc2.shape),
        stack=full(256, model),
        result_low=one_low,
        x_own=full(ROWS, model),
        g_low=one_low,
        g_t=low(4, 2, 96, 256),
        g_both=low(4, 96, 512),
        tok_own=one_low,
        tok_win=one_low,
        g_own=one_low,
        result_own=one_low,
        xw=one_low,
        xw_t=low(model, 512),
        query=one_low,
        key=low(KEYS, model),
        value=low(KEYS, model),
        key_bias=low(heads, KEYS, 128),
        row_scale=full(ROWS, model),
        probs=low(heads, KEYS, KEYS),
        att=one_low,
        att_t=low(model, 512),
        middle=full(ROWS, model),
        h2=one_low,
        h2_t=low(model, 512),
        act=low(512, hidden),
        dh=low(512, hidden),
        gf1=low(4, 2, 4, 96, 384),
        gf2=low(4, 4, 2, 48, 768),
        rzf2=low(4, 2, 48, 768),
        gq=low(4, 2, 4, 96, 384),
        r1f1=low(2, 2, 4, 96, 384),
        r1f2=low(2, 2, 3, 48, 768),
        r1q=low(2, 2, 4, 96, 384),
        r2f1=low(2, 4, 96, 384),
        r2f2=low(2, 3, 48, 768),
        r3f2=low(2, 48, 768),
        r2q=low(2, 4, 96, 384),
        r3f1=low(2, 2, 96, 384),
        r3q=low(2, 2, 96, 384),
        r4f1=low(2, 96, 384),
        r4f2=low(2, 48, 768),
        r4q=low(2, 96, 384),
        d_mid=full(ROWS, model),
        d_branch=one_low,
        db_pack=low(2, 512, 512),
        d_att=one_low,
        d_proj=low(ROWS, 3 * model),
        dy_pack=low(2, 512, 1536),
        d_win=one_low,
        d_own=one_low,
        rel_rows=full(64 * 24, 128),
        rel_grads=full(64 * 24, 128),
        mask_add=full(ROWS, KEYS),
        valid_col=full(ROWS, 1),
        sums=full(24, 768),
        sums_one=full(24, 768),
        sums_two=full(24, 768),
        sums_three=full(24, 768),
        got_core=full(24, 768),
        got_wide=full(3, 24, 768),
        got_narrow=full(2, 24, 768),
        local_sem=pltpu.SemaphoreType.DMA((32,)),
        send_sem=pltpu.SemaphoreType.DMA((S_COUNT,)),
        recv_sem=pltpu.SemaphoreType.DMA((S_COUNT,)),
    )
    shapes = (
        ((patches, images, model), LOW),
        ((patches, images, model), LOW),
        ((192, 288), FULL),
        ((192, 96), FULL),
        ((192, 384), FULL),
        ((96, 768), FULL),
        ((2, model), FULL),
        ((6, model), FULL),
        ((1, hidden), FULL),
        ((heads, 169), FULL),
        ((1, 3), FULL),
    )
    inputs = (
        ((patches, images, model), LOW),
        ((patches, images, model), LOW),
        ((2, images), jnp.int32),
        ((images, patches), jnp.int32),
        ((2, model), FULL),
        ((6, model), FULL),
        ((heads, 169), FULL),
        ((1, hidden), FULL),
        ((TABLE_ROWS, 256), LOW),
        ((ROWS, 8), jnp.int32),
    )
    outs = pl.pallas_call(
        block_kernel,
        out_shape=tuple(jax.ShapeDtypeStruct(*shape) for shape in shapes),
        in_specs=[hbm] * 14,
        out_specs=[hbm] * OUTPUTS,
        scratch_shapes=[pltpu.VMEM(*shape) for shape in inputs + shapes] + list(scratch.values()),
        compiler_params=pltpu.CompilerParams(
            collective_id=0, has_side_effects=True, vmem_limit_bytes=VMEM_LIMIT
        ),
    )(
        tokens[:, 0].transpose(1, 0, 2),
        cotangent[:, 0].transpose(1, 0, 2),
        crops.T,
        labels[:, 0],
        norm_gains,
        biases,
        rel_table.T,
        w_qkv,
        w_proj,
        w_fc1,
        fc1_bias.reshape(1, hidden),
        w_fc2,
        *[jnp.asarray(table) for table in place_tables()],
    )
    outs = pl.pallas_call(
        hand_over,
        out_shape=tuple(jax.ShapeDtypeStruct(*shape) for shape in shapes),
        in_specs=[hbm] * OUTPUTS,
        out_specs=[hbm] * OUTPUTS,
        scratch_shapes=[pltpu.VMEM(*shape) for shape in shapes]
        + [pltpu.SemaphoreType.DMA((2, OUTPUTS))],
    )(*outs)
    return (
        outs[0].transpose(1, 0, 2)[:, None],
        outs[1].transpose(1, 0, 2)[:, None],
        outs[2],
        outs[3],
        outs[4],
        outs[5].T,
        outs[6],
        outs[7],
        outs[8].reshape(hidden),
        outs[9].T,
        outs[10].reshape(3),
    )


def hand_over(*refs):
    sems = refs[-1]
    held = refs[2 * OUTPUTS : 3 * OUTPUTS]
    loads = [pltpu.make_async_copy(refs[k], held[k], sems.at[0, k]) for k in range(OUTPUTS)]
    stores = [pltpu.make_async_copy(held[k], refs[OUTPUTS + k], sems.at[1, k]) for k in range(OUTPUTS)]
    for load in loads:
        load.start()
    for load, store in zip(loads, stores):
        load.wait()
        store.start()
    for store in stores:
        store.wait()


VMEM_LIMIT = 62 * 1024 * 1024


def fused(mesh):
    each = P("wide", "narrow", None, None)
    cut = P("narrow", "wide")
    return jax.shard_map(
        fused_on_device,
        mesh=mesh,
        in_specs=(each, each, P("wide", None), P("wide", "narrow", None)) + (P(),) * 8,
        out_specs=(each, each) + (cut,) * 4 + (P(),) * 5,
        check_vma=False,
    )


def solution(mesh):
    if mesh.shape["wide"] == 8 and mesh.shape["narrow"] == 4:
        return fused(mesh)
    return plain(mesh)
```

```python
from functools import partial

import jax
import jax.numpy as jnp
import numpy as np
from jax import lax
from jax.experimental import pallas as pl
from jax.experimental.pallas import tpu as pltpu
from jax.sharding import PartitionSpec as P


def from_partner(shard, axis, stride):
    return lax.ppermute(shard, axis, [(i, i ^ 1 << stride) for i in range(lax.axis_size(axis))])


def layer_norm(values, gain, shift):
    centre = jnp.mean(values, axis=-1, keepdims=True)
    centred = values - centre
    spread = jnp.mean(centred * centred, axis=-1, keepdims=True)
    return centred * lax.rsqrt(spread + 1e-05) * gain + shift


def into_window(field, swap_rows, swap_cols):
    tall = jnp.concatenate([field[:, 3:], swap_rows(field[:, :3])], axis=1)
    return jnp.concatenate([tall[:, :, 3:], swap_cols(tall[:, :, :3])], axis=2)


def out_of_window(field, swap_rows, swap_cols):
    broad = jnp.concatenate([swap_cols(field[:, :, 4:]), field[:, :, :4]], axis=2)
    return jnp.concatenate([swap_rows(broad[:, 4:]), broad[:, :4]], axis=1)


def relative_index():
    positions = jnp.arange(49, dtype=jnp.int32)
    inner_rows = positions // 7
    inner_cols = positions % 7
    return (
        (inner_rows[:, None] - inner_rows[None, :] + 6) * 13
        + inner_cols[:, None]
        - inner_cols[None, :]
        + 6
    )


def column_sum(values):
    return jnp.sum(values, axis=0, dtype=jnp.float32)


def on_device(
    tokens,
    cotangent,
    crops,
    labels,
    norm_gains,
    biases,
    rel_table,
    w_qkv,
    w_proj,
    w_fc1,
    fc1_bias,
    w_fc2,
):
    images = tokens.shape[0]
    model_width = tokens.shape[-1]
    head_count = rel_table.shape[1]
    head_size = model_width // head_count
    rows_all = images * 49
    score_scale = head_size ** (-0.5)
    where_narrow = lax.axis_index("narrow")
    row_half = where_narrow // 2
    col_half = where_narrow % 2
    positions = jnp.arange(49, dtype=jnp.int32)
    own_row = 7 * row_half + positions // 7
    own_col = 7 * col_half + positions % 7
    shift_row = (own_row + 3) % 14
    shift_col = (own_col + 3) % 14
    valid_own = (own_row[None] < crops[:, 0:1]) & (own_col[None] < crops[:, 1:2])
    valid_shift = (shift_row[None] < crops[:, 0:1]) & (shift_col[None] < crops[:, 1:2])
    label_rows = labels[:, 0]
    allowed = (label_rows[:, :, None] == label_rows[:, None, :]) & valid_shift[
        :, None, :
    ] | jnp.eye(49, dtype=bool)[None]
    allowed_heads = allowed[:, None]
    inputs = tokens[:, 0].astype(jnp.float32)
    normed, ln1_back = jax.vjp(layer_norm, inputs, norm_gains[0], biases[4])
    normed_low = normed.astype(jnp.bfloat16).reshape(images, 7, 7, model_width)
    windows = into_window(
        normed_low,
        lambda strip: from_partner(strip, "narrow", 1),
        lambda strip: from_partner(strip, "narrow", 0),
    ).reshape(rows_all, model_width)
    projected = jnp.dot(windows, w_qkv, preferred_element_type=jnp.float32)
    head_shape = (images, 49, head_count, head_size)
    query_rows = (projected[:, :model_width] + biases[0]).astype(jnp.bfloat16).reshape(head_shape)
    key_rows = projected[:, model_width : 2 * model_width].astype(jnp.bfloat16).reshape(head_shape)
    value_rows = (
        (projected[:, 2 * model_width :] + biases[1]).astype(jnp.bfloat16).reshape(head_shape)
    )
    one_hot = (
        (relative_index()[:, :, None] == jnp.arange(169, dtype=jnp.int32))
        .reshape(2401, 169)
        .astype(jnp.float32)
    )
    bias_table = (
        jnp.dot(one_hot, rel_table, precision=lax.Precision.HIGHEST)
        .reshape(49, 49, head_count)
        .transpose(2, 0, 1)
    )

    def masked_scores():
        raw = jnp.einsum(
            "nphe,nqhe->nhpq", query_rows, key_rows, preferred_element_type=jnp.float32
        )
        return jnp.where(allowed_heads, raw * score_scale + bias_table[None], -1000000000.0)

    masked = masked_scores()
    row_top = jnp.max(masked, axis=-1, keepdims=True)
    log_total = row_top + jnp.log(jnp.sum(jnp.exp(masked - row_top), axis=-1, keepdims=True))
    attn_probs = jnp.exp(masked - log_total)
    probs_low = attn_probs.astype(jnp.bfloat16)
    attended = jnp.einsum(
        "nhpq,nqhe->nphe", probs_low, value_rows, preferred_element_type=jnp.float32
    ).astype(jnp.bfloat16)
    restored = out_of_window(
        attended.reshape(images, 7, 7, model_width),
        lambda strip: from_partner(strip, "narrow", 1),
        lambda strip: from_partner(strip, "narrow", 0),
    ).reshape(rows_all, model_width)
    branch_attn = jnp.dot(restored, w_proj, preferred_element_type=jnp.float32) + biases[2]
    middle = inputs.reshape(rows_all, model_width) + branch_attn
    normed_two, ln2_back = jax.vjp(layer_norm, middle, norm_gains[1], biases[5])
    normed_two_low = normed_two.astype(jnp.bfloat16)
    hidden = jnp.dot(normed_two_low, w_fc1, preferred_element_type=jnp.float32) + fc1_bias
    activated, gelu_back = jax.vjp(partial(jax.nn.gelu, approximate=False), hidden)
    activated_low = activated.astype(jnp.bfloat16)
    branch_mlp = jnp.dot(activated_low, w_fc2, preferred_element_type=jnp.float32) + biases[3]
    result = (middle + branch_mlp).astype(jnp.bfloat16).reshape(images, 1, 49, model_width)
    cot_rows = cotangent.reshape(rows_all, model_width)
    grad_fc2 = jnp.dot(activated_low.T, cot_rows, preferred_element_type=jnp.float32)
    d_activated = jnp.dot(cot_rows, w_fc2.T, preferred_element_type=jnp.float32)
    (d_hidden,) = gelu_back(d_activated)
    d_hidden_low = d_hidden.astype(jnp.bfloat16)
    grad_fc1 = jnp.dot(normed_two_low.T, d_hidden_low, preferred_element_type=jnp.float32)
    grad_fc1_bias = column_sum(d_hidden_low)
    d_normed_two = jnp.dot(d_hidden_low, w_fc1.T, preferred_element_type=jnp.float32)
    d_middle_norm, d_gain_two, d_shift_two = ln2_back(d_normed_two)
    d_middle = cot_rows.astype(jnp.float32) + d_middle_norm
    d_branch = d_middle.astype(jnp.bfloat16)
    grad_proj = jnp.dot(restored.T, d_branch, preferred_element_type=jnp.float32)
    d_restored = jnp.dot(d_branch, w_proj.T, preferred_element_type=jnp.float32).astype(
        jnp.bfloat16
    )
    d_attended = into_window(
        d_restored.reshape(images, 7, 7, model_width),
        lambda strip: from_partner(strip, "narrow", 1),
        lambda strip: from_partner(strip, "narrow", 0),
    ).reshape(head_shape)
    again = jnp.exp(masked_scores() - log_total)
    d_probs = jnp.einsum(
        "nphe,nqhe->nhpq", d_attended, value_rows, preferred_element_type=jnp.float32
    )
    d_scores = (again * (d_probs - jnp.sum(again * d_probs, axis=-1, keepdims=True))).astype(
        jnp.bfloat16
    )
    d_table = jnp.sum(d_scores, axis=0, dtype=jnp.float32).reshape(head_count, 2401)
    grad_rel = jnp.dot(d_table, one_hot, precision=lax.Precision.HIGHEST).T
    d_query = (
        jnp.einsum("nhpq,nqhe->nphe", d_scores, key_rows, preferred_element_type=jnp.float32)
        * score_scale
    ).astype(jnp.bfloat16)
    d_key = (
        jnp.einsum("nhpq,nphe->nqhe", d_scores, query_rows, preferred_element_type=jnp.float32)
        * score_scale
    ).astype(jnp.bfloat16)
    d_value = jnp.einsum(
        "nhpq,nphe->nqhe", probs_low, d_attended, preferred_element_type=jnp.float32
    ).astype(jnp.bfloat16)
    d_projected = jnp.concatenate(
        [
            d_query.reshape(rows_all, model_width),
            d_key.reshape(rows_all, model_width),
            d_value.reshape(rows_all, model_width),
        ],
        axis=1,
    )
    grad_qkv = jnp.dot(windows.T, d_projected, preferred_element_type=jnp.float32)
    d_windows = jnp.dot(d_projected, w_qkv.T, preferred_element_type=jnp.float32).astype(
        jnp.bfloat16
    )
    d_normed = out_of_window(
        d_windows.reshape(images, 7, 7, model_width),
        lambda strip: from_partner(strip, "narrow", 1),
        lambda strip: from_partner(strip, "narrow", 0),
    ).reshape(images, 49, model_width)
    d_inputs_norm, d_gain_one, d_shift_one = ln1_back(d_normed.astype(jnp.float32))
    grad_tokens = (
        (d_middle.reshape(images, 49, model_width) + d_inputs_norm)
        .astype(jnp.bfloat16)
        .reshape(images, 1, 49, model_width)
    )
    grad_biases = jnp.stack(
        [
            column_sum(d_query.reshape(rows_all, model_width)),
            column_sum(d_value.reshape(rows_all, model_width)),
            column_sum(d_branch),
            column_sum(cot_rows),
            d_shift_one,
            d_shift_two,
        ]
    )
    grad_gains = jnp.stack([d_gain_one, d_gain_two])
    valid_weight = valid_own.astype(jnp.float32).reshape(rows_all)
    flat_inputs = inputs.reshape(rows_all, model_width)
    stat_sums = jnp.stack(
        [
            jnp.sum(valid_weight),
            jnp.sum(valid_weight * jnp.sum(flat_inputs * flat_inputs, axis=-1)),
            jnp.sum(valid_weight * jnp.sum(branch_attn * branch_attn, axis=-1)),
            jnp.sum(valid_weight * jnp.sum(branch_mlp * branch_mlp, axis=-1)),
        ]
    )
    grad_biases, grad_gains, grad_fc1_bias, grad_rel, stat_sums = lax.psum(
        (grad_biases, grad_gains, grad_fc1_bias, grad_rel, stat_sums), ("wide", "narrow")
    )
    stats = jnp.sqrt(stat_sums[1:] / (model_width * stat_sums[0]))
    matrices = (grad_qkv, grad_proj, grad_fc1, grad_fc2)
    partial_sums = (
        lax.psum_scatter(matrices[0], "wide", scatter_dimension=1, tiled=True),
        lax.psum_scatter(matrices[1], "wide", scatter_dimension=1, tiled=True),
        lax.psum_scatter(matrices[2], "wide", scatter_dimension=1, tiled=True),
        lax.psum_scatter(matrices[3], "wide", scatter_dimension=1, tiled=True),
    )
    reduced = (
        lax.psum_scatter(
            partial_sums[0].astype(jnp.bfloat16), "narrow", scatter_dimension=0, tiled=True
        ).astype(jnp.float32),
        lax.psum_scatter(
            partial_sums[1].astype(jnp.bfloat16), "narrow", scatter_dimension=0, tiled=True
        ).astype(jnp.float32),
        lax.psum_scatter(
            partial_sums[2].astype(jnp.bfloat16), "narrow", scatter_dimension=0, tiled=True
        ).astype(jnp.float32),
        lax.psum_scatter(
            partial_sums[3].astype(jnp.bfloat16), "narrow", scatter_dimension=0, tiled=True
        ).astype(jnp.float32),
    )
    grad_qkv, grad_proj, grad_fc1, grad_fc2 = reduced
    return (
        result,
        grad_tokens,
        grad_qkv,
        grad_proj,
        grad_fc1,
        grad_fc2,
        grad_gains,
        grad_biases,
        grad_fc1_bias,
        grad_rel,
        stats,
    )


def plain(mesh):
    return jax.shard_map(
        on_device,
        mesh=mesh,
        in_specs=(
            P("wide", "narrow", None, None),
            P("wide", "narrow", None, None),
            P("wide", None),
            P("wide", "narrow", None),
            P(),
            P(),
            P(),
            P(),
            P(),
            P(),
            P(),
            P(),
        ),
        out_specs=(
            P("wide", "narrow", None, None),
            P("wide", "narrow", None, None),
            P("narrow", "wide"),
            P("narrow", "wide"),
            P("narrow", "wide"),
            P("narrow", "wide"),
            P(),
            P(),
            P(),
            P(),
            P(),
        ),
        check_vma=False,
    )


ROWS = 208
KEYS = 256
T_OWN, T_BACK, T_PICK, T_SPREAD, T_OFFSETS, T_GATHER, T_REPEAT = 0, 208, 464, 720, 928, 1184, 1248
TABLE_ROWS = 1504
MESH = pl.DeviceIdType.MESH
LOW = jnp.bfloat16
FULL = jnp.float32


def place_tables():
    places = []
    for tall, broad in ((0, 0), (1, 0), (0, 1), (1, 1)):
        for image in range(4):
            for i in range(4, 7) if tall else range(4):
                for j in range(4, 7) if broad else range(4):
                    places.append((image, i, j, i - 4 if tall else i + 3, j - 4 if broad else j + 3))
    own = np.zeros((ROWS, 256), np.float32)
    spread = np.zeros((ROWS, 128), np.float32)
    pick = np.zeros((256, 128), np.float32)
    repeat = np.zeros((KEYS, 64), np.float32)
    for spot in range(49):
        for lane in (spot, 64 + spot):
            pick[13 * (spot // 7) + spot % 7, lane] = 1
            pick[128 + 13 * (spot // 7) + spot % 7, lane] = 1
    gather = np.zeros((64, ROWS), np.float32)
    offsets = np.zeros((KEYS, 128), np.float32)
    info = np.zeros((ROWS, 8), np.int32)
    info[:, 3] = -1
    for row in range(ROWS):
        if row >= len(places):
            info[row, 0] = 4 + row - len(places)
            continue
        image, i, j, a, b = places[row]
        own[row, 4 * (7 * a + b) + image] = 1
        spread[row, 7 * i + j] = 1
        spread[row, 64 + 7 * i + j] = 1
        shift = (6 - i) * 13 + 6 - j
        repeat[row, 7 * i + j] = 1
        gather[7 * i + j, row] = 1
        offsets[row, shift] = 1
        info[row, :6] = (image, i, j, 7 * i + j, a, b)
    table = np.zeros((TABLE_ROWS, 256), np.float32)
    table[T_OWN : T_OWN + ROWS] = own
    table[T_BACK : T_BACK + 256, :ROWS] = own.T
    table[T_PICK : T_PICK + 256, :128] = pick
    table[T_REPEAT : T_REPEAT + KEYS, :64] = repeat
    table[T_SPREAD : T_SPREAD + ROWS, :128] = spread
    table[T_OFFSETS : T_OFFSETS + KEYS, :128] = offsets
    table[T_GATHER : T_GATHER + 64, :ROWS] = gather
    return table.astype(jnp.bfloat16), info


def dot(left, right):
    return jnp.dot(left, right, preferred_element_type=FULL)


def dot_t(left, right):
    return lax.dot_general(left, right, (((1,), (1,)), ((), ())), preferred_element_type=FULL)


def lanes(index, width):
    return pl.ds(pl.multiple_of(index * width, width), width)


def normed(values):
    centred = values - jnp.mean(values, axis=-1, keepdims=True)
    scale = lax.rsqrt(jnp.mean(centred * centred, axis=-1, keepdims=True) + 1e-05)
    return centred * scale, scale


def normed_back(grad, gain, unit, scale):
    inner = grad * gain
    along = jnp.mean(inner, axis=-1, keepdims=True)
    across = jnp.mean(inner * unit, axis=-1, keepdims=True)
    return scale * (inner - along - unit * across)


def sum_rows(values):
    return jnp.sum(values, axis=0, keepdims=True)


GROUPS = ((64, 48), (112, 48), (160, 48))

S_TOK = 0
S_COT = 3
S_RES = 6
S_GRAD = 9
S_GT = 12
S_XWT = 13
S_AOT = 14
S_H2T = 15
S_ACT = 16
S_DH = 20
S_DBK = 24
S_DYK = 25
S_AR = 26
S_F1 = 33
S_F2 = 51
S_Q = 75
S_COUNT = 93
OUTPUTS = 11
ROUTES = ((0, 0), (1, 0), (0, 1), (1, 1))


def block_kernel(
    tokens_hbm,
    cotangent_hbm,
    crops_hbm,
    labels_hbm,
    gains_hbm,
    biases_hbm,
    rel_hbm,
    wq_hbm,
    wp_hbm,
    w1_hbm,
    fc1_bias_hbm,
    w2_hbm,
    table_hbm,
    info_hbm,
    to_result,
    to_tokens,
    to_qkv,
    to_proj,
    to_f1,
    to_f2,
    to_gains,
    to_biases,
    to_fc1_bias,
    to_rel,
    to_stats,
    tokens,
    cotangent,
    crops,
    labels,
    gains,
    biases,
    rel_table,
    fc1_bias,
    table,
    info,
    out_result,
    out_tokens,
    out_qkv,
    out_proj,
    out_f1,
    out_f2,
    out_gains,
    out_biases,
    out_fc1_bias,
    out_rel,
    out_stats,
    wq,
    wp,
    w1,
    w2,
    stack,
    result_low,
    x_own,
    g_low,
    g_t,
    g_both,
    tok_own,
    tok_win,
    g_own,
    result_own,
    xw,
    xw_t,
    query,
    key,
    value,
    key_bias,
    row_scale,
    probs,
    att,
    att_t,
    middle,
    h2,
    h2_t,
    act,
    dh,
    gf1,
    gf2,
    rzf2,
    gq,
    r1f1,
    r1f2,
    r1q,
    r2f1,
    r2f2,
    r3f2,
    r2q,
    r3f1,
    r3q,
    r4f1,
    r4f2,
    r4q,
    d_mid,
    d_branch,
    db_pack,
    d_att,
    d_proj,
    dy_pack,
    d_win,
    d_own,
    rel_rows,
    rel_grads,
    mask_add,
    valid_col,
    sums,
    sums_one,
    sums_two,
    sums_three,
    got_core,
    got_wide,
    got_narrow,
    local_sem,
    send_sem,
    recv_sem,
):
    model = x_own.shape[1]
    width = lax.axis_index("wide")
    depth = lax.axis_index("narrow")
    core = width % 2
    mine = width // 2
    mate = {"wide": width ^ 1, "narrow": depth}
    beside = [None] + [{"wide": width ^ (2 * k), "narrow": depth} for k in (1, 2, 3)]
    along = [None] + [{"wide": width, "narrow": depth ^ k} for k in (1, 2, 3)]
    partners = [mate] + beside[1:] + along[1:]
    quadrant = (along[2], along[1], along[3])

    started = {}

    def copy_of(src, dst, index, device):
        return pltpu.make_async_remote_copy(
            src_ref=src,
            dst_ref=dst,
            send_sem=send_sem.at[index],
            recv_sem=recv_sem.at[index],
            device_id=device,
            device_id_type=MESH,
        )

    def send(*args):
        copy_of(*args).start()
        started[args[2]] = [lambda n: [args], 1, False]

    def got(*args):
        copy_of(*args).wait_recv()
        started[args[2]][2] = True

    def each(copies, count, act):
        def step(n, carry):
            for args in copies(n):
                act(copy_of(*args))
            return carry

        if count == 1:
            step(0, 0)
        else:
            lax.fori_loop(0, count, step, 0)

    def got_all(name):
        copies, count, _ = started[name]
        each(copies, count, lambda copy: copy.wait_recv())
        started[name][2] = True

    def leave():
        for copies, count, arrived in started.values():
            if not arrived:
                each(copies, count, lambda copy: copy.wait_recv())
        for copies, count, _ in started.values():
            each(copies, count, lambda copy: copy.wait_send())
        for copy in stores:
            copy.wait()

    barrier = pltpu.get_barrier_semaphore()
    for partner in partners:
        pl.semaphore_signal(barrier, inc=1, device_id=partner, device_id_type=MESH)
    pairs = ((wq_hbm, wq), (wp_hbm, wp), (w1_hbm, w1), (w2_hbm, w2))
    pairs += ((tokens_hbm, tokens), (table_hbm, table), (gains_hbm, gains), (biases_hbm, biases))
    pairs += ((cotangent_hbm, cotangent), (info_hbm, info), (crops_hbm, crops), (labels_hbm, labels))
    pairs += ((rel_hbm, rel_table), (fc1_bias_hbm, fc1_bias))
    loads = [pltpu.make_async_copy(src, dst, local_sem.at[k]) for k, (src, dst) in enumerate(pairs)]
    for load in loads[4:] + loads[:4]:
        load.start()
    own_t = table.at[pl.ds(T_OWN, ROWS), :]
    back_t = table.at[pl.ds(T_BACK, 256), pl.ds(0, ROWS)]
    pick_t = table.at[pl.ds(T_PICK, 256), pl.ds(0, 128)]
    repeat_t = table.at[pl.ds(T_REPEAT, KEYS), pl.ds(0, 64)]
    spread_t = table.at[pl.ds(T_SPREAD, ROWS), pl.ds(0, 128)]
    offsets_t = table.at[pl.ds(T_OFFSETS, KEYS), pl.ds(0, 128)]
    gather_t = table.at[pl.ds(T_GATHER, 64), pl.ds(0, ROWS)]

    def store(k, src, dst):
        copy = pltpu.make_async_copy(src, dst, local_sem.at[len(pairs) + k])
        copy.start()
        stores.append(copy)

    stores = []

    def in_places(source):
        stack[192:256, :] = jnp.zeros((64, model), FULL)
        for patch in range(49):
            stack[4 * patch : 4 * patch + 4, :] = source[patch].astype(FULL)
        return dot(own_t[...], stack[...].astype(LOW))

    def in_order(values, out):
        stack[...] = dot(back_t[...], values)
        for patch in range(49):
            out[patch] = stack[4 * patch : 4 * patch + 4, :].astype(LOW)

    def swap(src, dst, base):
        dst[0:64, :] = src[0:64, :]
        for k, (row, count) in enumerate(GROUPS):
            rows = pl.ds(row, count)
            send(src.at[rows], dst.at[rows], base + k, quadrant[k])

    def swapped(src, dst, base):
        for k, (row, count) in enumerate(GROUPS):
            rows = pl.ds(row, count)
            got(src.at[rows], dst.at[rows], base + k, quadrant[k])

    for load in loads[4:8]:
        load.wait()
    tok_own[...] = in_places(tokens).astype(LOW)
    pl.semaphore_wait(barrier, len(partners))
    swap(tok_own, tok_win, S_TOK)

    for load in loads[8:]:
        load.wait()
    g_value = in_places(cotangent)
    g_own[...] = g_value.astype(LOW)
    for buffer in (xw_t, att_t, h2_t):
        buffer[:, 128:256] = jnp.zeros((model, 128), LOW)
    for buffer in (act, dh, dy_pack.at[0], dy_pack.at[1], db_pack.at[0], db_pack.at[1]):
        for row in (ROWS, 256 + ROWS):
            buffer[row : row + 48, :] = jnp.zeros((48, buffer.shape[1]), LOW)
    g_t[...] = jnp.zeros_like(g_t)

    sums[...] = jnp.zeros_like(sums)
    sums[5:6, :] = sum_rows(g_value)

    row_half = depth // 2
    col_half = depth % 2
    image_col = info[:, 0:1]
    i_col = info[:, 1:2]
    j_col = info[:, 2:3]
    place_col = info[:, 3:4]
    zero_col = jnp.zeros((ROWS, 1), jnp.int32)
    crop_row = zero_col
    crop_col = zero_col
    label = jnp.zeros((ROWS, 1), FULL)
    lane49 = lax.broadcasted_iota(jnp.int32, (ROWS, 49), 1)
    for image in range(4):
        is_image = image_col == image
        crop_row = jnp.where(is_image, crops[0:1, image : image + 1], crop_row)
        crop_col = jnp.where(is_image, crops[1:2, image : image + 1], crop_col)
        picked = jnp.where(
            lane49 == place_col, labels[image : image + 1, :].astype(FULL), jnp.zeros((ROWS, 49), FULL)
        )
        label = jnp.where(is_image, jnp.sum(picked, axis=1, keepdims=True), label)
    shift_row = 7 * row_half + i_col + 3
    shift_row = jnp.where(shift_row >= 14, shift_row - 14, shift_row)
    shift_col = 7 * col_half + j_col + 3
    shift_col = jnp.where(shift_col >= 14, shift_col - 14, shift_col)
    valid_key = (shift_row < crop_row) & (shift_col < crop_col)
    valid_value = jnp.where(valid_key, 1.0, 0.0).astype(FULL)
    valid_col[...] = valid_value
    code = label + 8.0 * image_col.astype(FULL)
    key_code = jnp.where(valid_key, code, -1.0)
    diagonal = lax.broadcasted_iota(jnp.int32, (ROWS, KEYS), 0) == lax.broadcasted_iota(
        jnp.int32, (ROWS, KEYS), 1
    )
    key_row = jnp.sum(jnp.where(diagonal, key_code + 2.0, 0.0), axis=0, keepdims=True) - 2.0
    mask_add[...] = jnp.where((code == key_row) | diagonal, 0.0, -1000000000.0)

    rel_wide = jnp.concatenate([rel_table[...] * 32**0.5, jnp.zeros((24, 87), FULL)], axis=1)
    rel_rows[1176:1536, :] = jnp.zeros((360, 128), FULL)

    def shifted(spot, carry):
        start = 84 - 13 * (spot // 7) - spot % 7
        rel_rows[pl.ds(pl.multiple_of(24 * spot, 8), 24), :] = pltpu.roll(rel_wide, 256 - start, 1)[:, 0:128]
        return carry

    lax.fori_loop(0, 49, shifted, 0, unroll=7)

    def picked_rows(n, carry):
        rows = pl.ds(pl.multiple_of(168 * n, 8), 168)
        values = rel_rows[rows, :]
        high = values.astype(LOW)
        below = (values - high.astype(FULL)).astype(LOW)
        rel_rows[rows, :] = dot(jnp.concatenate([high, below], axis=1), pick_t[...])
        return carry

    lax.fori_loop(0, 7, picked_rows, 0)
    is_high = lax.broadcasted_iota(jnp.int32, (64, 128), 1) < 64

    def head_bias(head, carry):
        values = rel_rows[pl.ds(head, 64, stride=24), :]
        high = values.astype(LOW).astype(FULL)
        parts = jnp.where(is_high, high, values - high).astype(LOW)
        key_bias[head] = dot(repeat_t[...], parts).astype(LOW)
        return carry

    lax.fori_loop(0, 24, head_bias, 0, unroll=4)

    key[ROWS:KEYS, :] = jnp.zeros((KEYS - ROWS, model), LOW)
    value[ROWS:KEYS, :] = jnp.zeros((KEYS - ROWS, model), LOW)
    swapped(tok_own, tok_win, S_TOK)
    swap(g_own, g_low, S_COT)
    flat = tok_win[...].astype(FULL)
    x_own[...] = flat
    unit, _ = normed(flat)
    xw[...] = (unit * gains[0:1, :] + biases[4:5, :]).astype(LOW)
    stat_total = jnp.sum(valid_value, axis=0, keepdims=True)
    stat_input = sum_rows(valid_value * jnp.sum(flat * flat, axis=-1, keepdims=True))

    loads[0].wait()

    def project(n, carry):
        at = lanes(n, 256)
        window = xw[...]
        query[:, at] = (dot(window, wq[:, at]) + biases[0:1, at]).astype(LOW)
        key[0:ROWS, at] = dot(window, wq[:, lanes(n + 3, 256)]).astype(LOW)
        value[0:ROWS, at] = (dot(window, wq[:, lanes(n + 6, 256)]) + biases[1:2, at]).astype(LOW)
        return carry

    lax.fori_loop(0, 3, project, 0)

    lane_head = lax.broadcasted_iota(jnp.int32, (1, 128), 1) // 32
    only = [(lane_head == h).astype(FULL).astype(LOW) for h in range(4)]
    row_head = lax.broadcasted_iota(jnp.int32, (128, 1), 0) // 32
    only_row = [(row_head == h).astype(FULL).astype(LOW) for h in range(4)]
    scale = 32 ** (-0.5)

    def attend(t, carry):
        at = lanes(t, 128)
        q = query[:, at]
        k = key[:, at]
        v = value[:, at]
        powers = []
        right = []
        for h in range(4):
            left = jnp.concatenate([q * only[h], spread_t[...]], axis=1)
            scores = dot_t(left, jnp.concatenate([k, key_bias[4 * t + h]], axis=1)) + mask_add[...]
            top = jnp.max(scores, axis=-1, keepdims=True)
            power = jnp.exp2((scores - top) * (scale * 1.4426950408889634)).astype(LOW)
            probs[4 * t + h, 0:ROWS] = power
            probs[4 * t + h, ROWS:KEYS] = jnp.zeros((KEYS - ROWS, KEYS), LOW)
            powers.append(power)
            right.append(jnp.concatenate([v * only[h], jnp.ones((KEYS, 128), LOW) * only[h]], axis=1))
        both = dot(jnp.concatenate(powers, axis=1), jnp.concatenate(right, axis=0))
        total = both[:, 0:128]
        below = 1.0 / both[:, 128:256]
        row_scale[:, at] = below
        total = (total * below).astype(LOW)
        att[:, at] = total
        return carry

    lax.fori_loop(0, 6, attend, 0)

    def share(buffer, index):
        return buffer.at[:, pl.ds(0, 256)], buffer.at[:, pl.ds(256, 256)], index, mate

    loads[1].wait()

    def attn_branch(n, carry):
        at = lanes(n, 256)
        branch = dot(att[...], wp[:, at]) + biases[2:3, at]
        middle[:, at] = x_own[:, at] + branch
        return carry + jnp.sum(branch * branch, axis=-1, keepdims=True)

    branch_square = lax.fori_loop(0, 3, attn_branch, jnp.zeros((ROWS, 1), FULL))
    stat_attn = sum_rows(valid_col[...] * branch_square)

    unit, _ = normed(middle[...])
    h2[...] = (unit * gains[1:2, :] + biases[5:6, :]).astype(LOW)
    h2_t[:, 0:ROWS] = h2[...].T
    send(*share(h2_t, S_H2T))
    loads[2].wait()
    loads[3].wait()
    swapped(g_own, g_low, S_COT)

    def turn(r):
        return mine ^ jnp.where(r == 0, 3, jnp.where(r == 3, 0, r))

    def mlp_copies(r):
        at = lanes(turn(r), 768)
        return [
            (dh.at[pl.ds(0, ROWS), at], dh.at[pl.ds(256, ROWS), at], S_DH + r, mate),
            (act.at[pl.ds(0, ROWS), at], act.at[pl.ds(256, ROWS), at], S_ACT + r, mate),
        ]

    def hidden_quarter(r):
        quarter = turn(r)

        def hidden_part(n, carry):
            at = lanes(quarter * 3 + n, 256)
            hidden = dot(h2[...], w1[:, at]) + fc1_bias[:, at]
            d_act = dot_t(g_low[...], w2[at, :])
            below = 0.5 + 0.5 * lax.erf(hidden * 0.7071067811865476)
            act[0:ROWS, at] = (hidden * below).astype(LOW)
            slope = below + hidden * (0.3989422804014327 * jnp.exp(-0.5 * hidden * hidden))
            d_hidden = (slope * d_act).astype(LOW)
            dh[0:ROWS, at] = d_hidden
            sums[pl.ds(8 + quarter, 1), lanes(n, 256)] = sum_rows(d_hidden.astype(FULL))
            return carry

        lax.fori_loop(0, 3, hidden_part, 0, unroll=3)
        for args in mlp_copies(r):
            copy_of(*args).start()

    first = (beside[1], beside[2])
    second = (beside[2], beside[1])
    second_block = (mine ^ 2, mine ^ 1)
    groups = {"f1": (gf1, r1f1, r2f1, r3f1, r4f1, S_F1)}
    groups["q"] = (gq, r1q, r2q, r3q, r4q, S_Q)
    places = (depth ^ 3, depth ^ 1, depth ^ 2, depth)

    def step_one(name, route, slot):
        grads, landing, _, _, _, base = groups[name]
        block = mine ^ 3 if slot == 0 else mine ^ (1 + route)
        return grads.at[block, route], landing.at[route, slot], base + 2 * route + slot, first[route]

    def step_two(name, route, slot):
        grads, _, landing, _, _, base = groups[name]
        place = places[slot]
        return (
            grads.at[second_block[route], route, place],
            landing.at[route, place],
            base + 4 + 4 * route + slot,
            second[route],
        )

    def step_three(name, route, slot):
        grads, _, _, landing, _, base = groups[name]
        return (
            grads.at[mine, route, places[slot]],
            landing.at[route, slot],
            base + 12 + 2 * route + slot,
            along[1],
        )

    def step_four(name, route):
        grads, _, _, _, landing, base = groups[name]
        return grads.at[mine, route, depth ^ 2], landing.at[route], base + 16 + route, along[2]

    kept = (depth ^ 3, depth ^ 2, depth)

    def aside():
        return gf2.at[depth ^ 1], rzf2, S_F2, along[1]

    def f2_one(route, slot, k):
        block = mine ^ 3 if slot == 0 else mine ^ (1 + route)
        return (
            gf2.at[kept[k], block, route],
            r1f2.at[route, slot, k],
            S_F2 + 1 + 6 * slot + 3 * route + k,
            first[route],
        )

    def f2_two(route, k):
        return gf2.at[kept[k], second_block[route], route], r2f2.at[route, k], S_F2 + 13 + 3 * route + k, second[route]

    def f2_three(route):
        return gf2.at[kept[0], mine, route], r3f2.at[route], S_F2 + 19 + route, along[1]

    def f2_four(route):
        return gf2.at[kept[1], mine, route], r4f2.at[route], S_F2 + 21 + route, along[2]

    def f2_begin(*which):
        for slot in range(2):
            for k in which:
                for route in range(2):
                    send(*f2_one(route, slot, k))

    def begin(name, slot):
        for route in range(2):
            send(*step_one(name, route, slot))

    def fc1_quarter(r):
        quarter = turn(r)
        copy_of(*mlp_copies(r)[0]).wait_recv()
        at = lanes(2 * quarter + core, 384)

        total = dot(h2_t[...], dh[:, at])
        for n in range(4):
            for half in range(2):
                row = 192 * n + 96 * half
                gf1[quarter, half, n] = total[row : row + 96].astype(LOW)

        @pl.when(r == 0)
        def _():
            copy_of(*step_one("f1", 0, 0)).start()
            copy_of(*step_one("f1", 1, 0)).start()

        @pl.when(r == 1)
        def _():
            copy_of(*step_one("f1", 0, 1)).start()

        @pl.when(r == 2)
        def _():
            copy_of(*step_one("f1", 1, 1)).start()

    def fc2_quarter(r):
        quarter = turn(r)
        copy_of(*mlp_copies(r)[1]).wait_recv()
        total = dot(g_both[...].reshape(384, 512), act[:, lanes(quarter, 768)])
        for n in range(4):
            for half in range(2):
                row = 96 * n + 48 * half
                gf2[quarter, n, half] = total[row : row + 48].astype(LOW)

        @pl.when(quarter == depth ^ 1)
        def _():
            copy_of(*aside()).start()


    hidden_quarter(jnp.int32(0))
    turned = g_low[...].T
    for j in range(8):
        g_t[j // 2, j % 2, :, 0:ROWS] = turned[96 * j : 96 * j + 96]
    g_both[:, :, 0:256] = g_t[:, core]
    send(g_t.at[:, 1 - core], g_both.at[:, :, pl.ds(256, 256)], S_GT, mate)
    got(*share(h2_t, S_H2T))
    fc1_quarter(jnp.int32(0))
    got(g_t.at[:, 1 - core], g_both.at[:, :, pl.ds(256, 256)], S_GT, mate)
    fc2_quarter(jnp.int32(0))
    hidden_quarter(jnp.int32(1))

    def quarters(r, carry):
        hidden_quarter(r)
        fc1_quarter(r - 1)
        fc2_quarter(r - 1)
        return carry

    lax.fori_loop(2, 4, quarters, 0)
    fc1_quarter(jnp.int32(3))
    fc2_quarter(jnp.int32(3))
    started["mlp"] = [mlp_copies, 4, True]
    for route, slot in ROUTES:
        args = step_one("f1", route, slot)
        started[args[2]] = [lambda n, args=args: [args], 1, False]
    started["aside"] = [lambda n: [aside()], 1, False]
    f2_begin(0, 1)
    xw_t[:, 0:ROWS] = xw[...].T
    send(*share(xw_t, S_XWT))
    att_t[:, 0:ROWS] = att[...].T
    send(*share(att_t, S_AOT))

    def mlp_branch(n, carry):
        at = lanes(n, 256)
        branch = dot(act[0:ROWS, :], w2[:, at]) + biases[3:4, at]
        result_low[:, at] = (middle[:, at] + branch).astype(LOW)
        return carry + jnp.sum(branch * branch, axis=-1, keepdims=True)

    branch_square = lax.fori_loop(0, 3, mlp_branch, jnp.zeros((ROWS, 1), FULL))
    stat_mlp = sum_rows(valid_col[...] * branch_square)
    swap(result_low, result_own, S_RES)
    lane = lax.broadcasted_iota(jnp.int32, (1, 128), 1)
    stat_row = jnp.zeros((1, 128), FULL)
    for k, total in enumerate((stat_total, stat_input, stat_attn, stat_mlp)):
        stat_row = jnp.where(lane == k, total, stat_row)
    sums[12:13, 0:128] = stat_row

    def d_normed_part(n, carry):
        at = lanes(n, 256)
        d_mid[:, at] = dot_t(dh[0:ROWS, :], w1[at, :])
        return carry

    lax.fori_loop(0, 3, d_normed_part, 0)
    unit, spread_two = normed(middle[...])
    d_normed = d_mid[...]
    sums[1:2, :] = sum_rows(d_normed * unit)
    sums[7:8, :] = sum_rows(d_normed)
    d_middle = g_low[...].astype(FULL) + normed_back(d_normed, gains[1:2, :], unit, spread_two)
    d_mid[...] = d_middle
    d_low = d_middle.astype(LOW)
    d_branch[...] = d_low
    sums[4:5, :] = sum_rows(d_low.astype(FULL))

    def d_res_part(n, carry):
        at = lanes(n, 256)
        d_att[:, at] = dot_t(d_branch[...], wp[at, :]).astype(LOW)
        return carry

    lax.fori_loop(0, 3, d_res_part, 0)

    for j in range(8):
        db_pack[j % 2, 0:ROWS, 128 * (j // 2) : 128 * (j // 2) + 128] = jnp.concatenate(
            [jnp.zeros((ROWS, 32), LOW), d_branch[:, 96 * j : 96 * j + 96]], axis=1
        )

    def share_pack(buffer, index):
        return buffer.at[1 - core, pl.ds(0, ROWS)], buffer.at[1 - core, pl.ds(256, ROWS)], index, mate

    send(*share_pack(db_pack, S_DBK))

    def add_in(grads, index, landing):
        grads[index] = (grads[index].astype(FULL) + landing[...].astype(FULL)).astype(LOW)

    def run_two(name):
        grads, landing, _, _, _, _ = groups[name]
        for route in range(2):
            got(*step_one(name, route, 0))
            for slot in range(4):
                place = places[slot]
                add_in(grads, (second_block[route], route, place), landing.at[route, 0, place])
                send(*step_two(name, route, slot))

    def run_two_own(name):
        grads, landing, _, _, _, _ = groups[name]
        for route in range(2):
            got(*step_one(name, route, 1))

            def add(n, carry):
                add_in(grads, (mine, route, n), landing.at[route, 1, n])
                return carry

            lax.fori_loop(0, 4, add, 0)

    def f2_aside():
        got_all("aside")

        def add(block, carry):
            for route in range(2):
                add_in(gf2, (depth, block, route), rzf2.at[block, route])
            return carry

        lax.fori_loop(0, 4, add, 0)
        f2_begin(2)

    def f2_run_two(*which):
        for k in which:
            for route in range(2):
                got(*f2_one(route, 0, k))
                add_in(gf2, (kept[k], second_block[route], route), r1f2.at[route, 0, k])
                send(*f2_two(route, k))
        for k in which:
            for route in range(2):
                got(*f2_one(route, 1, k))
                add_in(gf2, (kept[k], mine, route), r1f2.at[route, 1, k])

    def f2_run_three(*which):
        for k in which:
            for route in range(2):
                got(*f2_two(route, k))
                add_in(gf2, (kept[k], mine, route), r2f2.at[route, k])
                if k == 0:
                    send(*f2_three(route))

    def f2_run_four():
        for route in range(2):
            got(*f2_three(route))
            add_in(gf2, (kept[1], mine, route), r3f2.at[route])
            send(*f2_four(route))

    def f2_finish():
        for route in range(2):
            got(*f2_four(route))
            out_f2[48 * route : 48 * route + 48, :] = gf2[depth, mine, route].astype(FULL) + r4f2[route].astype(FULL)

    def run_three(name):
        grads, _, landing, _, _, _ = groups[name]
        for slot in range(4):
            for route in range(2):
                got(*step_two(name, route, slot))
                add_in(grads, (mine, route, places[slot]), landing.at[route, places[slot]])
                if slot < 2:
                    send(*step_three(name, route, slot))

    def run_four(name, slots=(0, 1)):
        grads, _, _, landing, _, _ = groups[name]
        for slot in slots:
            for route in range(2):
                got(*step_three(name, route, slot))
                add_in(grads, (mine, route, places[2 + slot]), landing.at[route, slot])
                if slot == 0:
                    send(*step_four(name, route))

    def finish(name):
        grads, _, _, _, landing, _ = groups[name]
        for route in range(2):
            got(*step_four(name, route))
            total = grads[mine, route, depth].astype(FULL) + landing[route].astype(FULL)
            if name == "q":
                out_qkv[96 * route : 96 * route + 96, :] = total[:, 0:288]
                out_proj[96 * route : 96 * route + 96, :] = total[:, 288:384]
            else:
                out_f1[96 * route : 96 * route + 96, :] = total

    def attend_back(t, carry):
        at = lanes(t, 128)
        q = query[:, at]
        k = key[:, at]
        v = value[:, at]
        d_out = d_att[:, at].astype(FULL) * row_scale[:, at]
        common = (d_out * att[:, at].astype(FULL)).astype(LOW)
        d_out = d_out.astype(LOW)
        rest = jnp.zeros((KEYS - ROWS, 128), LOW)
        q_t = jnp.concatenate([q, rest], axis=0).T
        d_out_t = jnp.concatenate([d_out, rest], axis=0).T
        all_scores = []
        right = jnp.concatenate([v, jnp.full((KEYS, 128), -1.0, LOW)], axis=1)
        for h in range(4):
            d_probs = dot_t(jnp.concatenate([d_out * only[h], common * only[h]], axis=1), right)
            low_probs = probs[4 * t + h, 0:ROWS]
            d_scores = (low_probs.astype(FULL) * d_probs).astype(LOW)
            all_scores.append(d_scores)
        d_query = dot(
            jnp.concatenate(all_scores, axis=1), jnp.concatenate([k * only[h] for h in range(4)], axis=0)
        )
        four = pl.ds(4 * t, 4)
        d_value = dot(
            jnp.concatenate([d_out_t * only_row[h] for h in range(4)], axis=1),
            probs[four].reshape(4 * KEYS, KEYS),
        )
        for h in range(4):
            probs[4 * t + h, 0:ROWS] = all_scores[h]
        d_key = dot(
            jnp.concatenate([q_t * only_row[h] for h in range(4)], axis=1),
            probs[four].reshape(4 * KEYS, KEYS),
        )
        d_query = (d_query * scale).astype(LOW)
        d_key = (d_key * scale).astype(LOW).T[0:ROWS]
        d_value = d_value.astype(LOW).T[0:ROWS]
        d_proj[:, at] = d_query
        d_proj[:, lanes(6 + t, 128)] = d_key
        d_proj[:, lanes(12 + t, 128)] = d_value
        sums[2:3, at] = sum_rows(d_query.astype(FULL))
        sums[3:4, at] = sum_rows(d_value.astype(FULL))
        return carry

    run_two("f1")
    lax.fori_loop(0, 6, attend_back, 0)

    for j in range(8):
        dy_pack[j % 2, 0:ROWS, 384 * (j // 2) : 384 * (j // 2) + 384] = jnp.concatenate(
            [d_proj[:, 288 * j : 288 * j + 288], jnp.zeros((ROWS, 96), LOW)], axis=1
        )
    send(*share_pack(dy_pack, S_DYK))

    def d_win_part(n, carry):
        at = lanes(n, 256)
        d_win[:, at] = dot_t(d_proj[...], wq[at, :]).astype(LOW)
        return carry

    lax.fori_loop(0, 3, d_win_part, 0)
    unit, spread_one = normed(x_own[...])
    d_normed = d_win[...].astype(FULL)
    sums[0:1, :] = sum_rows(d_normed * unit)
    sums[6:7, :] = sum_rows(d_normed)
    d_win[...] = (d_mid[...] + normed_back(d_normed, gains[0:1, :], unit, spread_one)).astype(LOW)
    swap(d_win, d_own, S_GRAD)

    got(*share(xw_t, S_XWT))
    got(*share(att_t, S_AOT))
    got(*share_pack(db_pack, S_DBK))
    got(*share_pack(dy_pack, S_DYK))

    def qp_block(block):
        total = dot(xw_t[...], dy_pack[core, :, lanes(block, 384)])
        more = dot(att_t[...], db_pack[core, :, lanes(block, 128)])
        for n in range(4):
            for half in range(2):
                row = 192 * n + 96 * half
                cut = slice(row, row + 96)
                gq[block, half, n, :, 0:256] = total[cut, 0:256].astype(LOW)
                gq[block, half, n, :, 256:384] = (total[cut, 256:384] + more[cut]).astype(LOW)

    for block in range(4):
        qp_block(block)

    begin("q", 0)
    f2_run_two(0, 1)
    def spread_rel(head, carry):
        rows = dot(gather_t[...], probs[head, 0:ROWS]).astype(LOW)
        rel_grads[pl.ds(pl.multiple_of(64 * head, 64), 64), :] = dot(rows, offsets_t[...])
        return carry

    lax.fori_loop(0, 24, spread_rel, 0, unroll=4)

    def gather_rel(i, carry):
        start = 13 * (i // 7) + i % 7
        rows = rel_grads[pl.ds(i, 24, stride=64), :]
        return carry + pltpu.roll(jnp.concatenate([rows, jnp.zeros((24, 128), FULL)], axis=1), start, 1)

    rel_sum = lax.fori_loop(0, 49, gather_rel, jnp.zeros((24, 256), FULL), unroll=7)
    for k in range(3):
        sums[16:24, 256 * k : 256 * k + 256] = rel_sum[8 * k : 8 * k + 8, :]

    send(sums, got_core, S_AR, mate)
    run_two_own("f1")
    got(sums, got_core, S_AR, mate)
    sums_one[...] = sums[...] + got_core[...]
    for k in (1, 2, 3):
        send(sums_one, got_wide.at[k - 1], S_AR + k, beside[k])
    begin("q", 1)
    run_three("f1")
    swapped(result_low, result_own, S_RES)
    in_order(result_own[...], out_result)
    store(0, out_result, to_result)
    run_two("q")
    f2_aside()
    swapped(d_win, d_own, S_GRAD)
    in_order(d_own[...], out_tokens)
    store(1, out_tokens, to_tokens)
    f2_run_three(0, 1)
    run_four("f1")
    for k in (1, 2, 3):
        got(sums_one, got_wide.at[k - 1], S_AR + k, beside[k])
    sums_two[...] = (sums_one[...] + got_wide[0]) + (got_wide[1] + got_wide[2])
    send(sums_two, got_narrow.at[0], S_AR + 4, along[1])
    f2_run_four()
    got(sums_two, got_narrow.at[0], S_AR + 4, along[1])
    sums_three[...] = sums_two[...] + got_narrow[0]
    send(sums_three, got_narrow.at[1], S_AR + 5, along[2])
    run_two_own("q")
    run_three("q")
    finish("f1")
    store(2, out_f1, to_f1)
    run_four("q", (0,))
    f2_run_two(2)
    run_four("q", (1,))
    got(sums_three, got_narrow.at[1], S_AR + 5, along[2])
    small = sums_three[...] + got_narrow[1]
    out_gains[...] = small[0:2]
    out_biases[...] = small[2:8]
    for k in range(4):
        out_fc1_bias[:, 768 * k : 768 * k + 768] = small[8 + k : 9 + k]
    for k in range(3):
        out_rel[8 * k : 8 * k + 8, :] = small[16:24, 256 * k : 256 * k + 169]
    out_stats[...] = jnp.sqrt(small[12:13, 1:4] / (model * small[12:13, 0:1]))
    for k, (src, dst) in enumerate(
        (
            (out_gains, to_gains),
            (out_biases, to_biases),
            (out_fc1_bias, to_fc1_bias),
            (out_rel, to_rel),
            (out_stats, to_stats),
        )
    ):
        store(4 + k, src, dst)
    f2_run_three(2)
    f2_finish()
    store(3, out_f2, to_f2)
    finish("q")
    store(9, out_qkv, to_qkv)
    store(10, out_proj, to_proj)

    leave()


def fused_on_device(
    tokens, cotangent, crops, labels, norm_gains, biases, rel_table, w_qkv, w_proj, w_fc1, fc1_bias, w_fc2
):
    images, _, patches, model = tokens.shape
    hidden = w_fc1.shape[1]
    heads = rel_table.shape[1]
    vmem = pl.BlockSpec(memory_space=pltpu.VMEM)
    hbm = pl.BlockSpec(memory_space=pl.ANY)

    def low(*shape):
        return pltpu.VMEM(shape, LOW)

    def full(*shape):
        return pltpu.VMEM(shape, FULL)

    one_low = low(ROWS, model)
    one_t = low(model, ROWS)
    scratch = dict(
        wq=low(*w_qkv.shape),
        wp=low(*w_proj.shape),
        w1=low(*w_fc1.shape),
        w2=low(*w_fc2.shape),
        stack=full(256, model),
        result_low=one_low,
        x_own=full(ROWS, model),
        g_low=one_low,
        g_t=low(4, 2, 96, 256),
        g_both=low(4, 96, 512),
        tok_own=one_low,
        tok_win=one_low,
        g_own=one_low,
        result_own=one_low,
        xw=one_low,
        xw_t=low(model, 512),
        query=one_low,
        key=low(KEYS, model),
        value=low(KEYS, model),
        key_bias=low(heads, KEYS, 128),
        row_scale=full(ROWS, model),
        probs=low(heads, KEYS, KEYS),
        att=one_low,
        att_t=low(model, 512),
        middle=full(ROWS, model),
        h2=one_low,
        h2_t=low(model, 512),
        act=low(512, hidden),
        dh=low(512, hidden),
        gf1=low(4, 2, 4, 96, 384),
        gf2=low(4, 4, 2, 48, 768),
        rzf2=low(4, 2, 48, 768),
        gq=low(4, 2, 4, 96, 384),
        r1f1=low(2, 2, 4, 96, 384),
        r1f2=low(2, 2, 3, 48, 768),
        r1q=low(2, 2, 4, 96, 384),
        r2f1=low(2, 4, 96, 384),
        r2f2=low(2, 3, 48, 768),
        r3f2=low(2, 48, 768),
        r2q=low(2, 4, 96, 384),
        r3f1=low(2, 2, 96, 384),
        r3q=low(2, 2, 96, 384),
        r4f1=low(2, 96, 384),
        r4f2=low(2, 48, 768),
        r4q=low(2, 96, 384),
        d_mid=full(ROWS, model),
        d_branch=one_low,
        db_pack=low(2, 512, 512),
        d_att=one_low,
        d_proj=low(ROWS, 3 * model),
        dy_pack=low(2, 512, 1536),
        d_win=one_low,
        d_own=one_low,
        rel_rows=full(64 * 24, 128),
        rel_grads=full(64 * 24, 128),
        mask_add=full(ROWS, KEYS),
        valid_col=full(ROWS, 1),
        sums=full(24, 768),
        sums_one=full(24, 768),
        sums_two=full(24, 768),
        sums_three=full(24, 768),
        got_core=full(24, 768),
        got_wide=full(3, 24, 768),
        got_narrow=full(2, 24, 768),
        local_sem=pltpu.SemaphoreType.DMA((32,)),
        send_sem=pltpu.SemaphoreType.DMA((S_COUNT,)),
        recv_sem=pltpu.SemaphoreType.DMA((S_COUNT,)),
    )
    shapes = (
        ((patches, images, model), LOW),
        ((patches, images, model), LOW),
        ((192, 288), FULL),
        ((192, 96), FULL),
        ((192, 384), FULL),
        ((96, 768), FULL),
        ((2, model), FULL),
        ((6, model), FULL),
        ((1, hidden), FULL),
        ((heads, 169), FULL),
        ((1, 3), FULL),
    )
    inputs = (
        ((patches, images, model), LOW),
        ((patches, images, model), LOW),
        ((2, images), jnp.int32),
        ((images, patches), jnp.int32),
        ((2, model), FULL),
        ((6, model), FULL),
        ((heads, 169), FULL),
        ((1, hidden), FULL),
        ((TABLE_ROWS, 256), LOW),
        ((ROWS, 8), jnp.int32),
    )
    outs = pl.pallas_call(
        block_kernel,
        out_shape=tuple(jax.ShapeDtypeStruct(*shape) for shape in shapes),
        in_specs=[hbm] * 14,
        out_specs=[hbm] * OUTPUTS,
        scratch_shapes=[pltpu.VMEM(*shape) for shape in inputs + shapes] + list(scratch.values()),
        compiler_params=pltpu.CompilerParams(
            collective_id=0, has_side_effects=True, vmem_limit_bytes=VMEM_LIMIT
        ),
    )(
        tokens[:, 0].transpose(1, 0, 2),
        cotangent[:, 0].transpose(1, 0, 2),
        crops.T,
        labels[:, 0],
        norm_gains,
        biases,
        rel_table.T,
        w_qkv,
        w_proj,
        w_fc1,
        fc1_bias.reshape(1, hidden),
        w_fc2,
        *[jnp.asarray(table) for table in place_tables()],
    )
    outs = pl.pallas_call(
        hand_over,
        out_shape=tuple(jax.ShapeDtypeStruct(*shape) for shape in shapes),
        in_specs=[hbm] * OUTPUTS,
        out_specs=[hbm] * OUTPUTS,
        scratch_shapes=[pltpu.VMEM(*shape) for shape in shapes]
        + [pltpu.SemaphoreType.DMA((2, OUTPUTS))],
    )(*outs)
    return (
        outs[0].transpose(1, 0, 2)[:, None],
        outs[1].transpose(1, 0, 2)[:, None],
        outs[2],
        outs[3],
        outs[4],
        outs[5].T,
        outs[6],
        outs[7],
        outs[8].reshape(hidden),
        outs[9].T,
        outs[10].reshape(3),
    )


def hand_over(*refs):
    sems = refs[-1]
    held = refs[2 * OUTPUTS : 3 * OUTPUTS]
    loads = [pltpu.make_async_copy(refs[k], held[k], sems.at[0, k]) for k in range(OUTPUTS)]
    stores = [pltpu.make_async_copy(held[k], refs[OUTPUTS + k], sems.at[1, k]) for k in range(OUTPUTS)]
    for load in loads:
        load.start()
    for load, store in zip(loads, stores):
        load.wait()
        store.start()
    for store in stores:
        store.wait()


VMEM_LIMIT = 62 * 1024 * 1024


def fused(mesh):
    each = P("wide", "narrow", None, None)
    cut = P("narrow", "wide")
    return jax.shard_map(
        fused_on_device,
        mesh=mesh,
        in_specs=(each, each, P("wide", None), P("wide", "narrow", None)) + (P(),) * 8,
        out_specs=(each, each) + (cut,) * 4 + (P(),) * 5,
        check_vma=False,
    )


def solution(mesh):
    if mesh.shape["wide"] == 8 and mesh.shape["narrow"] == 4:
        return fused(mesh)
    return plain(mesh)
```

```python
from functools import partial

import jax
import jax.numpy as jnp
import numpy as np
from jax import lax
from jax.experimental import pallas as pl
from jax.experimental.pallas import tpu as pltpu
from jax.sharding import PartitionSpec as P


def from_partner(shard, axis, stride):
    return lax.ppermute(shard, axis, [(i, i ^ 1 << stride) for i in range(lax.axis_size(axis))])


def layer_norm(values, gain, shift):
    centre = jnp.mean(values, axis=-1, keepdims=True)
    centred = values - centre
    spread = jnp.mean(centred * centred, axis=-1, keepdims=True)
    return centred * lax.rsqrt(spread + 1e-05) * gain + shift


def into_window(field, swap_rows, swap_cols):
    tall = jnp.concatenate([field[:, 3:], swap_rows(field[:, :3])], axis=1)
    return jnp.concatenate([tall[:, :, 3:], swap_cols(tall[:, :, :3])], axis=2)


def out_of_window(field, swap_rows, swap_cols):
    broad = jnp.concatenate([swap_cols(field[:, :, 4:]), field[:, :, :4]], axis=2)
    return jnp.concatenate([swap_rows(broad[:, 4:]), broad[:, :4]], axis=1)


def relative_index():
    positions = jnp.arange(49, dtype=jnp.int32)
    inner_rows = positions // 7
    inner_cols = positions % 7
    return (
        (inner_rows[:, None] - inner_rows[None, :] + 6) * 13
        + inner_cols[:, None]
        - inner_cols[None, :]
        + 6
    )


def column_sum(values):
    return jnp.sum(values, axis=0, dtype=jnp.float32)


def on_device(
    tokens,
    cotangent,
    crops,
    labels,
    norm_gains,
    biases,
    rel_table,
    w_qkv,
    w_proj,
    w_fc1,
    fc1_bias,
    w_fc2,
):
    images = tokens.shape[0]
    model_width = tokens.shape[-1]
    head_count = rel_table.shape[1]
    head_size = model_width // head_count
    rows_all = images * 49
    score_scale = head_size ** (-0.5)
    where_narrow = lax.axis_index("narrow")
    row_half = where_narrow // 2
    col_half = where_narrow % 2
    positions = jnp.arange(49, dtype=jnp.int32)
    own_row = 7 * row_half + positions // 7
    own_col = 7 * col_half + positions % 7
    shift_row = (own_row + 3) % 14
    shift_col = (own_col + 3) % 14
    valid_own = (own_row[None] < crops[:, 0:1]) & (own_col[None] < crops[:, 1:2])
    valid_shift = (shift_row[None] < crops[:, 0:1]) & (shift_col[None] < crops[:, 1:2])
    label_rows = labels[:, 0]
    allowed = (label_rows[:, :, None] == label_rows[:, None, :]) & valid_shift[
        :, None, :
    ] | jnp.eye(49, dtype=bool)[None]
    allowed_heads = allowed[:, None]
    inputs = tokens[:, 0].astype(jnp.float32)
    normed, ln1_back = jax.vjp(layer_norm, inputs, norm_gains[0], biases[4])
    normed_low = normed.astype(jnp.bfloat16).reshape(images, 7, 7, model_width)
    windows = into_window(
        normed_low,
        lambda strip: from_partner(strip, "narrow", 1),
        lambda strip: from_partner(strip, "narrow", 0),
    ).reshape(rows_all, model_width)
    projected = jnp.dot(windows, w_qkv, preferred_element_type=jnp.float32)
    head_shape = (images, 49, head_count, head_size)
    query_rows = (projected[:, :model_width] + biases[0]).astype(jnp.bfloat16).reshape(head_shape)
    key_rows = projected[:, model_width : 2 * model_width].astype(jnp.bfloat16).reshape(head_shape)
    value_rows = (
        (projected[:, 2 * model_width :] + biases[1]).astype(jnp.bfloat16).reshape(head_shape)
    )
    one_hot = (
        (relative_index()[:, :, None] == jnp.arange(169, dtype=jnp.int32))
        .reshape(2401, 169)
        .astype(jnp.float32)
    )
    bias_table = (
        jnp.dot(one_hot, rel_table, precision=lax.Precision.HIGHEST)
        .reshape(49, 49, head_count)
        .transpose(2, 0, 1)
    )

    def masked_scores():
        raw = jnp.einsum(
            "nphe,nqhe->nhpq", query_rows, key_rows, preferred_element_type=jnp.float32
        )
        return jnp.where(allowed_heads, raw * score_scale + bias_table[None], -1000000000.0)

    masked = masked_scores()
    row_top = jnp.max(masked, axis=-1, keepdims=True)
    log_total = row_top + jnp.log(jnp.sum(jnp.exp(masked - row_top), axis=-1, keepdims=True))
    attn_probs = jnp.exp(masked - log_total)
    probs_low = attn_probs.astype(jnp.bfloat16)
    attended = jnp.einsum(
        "nhpq,nqhe->nphe", probs_low, value_rows, preferred_element_type=jnp.float32
    ).astype(jnp.bfloat16)
    restored = out_of_window(
        attended.reshape(images, 7, 7, model_width),
        lambda strip: from_partner(strip, "narrow", 1),
        lambda strip: from_partner(strip, "narrow", 0),
    ).reshape(rows_all, model_width)
    branch_attn = jnp.dot(restored, w_proj, preferred_element_type=jnp.float32) + biases[2]
    middle = inputs.reshape(rows_all, model_width) + branch_attn
    normed_two, ln2_back = jax.vjp(layer_norm, middle, norm_gains[1], biases[5])
    normed_two_low = normed_two.astype(jnp.bfloat16)
    hidden = jnp.dot(normed_two_low, w_fc1, preferred_element_type=jnp.float32) + fc1_bias
    activated, gelu_back = jax.vjp(partial(jax.nn.gelu, approximate=False), hidden)
    activated_low = activated.astype(jnp.bfloat16)
    branch_mlp = jnp.dot(activated_low, w_fc2, preferred_element_type=jnp.float32) + biases[3]
    result = (middle + branch_mlp).astype(jnp.bfloat16).reshape(images, 1, 49, model_width)
    cot_rows = cotangent.reshape(rows_all, model_width)
    grad_fc2 = jnp.dot(activated_low.T, cot_rows, preferred_element_type=jnp.float32)
    d_activated = jnp.dot(cot_rows, w_fc2.T, preferred_element_type=jnp.float32)
    (d_hidden,) = gelu_back(d_activated)
    d_hidden_low = d_hidden.astype(jnp.bfloat16)
    grad_fc1 = jnp.dot(normed_two_low.T, d_hidden_low, preferred_element_type=jnp.float32)
    grad_fc1_bias = column_sum(d_hidden_low)
    d_normed_two = jnp.dot(d_hidden_low, w_fc1.T, preferred_element_type=jnp.float32)
    d_middle_norm, d_gain_two, d_shift_two = ln2_back(d_normed_two)
    d_middle = cot_rows.astype(jnp.float32) + d_middle_norm
    d_branch = d_middle.astype(jnp.bfloat16)
    grad_proj = jnp.dot(restored.T, d_branch, preferred_element_type=jnp.float32)
    d_restored = jnp.dot(d_branch, w_proj.T, preferred_element_type=jnp.float32).astype(
        jnp.bfloat16
    )
    d_attended = into_window(
        d_restored.reshape(images, 7, 7, model_width),
        lambda strip: from_partner(strip, "narrow", 1),
        lambda strip: from_partner(strip, "narrow", 0),
    ).reshape(head_shape)
    again = jnp.exp(masked_scores() - log_total)
    d_probs = jnp.einsum(
        "nphe,nqhe->nhpq", d_attended, value_rows, preferred_element_type=jnp.float32
    )
    d_scores = (again * (d_probs - jnp.sum(again * d_probs, axis=-1, keepdims=True))).astype(
        jnp.bfloat16
    )
    d_table = jnp.sum(d_scores, axis=0, dtype=jnp.float32).reshape(head_count, 2401)
    grad_rel = jnp.dot(d_table, one_hot, precision=lax.Precision.HIGHEST).T
    d_query = (
        jnp.einsum("nhpq,nqhe->nphe", d_scores, key_rows, preferred_element_type=jnp.float32)
        * score_scale
    ).astype(jnp.bfloat16)
    d_key = (
        jnp.einsum("nhpq,nphe->nqhe", d_scores, query_rows, preferred_element_type=jnp.float32)
        * score_scale
    ).astype(jnp.bfloat16)
    d_value = jnp.einsum(
        "nhpq,nphe->nqhe", probs_low, d_attended, preferred_element_type=jnp.float32
    ).astype(jnp.bfloat16)
    d_projected = jnp.concatenate(
        [
            d_query.reshape(rows_all, model_width),
            d_key.reshape(rows_all, model_width),
            d_value.reshape(rows_all, model_width),
        ],
        axis=1,
    )
    grad_qkv = jnp.dot(windows.T, d_projected, preferred_element_type=jnp.float32)
    d_windows = jnp.dot(d_projected, w_qkv.T, preferred_element_type=jnp.float32).astype(
        jnp.bfloat16
    )
    d_normed = out_of_window(
        d_windows.reshape(images, 7, 7, model_width),
        lambda strip: from_partner(strip, "narrow", 1),
        lambda strip: from_partner(strip, "narrow", 0),
    ).reshape(images, 49, model_width)
    d_inputs_norm, d_gain_one, d_shift_one = ln1_back(d_normed.astype(jnp.float32))
    grad_tokens = (
        (d_middle.reshape(images, 49, model_width) + d_inputs_norm)
        .astype(jnp.bfloat16)
        .reshape(images, 1, 49, model_width)
    )
    grad_biases = jnp.stack(
        [
            column_sum(d_query.reshape(rows_all, model_width)),
            column_sum(d_value.reshape(rows_all, model_width)),
            column_sum(d_branch),
            column_sum(cot_rows),
            d_shift_one,
            d_shift_two,
        ]
    )
    grad_gains = jnp.stack([d_gain_one, d_gain_two])
    valid_weight = valid_own.astype(jnp.float32).reshape(rows_all)
    flat_inputs = inputs.reshape(rows_all, model_width)
    stat_sums = jnp.stack(
        [
            jnp.sum(valid_weight),
            jnp.sum(valid_weight * jnp.sum(flat_inputs * flat_inputs, axis=-1)),
            jnp.sum(valid_weight * jnp.sum(branch_attn * branch_attn, axis=-1)),
            jnp.sum(valid_weight * jnp.sum(branch_mlp * branch_mlp, axis=-1)),
        ]
    )
    grad_biases, grad_gains, grad_fc1_bias, grad_rel, stat_sums = lax.psum(
        (grad_biases, grad_gains, grad_fc1_bias, grad_rel, stat_sums), ("wide", "narrow")
    )
    stats = jnp.sqrt(stat_sums[1:] / (model_width * stat_sums[0]))
    matrices = (grad_qkv, grad_proj, grad_fc1, grad_fc2)
    partial_sums = (
        lax.psum_scatter(matrices[0], "wide", scatter_dimension=1, tiled=True),
        lax.psum_scatter(matrices[1], "wide", scatter_dimension=1, tiled=True),
        lax.psum_scatter(matrices[2], "wide", scatter_dimension=1, tiled=True),
        lax.psum_scatter(matrices[3], "wide", scatter_dimension=1, tiled=True),
    )
    reduced = (
        lax.psum_scatter(
            partial_sums[0].astype(jnp.bfloat16), "narrow", scatter_dimension=0, tiled=True
        ).astype(jnp.float32),
        lax.psum_scatter(
            partial_sums[1].astype(jnp.bfloat16), "narrow", scatter_dimension=0, tiled=True
        ).astype(jnp.float32),
        lax.psum_scatter(
            partial_sums[2].astype(jnp.bfloat16), "narrow", scatter_dimension=0, tiled=True
        ).astype(jnp.float32),
        lax.psum_scatter(
            partial_sums[3].astype(jnp.bfloat16), "narrow", scatter_dimension=0, tiled=True
        ).astype(jnp.float32),
    )
    grad_qkv, grad_proj, grad_fc1, grad_fc2 = reduced
    return (
        result,
        grad_tokens,
        grad_qkv,
        grad_proj,
        grad_fc1,
        grad_fc2,
        grad_gains,
        grad_biases,
        grad_fc1_bias,
        grad_rel,
        stats,
    )


def plain(mesh):
    return jax.shard_map(
        on_device,
        mesh=mesh,
        in_specs=(
            P("wide", "narrow", None, None),
            P("wide", "narrow", None, None),
            P("wide", None),
            P("wide", "narrow", None),
            P(),
            P(),
            P(),
            P(),
            P(),
            P(),
            P(),
            P(),
        ),
        out_specs=(
            P("wide", "narrow", None, None),
            P("wide", "narrow", None, None),
            P("narrow", "wide"),
            P("narrow", "wide"),
            P("narrow", "wide"),
            P("narrow", "wide"),
            P(),
            P(),
            P(),
            P(),
            P(),
        ),
        check_vma=False,
    )


ROWS = 208
KEYS = 256
T_OWN, T_BACK, T_PICK, T_SPREAD, T_OFFSETS, T_GATHER, T_REPEAT = 0, 208, 464, 720, 928, 1184, 1248
TABLE_ROWS = 1504
MESH = pl.DeviceIdType.MESH
LOW = jnp.bfloat16
FULL = jnp.float32


def place_tables():
    places = []
    for tall, broad in ((0, 0), (1, 0), (0, 1), (1, 1)):
        for image in range(4):
            for i in range(4, 7) if tall else range(4):
                for j in range(4, 7) if broad else range(4):
                    places.append((image, i, j, i - 4 if tall else i + 3, j - 4 if broad else j + 3))
    own = np.zeros((ROWS, 256), np.float32)
    spread = np.zeros((ROWS, 128), np.float32)
    pick = np.zeros((256, 128), np.float32)
    repeat = np.zeros((KEYS, 64), np.float32)
    for spot in range(49):
        for lane in (spot, 64 + spot):
            pick[13 * (spot // 7) + spot % 7, lane] = 1
            pick[128 + 13 * (spot // 7) + spot % 7, lane] = 1
    gather = np.zeros((64, ROWS), np.float32)
    offsets = np.zeros((KEYS, 128), np.float32)
    info = np.zeros((ROWS, 8), np.int32)
    info[:, 3] = -1
    for row in range(ROWS):
        if row >= len(places):
            info[row, 0] = 4 + row - len(places)
            continue
        image, i, j, a, b = places[row]
        own[row, 4 * (7 * a + b) + image] = 1
        spread[row, 7 * i + j] = 1
        spread[row, 64 + 7 * i + j] = 1
        shift = (6 - i) * 13 + 6 - j
        repeat[row, 7 * i + j] = 1
        gather[7 * i + j, row] = 1
        offsets[row, shift] = 1
        info[row, :6] = (image, i, j, 7 * i + j, a, b)
    table = np.zeros((TABLE_ROWS, 256), np.float32)
    table[T_OWN : T_OWN + ROWS] = own
    table[T_BACK : T_BACK + 256, :ROWS] = own.T
    table[T_PICK : T_PICK + 256, :128] = pick
    table[T_REPEAT : T_REPEAT + KEYS, :64] = repeat
    table[T_SPREAD : T_SPREAD + ROWS, :128] = spread
    table[T_OFFSETS : T_OFFSETS + KEYS, :128] = offsets
    table[T_GATHER : T_GATHER + 64, :ROWS] = gather
    return table.astype(jnp.bfloat16), info


def dot(left, right):
    return jnp.dot(left, right, preferred_element_type=FULL)


def dot_t(left, right):
    return lax.dot_general(left, right, (((1,), (1,)), ((), ())), preferred_element_type=FULL)


def lanes(index, width):
    return pl.ds(pl.multiple_of(index * width, width), width)


def normed(values):
    centred = values - jnp.mean(values, axis=-1, keepdims=True)
    scale = lax.rsqrt(jnp.mean(centred * centred, axis=-1, keepdims=True) + 1e-05)
    return centred * scale, scale


def normed_back(grad, gain, unit, scale):
    inner = grad * gain
    along = jnp.mean(inner, axis=-1, keepdims=True)
    across = jnp.mean(inner * unit, axis=-1, keepdims=True)
    return scale * (inner - along - unit * across)


def sum_rows(values):
    return jnp.sum(values, axis=0, keepdims=True)


GROUPS = ((64, 48), (112, 48), (160, 48))

S_TOK = 0
S_COT = 3
S_RES = 6
S_GRAD = 9
S_GT = 12
S_XWT = 13
S_AOT = 14
S_H2T = 15
S_ACT = 16
S_DH = 20
S_DBK = 24
S_DYK = 25
S_AR = 26
S_F1 = 33
S_F2 = 51
S_Q = 75
S_COUNT = 93
OUTPUTS = 11
ROUTES = ((0, 0), (1, 0), (0, 1), (1, 1))


def block_kernel(
    tokens_hbm,
    cotangent_hbm,
    crops_hbm,
    labels_hbm,
    gains_hbm,
    biases_hbm,
    rel_hbm,
    wq_hbm,
    wp_hbm,
    w1_hbm,
    fc1_bias_hbm,
    w2_hbm,
    table_hbm,
    info_hbm,
    to_result,
    to_tokens,
    to_qkv,
    to_proj,
    to_f1,
    to_f2,
    to_gains,
    to_biases,
    to_fc1_bias,
    to_rel,
    to_stats,
    tokens,
    cotangent,
    crops,
    labels,
    gains,
    biases,
    rel_table,
    fc1_bias,
    table,
    info,
    out_result,
    out_tokens,
    out_qkv,
    out_proj,
    out_f1,
    out_f2,
    out_gains,
    out_biases,
    out_fc1_bias,
    out_rel,
    out_stats,
    wq,
    wp,
    w1,
    w2,
    stack,
    result_low,
    x_own,
    g_low,
    g_t,
    g_both,
    tok_own,
    tok_win,
    g_own,
    result_own,
    xw,
    xw_t,
    query,
    key,
    value,
    key_bias,
    row_scale,
    probs,
    att,
    att_t,
    middle,
    h2,
    h2_t,
    act,
    dh,
    gf1,
    gf2,
    rzf2,
    gq,
    r1f1,
    r1f2,
    r1q,
    r2f1,
    r2f2,
    r3f2,
    r2q,
    r3f1,
    r3q,
    r4f1,
    r4f2,
    r4q,
    d_mid,
    d_branch,
    db_pack,
    d_att,
    d_proj,
    dy_pack,
    d_win,
    d_own,
    rel_rows,
    rel_grads,
    mask_add,
    valid_col,
    sums,
    sums_one,
    sums_two,
    sums_three,
    sums_all,
    got_core,
    got_wide,
    got_narrow,
    local_sem,
    send_sem,
    recv_sem,
):
    model = x_own.shape[1]
    width = lax.axis_index("wide")
    depth = lax.axis_index("narrow")
    core = width % 2
    mine = width // 2
    mate = {"wide": width ^ 1, "narrow": depth}
    beside = [None] + [{"wide": width ^ (2 * k), "narrow": depth} for k in (1, 2, 3)]
    along = [None] + [{"wide": width, "narrow": depth ^ k} for k in (1, 2, 3)]
    partners = [mate] + beside[1:] + along[1:]
    quadrant = (along[2], along[1], along[3])

    started = {}

    def copy_of(src, dst, index, device):
        return pltpu.make_async_remote_copy(
            src_ref=src,
            dst_ref=dst,
            send_sem=send_sem.at[index],
            recv_sem=recv_sem.at[index],
            device_id=device,
            device_id_type=MESH,
        )

    def send(*args):
        copy_of(*args).start()
        started[args[2]] = [lambda n: [args], 1, False]

    def got(*args):
        copy_of(*args).wait_recv()
        started[args[2]][2] = True

    def each(copies, count, act):
        def step(n, carry):
            for args in copies(n):
                act(copy_of(*args))
            return carry

        if count == 1:
            step(0, 0)
        else:
            lax.fori_loop(0, count, step, 0)

    def got_all(name):
        copies, count, _ = started[name]
        each(copies, count, lambda copy: copy.wait_recv())
        started[name][2] = True

    def leave():
        for copies, count, arrived in started.values():
            if not arrived:
                each(copies, count, lambda copy: copy.wait_recv())
        for copies, count, _ in started.values():
            each(copies, count, lambda copy: copy.wait_send())
        for copy in stores:
            copy.wait()

    barrier = pltpu.get_barrier_semaphore()
    for partner in partners:
        pl.semaphore_signal(barrier, inc=1, device_id=partner, device_id_type=MESH)
    pairs = ((wq_hbm, wq), (wp_hbm, wp), (w1_hbm, w1), (w2_hbm, w2))
    pairs += ((tokens_hbm, tokens), (table_hbm, table), (gains_hbm, gains), (biases_hbm, biases))
    pairs += ((cotangent_hbm, cotangent), (info_hbm, info), (crops_hbm, crops), (labels_hbm, labels))
    pairs += ((rel_hbm, rel_table), (fc1_bias_hbm, fc1_bias))
    loads = [pltpu.make_async_copy(src, dst, local_sem.at[k]) for k, (src, dst) in enumerate(pairs)]
    for load in loads[4:] + loads[:4]:
        load.start()
    own_t = table.at[pl.ds(T_OWN, ROWS), :]
    back_t = table.at[pl.ds(T_BACK, 256), pl.ds(0, ROWS)]
    pick_t = table.at[pl.ds(T_PICK, 256), pl.ds(0, 128)]
    repeat_t = table.at[pl.ds(T_REPEAT, KEYS), pl.ds(0, 64)]
    spread_t = table.at[pl.ds(T_SPREAD, ROWS), pl.ds(0, 128)]
    offsets_t = table.at[pl.ds(T_OFFSETS, KEYS), pl.ds(0, 128)]
    gather_t = table.at[pl.ds(T_GATHER, 64), pl.ds(0, ROWS)]

    def store(k, src, dst):
        copy = pltpu.make_async_copy(src, dst, local_sem.at[len(pairs) + k])
        copy.start()
        stores.append(copy)

    stores = []

    def in_places(source):
        stack[192:256, :] = jnp.zeros((64, model), FULL)
        for patch in range(49):
            stack[4 * patch : 4 * patch + 4, :] = source[patch].astype(FULL)
        return dot(own_t[...], stack[...].astype(LOW))

    def in_order(values, out):
        stack[...] = dot(back_t[...], values)
        for patch in range(49):
            out[patch] = stack[4 * patch : 4 * patch + 4, :].astype(LOW)

    def swap(src, dst, base):
        dst[0:64, :] = src[0:64, :]
        for k in (2, 0, 1):
            row, count = GROUPS[k]
            rows = pl.ds(row, count)
            send(src.at[rows], dst.at[rows], base + k, quadrant[k])

    def swapped(src, dst, base):
        for k, (row, count) in enumerate(GROUPS):
            rows = pl.ds(row, count)
            got(src.at[rows], dst.at[rows], base + k, quadrant[k])

    for load in loads[4:8]:
        load.wait()
    tok_own[...] = in_places(tokens).astype(LOW)
    pl.semaphore_wait(barrier, len(partners))
    swap(tok_own, tok_win, S_TOK)

    for load in loads[8:]:
        load.wait()
    g_value = in_places(cotangent)
    g_own[...] = g_value.astype(LOW)
    for buffer in (xw_t, att_t, h2_t):
        buffer[:, 128:256] = jnp.zeros((model, 128), LOW)
    for buffer in (act, dh, dy_pack.at[0], dy_pack.at[1], db_pack.at[0], db_pack.at[1]):
        for row in (ROWS, 256 + ROWS):
            buffer[row : row + 48, :] = jnp.zeros((48, buffer.shape[1]), LOW)
    g_t[...] = jnp.zeros_like(g_t)

    sums[...] = jnp.zeros_like(sums)
    sums[5:6, :] = sum_rows(g_value)

    row_half = depth // 2
    col_half = depth % 2
    image_col = info[:, 0:1]
    i_col = info[:, 1:2]
    j_col = info[:, 2:3]
    place_col = info[:, 3:4]
    zero_col = jnp.zeros((ROWS, 1), jnp.int32)
    crop_row = zero_col
    crop_col = zero_col
    label = jnp.zeros((ROWS, 1), FULL)
    lane49 = lax.broadcasted_iota(jnp.int32, (ROWS, 49), 1)
    for image in range(4):
        is_image = image_col == image
        crop_row = jnp.where(is_image, crops[0:1, image : image + 1], crop_row)
        crop_col = jnp.where(is_image, crops[1:2, image : image + 1], crop_col)
        picked = jnp.where(
            lane49 == place_col, labels[image : image + 1, :].astype(FULL), jnp.zeros((ROWS, 49), FULL)
        )
        label = jnp.where(is_image, jnp.sum(picked, axis=1, keepdims=True), label)
    shift_row = 7 * row_half + i_col + 3
    shift_row = jnp.where(shift_row >= 14, shift_row - 14, shift_row)
    shift_col = 7 * col_half + j_col + 3
    shift_col = jnp.where(shift_col >= 14, shift_col - 14, shift_col)
    valid_key = (shift_row < crop_row) & (shift_col < crop_col)
    valid_value = jnp.where(valid_key, 1.0, 0.0).astype(FULL)
    valid_col[...] = valid_value
    code = label + 8.0 * image_col.astype(FULL)
    key_code = jnp.where(valid_key, code, -1.0)
    diagonal = lax.broadcasted_iota(jnp.int32, (ROWS, KEYS), 0) == lax.broadcasted_iota(
        jnp.int32, (ROWS, KEYS), 1
    )
    key_row = jnp.sum(jnp.where(diagonal, key_code + 2.0, 0.0), axis=0, keepdims=True) - 2.0
    mask_add[...] = jnp.where((code == key_row) | diagonal, 0.0, -1000000000.0)

    rel_wide = jnp.concatenate([rel_table[...] * 32**0.5, jnp.zeros((24, 87), FULL)], axis=1)
    rel_rows[1176:1536, :] = jnp.zeros((360, 128), FULL)

    def shifted(spot, carry):
        start = 84 - 13 * (spot // 7) - spot % 7
        rel_rows[pl.ds(pl.multiple_of(24 * spot, 8), 24), :] = pltpu.roll(rel_wide, 256 - start, 1)[:, 0:128]
        return carry

    lax.fori_loop(0, 49, shifted, 0, unroll=7)

    def picked_rows(n, carry):
        rows = pl.ds(pl.multiple_of(168 * n, 8), 168)
        values = rel_rows[rows, :]
        high = values.astype(LOW)
        below = (values - high.astype(FULL)).astype(LOW)
        rel_rows[rows, :] = dot(jnp.concatenate([high, below], axis=1), pick_t[...])
        return carry

    lax.fori_loop(0, 7, picked_rows, 0)
    is_high = lax.broadcasted_iota(jnp.int32, (64, 128), 1) < 64

    def head_bias(head, carry):
        values = rel_rows[pl.ds(head, 64, stride=24), :]
        high = values.astype(LOW).astype(FULL)
        parts = jnp.where(is_high, high, values - high).astype(LOW)
        key_bias[head] = dot(repeat_t[...], parts).astype(LOW)
        return carry

    lax.fori_loop(0, 24, head_bias, 0, unroll=4)

    key[ROWS:KEYS, :] = jnp.zeros((KEYS - ROWS, model), LOW)
    value[ROWS:KEYS, :] = jnp.zeros((KEYS - ROWS, model), LOW)
    swapped(tok_own, tok_win, S_TOK)
    swap(g_own, g_low, S_COT)
    flat = tok_win[...].astype(FULL)
    x_own[...] = flat
    unit, _ = normed(flat)
    xw[...] = (unit * gains[0:1, :] + biases[4:5, :]).astype(LOW)
    stat_total = jnp.sum(valid_value, axis=0, keepdims=True)
    stat_input = sum_rows(valid_value * jnp.sum(flat * flat, axis=-1, keepdims=True))

    loads[0].wait()

    def project(n, carry):
        at = lanes(n, 256)
        window = xw[...]
        query[:, at] = (dot(window, wq[:, at]) + biases[0:1, at]).astype(LOW)
        key[0:ROWS, at] = dot(window, wq[:, lanes(n + 3, 256)]).astype(LOW)
        value[0:ROWS, at] = (dot(window, wq[:, lanes(n + 6, 256)]) + biases[1:2, at]).astype(LOW)
        return carry

    lax.fori_loop(0, 3, project, 0, unroll=3)

    lane_head = lax.broadcasted_iota(jnp.int32, (1, 128), 1) // 32
    only = [(lane_head == h).astype(FULL).astype(LOW) for h in range(4)]
    row_head = lax.broadcasted_iota(jnp.int32, (128, 1), 0) // 32
    only_row = [(row_head == h).astype(FULL).astype(LOW) for h in range(4)]
    scale = 32 ** (-0.5)

    def attend(t, carry):
        at = lanes(t, 128)
        q = query[:, at]
        k = key[:, at]
        v = value[:, at]
        powers = []
        right = []
        for h in range(4):
            left = jnp.concatenate([q * only[h], spread_t[...]], axis=1)
            scores = dot_t(left, jnp.concatenate([k, key_bias[4 * t + h]], axis=1)) + mask_add[...]
            top = jnp.max(scores, axis=-1, keepdims=True)
            power = jnp.exp2((scores - top) * (scale * 1.4426950408889634)).astype(LOW)
            probs[4 * t + h, 0:ROWS] = power
            probs[4 * t + h, ROWS:KEYS] = jnp.zeros((KEYS - ROWS, KEYS), LOW)
            powers.append(power)
            right.append(jnp.concatenate([v * only[h], jnp.ones((KEYS, 128), LOW) * only[h]], axis=1))
        both = dot(jnp.concatenate(powers, axis=1), jnp.concatenate(right, axis=0))
        total = both[:, 0:128]
        below = 1.0 / both[:, 128:256]
        row_scale[:, at] = below
        total = (total * below).astype(LOW)
        att[:, at] = total
        return carry

    lax.fori_loop(0, 6, attend, 0)

    def share(buffer, index):
        return buffer.at[:, pl.ds(0, 256)], buffer.at[:, pl.ds(256, 256)], index, mate

    loads[1].wait()

    def attn_branch(n, carry):
        at = lanes(n, 256)
        branch = dot(att[...], wp[:, at]) + biases[2:3, at]
        middle[:, at] = x_own[:, at] + branch
        return carry + jnp.sum(branch * branch, axis=-1, keepdims=True)

    branch_square = lax.fori_loop(0, 3, attn_branch, jnp.zeros((ROWS, 1), FULL), unroll=3)
    stat_attn = sum_rows(valid_col[...] * branch_square)

    unit, _ = normed(middle[...])
    h2[...] = (unit * gains[1:2, :] + biases[5:6, :]).astype(LOW)
    h2_t[:, 0:ROWS] = h2[...].T
    send(*share(h2_t, S_H2T))
    loads[2].wait()
    loads[3].wait()
    swapped(g_own, g_low, S_COT)

    def turn(r):
        return mine ^ jnp.where(r == 0, 3, jnp.where(r == 3, 0, r))

    def mlp_copies(r):
        at = lanes(turn(r), 768)
        return [
            (dh.at[pl.ds(0, ROWS), at], dh.at[pl.ds(256, ROWS), at], S_DH + r, mate),
            (act.at[pl.ds(0, ROWS), at], act.at[pl.ds(256, ROWS), at], S_ACT + r, mate),
        ]

    def hidden_quarter(r):
        quarter = turn(r)

        def hidden_part(n, carry):
            at = lanes(quarter * 3 + n, 256)
            hidden = dot(h2[...], w1[:, at]) + fc1_bias[:, at]
            d_act = dot_t(g_low[...], w2[at, :])
            below = 0.5 + 0.5 * lax.erf(hidden * 0.7071067811865476)
            act[0:ROWS, at] = (hidden * below).astype(LOW)
            slope = below + hidden * (0.3989422804014327 * jnp.exp(-0.5 * hidden * hidden))
            d_hidden = (slope * d_act).astype(LOW)
            dh[0:ROWS, at] = d_hidden
            sums[pl.ds(8 + quarter, 1), lanes(n, 256)] = sum_rows(d_hidden.astype(FULL))
            return carry

        lax.fori_loop(0, 3, hidden_part, 0, unroll=3)
        for args in mlp_copies(r):
            copy_of(*args).start()

    first = (beside[1], beside[2])
    second = (beside[2], beside[1])
    second_block = (mine ^ 2, mine ^ 1)
    groups = {"f1": (gf1, r1f1, r2f1, r3f1, r4f1, S_F1)}
    groups["q"] = (gq, r1q, r2q, r3q, r4q, S_Q)
    places = (depth ^ 3, depth ^ 1, depth ^ 2, depth)

    def step_one(name, route, slot):
        grads, landing, _, _, _, base = groups[name]
        block = mine ^ 3 if slot == 0 else mine ^ (1 + route)
        return grads.at[block, route], landing.at[route, slot], base + 2 * route + slot, first[route]

    def step_two(name, route, slot):
        grads, _, landing, _, _, base = groups[name]
        place = places[slot]
        return (
            grads.at[second_block[route], route, place],
            landing.at[route, place],
            base + 4 + 4 * route + slot,
            second[route],
        )

    def step_three(name, route, slot):
        grads, _, _, landing, _, base = groups[name]
        return (
            grads.at[mine, route, places[slot]],
            landing.at[route, slot],
            base + 12 + 2 * route + slot,
            along[1],
        )

    def step_four(name, route):
        grads, _, _, _, landing, base = groups[name]
        return grads.at[mine, route, depth ^ 2], landing.at[route], base + 16 + route, along[2]

    kept = (depth ^ 3, depth ^ 2, depth)

    def aside():
        return gf2.at[depth ^ 1], rzf2, S_F2, along[1]

    def f2_one(route, slot, k):
        block = mine ^ 3 if slot == 0 else mine ^ (1 + route)
        return (
            gf2.at[kept[k], block, route],
            r1f2.at[route, slot, k],
            S_F2 + 1 + 6 * slot + 3 * route + k,
            first[route],
        )

    def f2_two(route, k):
        return gf2.at[kept[k], second_block[route], route], r2f2.at[route, k], S_F2 + 13 + 3 * route + k, second[route]

    def f2_three(route):
        return gf2.at[kept[0], mine, route], r3f2.at[route], S_F2 + 19 + route, along[1]

    def f2_four(route):
        return gf2.at[kept[1], mine, route], r4f2.at[route], S_F2 + 21 + route, along[2]

    def f2_begin(*which):
        for slot in range(2):
            for k in which:
                for route in range(2):
                    send(*f2_one(route, slot, k))

    def begin(name, slot):
        for route in range(2):
            send(*step_one(name, route, slot))

    def fc1_quarter(r):
        quarter = turn(r)
        copy_of(*mlp_copies(r)[0]).wait_recv()
        at = lanes(2 * quarter + core, 384)

        total = dot(h2_t[...], dh[:, at])
        for n in range(4):
            for half in range(2):
                row = 192 * n + 96 * half
                gf1[quarter, half, n] = total[row : row + 96].astype(LOW)

        @pl.when(r == 0)
        def _():
            copy_of(*step_one("f1", 0, 0)).start()
            copy_of(*step_one("f1", 1, 0)).start()

        @pl.when(r == 1)
        def _():
            copy_of(*step_one("f1", 0, 1)).start()

        @pl.when(r == 2)
        def _():
            copy_of(*step_one("f1", 1, 1)).start()

    def fc2_quarter(r):
        quarter = turn(r)
        copy_of(*mlp_copies(r)[1]).wait_recv()
        total = dot(g_both[...].reshape(384, 512), act[:, lanes(quarter, 768)])
        for n in range(4):
            for half in range(2):
                row = 96 * n + 48 * half
                gf2[quarter, n, half] = total[row : row + 48].astype(LOW)

        @pl.when(quarter == depth ^ 1)
        def _():
            copy_of(*aside()).start()


    hidden_quarter(jnp.int32(0))
    turned = g_low[...].T
    for j in range(8):
        g_t[j // 2, j % 2, :, 0:ROWS] = turned[96 * j : 96 * j + 96]
    g_both[:, :, 0:256] = g_t[:, core]
    send(g_t.at[:, 1 - core], g_both.at[:, :, pl.ds(256, 256)], S_GT, mate)
    got(*share(h2_t, S_H2T))
    fc1_quarter(jnp.int32(0))
    got(g_t.at[:, 1 - core], g_both.at[:, :, pl.ds(256, 256)], S_GT, mate)
    fc2_quarter(jnp.int32(0))
    hidden_quarter(jnp.int32(1))

    def quarters(r, carry):
        hidden_quarter(r)
        fc1_quarter(r - 1)
        fc2_quarter(r - 1)
        return carry

    lax.fori_loop(2, 4, quarters, 0)
    fc1_quarter(jnp.int32(3))
    fc2_quarter(jnp.int32(3))
    started["mlp"] = [mlp_copies, 4, True]
    for route, slot in ROUTES:
        args = step_one("f1", route, slot)
        started[args[2]] = [lambda n, args=args: [args], 1, False]
    started["aside"] = [lambda n: [aside()], 1, False]
    f2_begin(0, 1)
    xw_t[:, 0:ROWS] = xw[...].T
    send(*share(xw_t, S_XWT))
    att_t[:, 0:ROWS] = att[...].T
    send(*share(att_t, S_AOT))

    def d_normed_part(n, carry):
        at = lanes(n, 256)
        d_mid[:, at] = dot_t(dh[0:ROWS, :], w1[at, :])
        return carry

    lax.fori_loop(0, 3, d_normed_part, 0)
    unit, spread_two = normed(middle[...])
    d_normed = d_mid[...]
    sums[1:2, :] = sum_rows(d_normed * unit)
    sums[7:8, :] = sum_rows(d_normed)
    d_middle = g_low[...].astype(FULL) + normed_back(d_normed, gains[1:2, :], unit, spread_two)
    d_mid[...] = d_middle
    d_low = d_middle.astype(LOW)
    d_branch[...] = d_low
    sums[4:5, :] = sum_rows(d_low.astype(FULL))

    def d_res_part(n, carry):
        at = lanes(n, 256)
        d_att[:, at] = dot_t(d_branch[...], wp[at, :]).astype(LOW)
        return carry

    lax.fori_loop(0, 3, d_res_part, 0)

    for j in range(8):
        db_pack[j % 2, 0:ROWS, 128 * (j // 2) : 128 * (j // 2) + 128] = jnp.concatenate(
            [jnp.zeros((ROWS, 32), LOW), d_branch[:, 96 * j : 96 * j + 96]], axis=1
        )

    def share_pack(buffer, index):
        return buffer.at[1 - core, pl.ds(0, ROWS)], buffer.at[1 - core, pl.ds(256, ROWS)], index, mate

    send(*share_pack(db_pack, S_DBK))

    def add_in(grads, index, landing):
        grads[index] = (grads[index].astype(FULL) + landing[...].astype(FULL)).astype(LOW)

    def run_two(name):
        grads, landing, _, _, _, _ = groups[name]
        for route in range(2):
            got(*step_one(name, route, 0))
            for slot in range(4):
                place = places[slot]
                add_in(grads, (second_block[route], route, place), landing.at[route, 0, place])
                send(*step_two(name, route, slot))

    def run_two_own(name):
        grads, landing, _, _, _, _ = groups[name]
        for route in range(2):
            got(*step_one(name, route, 1))

            def add(n, carry):
                add_in(grads, (mine, route, n), landing.at[route, 1, n])
                return carry

            lax.fori_loop(0, 4, add, 0)

    def f2_aside():
        got_all("aside")

        def add(block, carry):
            for route in range(2):
                add_in(gf2, (depth, block, route), rzf2.at[block, route])
            return carry

        lax.fori_loop(0, 4, add, 0)
        f2_begin(2)

    def f2_run_two(*which):
        for k in which:
            for route in range(2):
                got(*f2_one(route, 0, k))
                add_in(gf2, (kept[k], second_block[route], route), r1f2.at[route, 0, k])
                send(*f2_two(route, k))
        for k in which:
            for route in range(2):
                got(*f2_one(route, 1, k))
                add_in(gf2, (kept[k], mine, route), r1f2.at[route, 1, k])

    def f2_run_three(*which):
        for k in which:
            for route in range(2):
                got(*f2_two(route, k))
                add_in(gf2, (kept[k], mine, route), r2f2.at[route, k])
                if k == 0:
                    send(*f2_three(route))

    def f2_run_four():
        for route in range(2):
            got(*f2_three(route))
            add_in(gf2, (kept[1], mine, route), r3f2.at[route])
            send(*f2_four(route))

    def f2_finish():
        for route in range(2):
            got(*f2_four(route))
            out_f2[48 * route : 48 * route + 48, :] = gf2[depth, mine, route].astype(FULL) + r4f2[route].astype(FULL)

    def run_three(name):
        grads, _, landing, _, _, _ = groups[name]
        for slot in range(4):
            for route in range(2):
                got(*step_two(name, route, slot))
                add_in(grads, (mine, route, places[slot]), landing.at[route, places[slot]])
                if slot < 2:
                    send(*step_three(name, route, slot))

    def run_four(name, slots=(0, 1)):
        grads, _, _, landing, _, _ = groups[name]
        for slot in slots:
            for route in range(2):
                got(*step_three(name, route, slot))
                add_in(grads, (mine, route, places[2 + slot]), landing.at[route, slot])
                if slot == 0:
                    send(*step_four(name, route))

    def finish(name):
        grads, _, _, _, landing, _ = groups[name]
        for route in range(2):
            got(*step_four(name, route))
            total = grads[mine, route, depth].astype(FULL) + landing[route].astype(FULL)
            if name == "q":
                out_qkv[96 * route : 96 * route + 96, :] = total[:, 0:288]
                out_proj[96 * route : 96 * route + 96, :] = total[:, 288:384]
            else:
                out_f1[96 * route : 96 * route + 96, :] = total

    def attend_back(t, carry):
        at = lanes(t, 128)
        q = query[:, at]
        k = key[:, at]
        v = value[:, at]
        d_out = d_att[:, at].astype(FULL) * row_scale[:, at]
        common = (d_out * att[:, at].astype(FULL)).astype(LOW)
        d_out = d_out.astype(LOW)
        rest = jnp.zeros((KEYS - ROWS, 128), LOW)
        q_t = jnp.concatenate([q, rest], axis=0).T
        d_out_t = jnp.concatenate([d_out, rest], axis=0).T
        all_scores = []
        right = jnp.concatenate([v, jnp.full((KEYS, 128), -1.0, LOW)], axis=1)
        for h in range(4):
            d_probs = dot_t(jnp.concatenate([d_out * only[h], common * only[h]], axis=1), right)
            low_probs = probs[4 * t + h, 0:ROWS]
            d_scores = (low_probs.astype(FULL) * d_probs).astype(LOW)
            all_scores.append(d_scores)
        d_query = dot(
            jnp.concatenate(all_scores, axis=1), jnp.concatenate([k * only[h] for h in range(4)], axis=0)
        )
        four = pl.ds(4 * t, 4)
        d_value = dot(
            jnp.concatenate([d_out_t * only_row[h] for h in range(4)], axis=1),
            probs[four].reshape(4 * KEYS, KEYS),
        )
        for h in range(4):
            probs[4 * t + h, 0:ROWS] = all_scores[h]
        d_key = dot(
            jnp.concatenate([q_t * only_row[h] for h in range(4)], axis=1),
            probs[four].reshape(4 * KEYS, KEYS),
        )
        d_query = (d_query * scale).astype(LOW)
        d_key = (d_key * scale).astype(LOW).T[0:ROWS]
        d_value = d_value.astype(LOW).T[0:ROWS]
        d_proj[:, at] = d_query
        d_proj[:, lanes(6 + t, 128)] = d_key
        d_proj[:, lanes(12 + t, 128)] = d_value
        sums[2:3, at] = sum_rows(d_query.astype(FULL))
        sums[3:4, at] = sum_rows(d_value.astype(FULL))
        return carry

    run_two("f1")
    lax.fori_loop(0, 6, attend_back, 0)

    for j in range(8):
        dy_pack[j % 2, 0:ROWS, 384 * (j // 2) : 384 * (j // 2) + 384] = jnp.concatenate(
            [d_proj[:, 288 * j : 288 * j + 288], jnp.zeros((ROWS, 96), LOW)], axis=1
        )
    send(*share_pack(dy_pack, S_DYK))

    def d_win_part(n, carry):
        at = lanes(n, 256)
        d_win[:, at] = dot_t(d_proj[...], wq[at, :]).astype(LOW)
        return carry

    lax.fori_loop(0, 3, d_win_part, 0)
    unit, spread_one = normed(x_own[...])
    d_normed = d_win[...].astype(FULL)
    sums[0:1, :] = sum_rows(d_normed * unit)
    sums[6:7, :] = sum_rows(d_normed)
    d_win[...] = (d_mid[...] + normed_back(d_normed, gains[0:1, :], unit, spread_one)).astype(LOW)
    swap(d_win, d_own, S_GRAD)

    got(*share(xw_t, S_XWT))
    got(*share(att_t, S_AOT))
    got(*share_pack(db_pack, S_DBK))
    got(*share_pack(dy_pack, S_DYK))

    def qp_block(block):
        total = dot(xw_t[...], dy_pack[core, :, lanes(block, 384)])
        more = dot(att_t[...], db_pack[core, :, lanes(block, 128)])
        for n in range(4):
            for half in range(2):
                row = 192 * n + 96 * half
                cut = slice(row, row + 96)
                gq[block, half, n, :, 0:256] = total[cut, 0:256].astype(LOW)
                gq[block, half, n, :, 256:384] = (total[cut, 256:384] + more[cut]).astype(LOW)

    for block in range(4):
        qp_block(block)

    begin("q", 0)
    f2_run_two(0, 1)
    def mlp_branch(n, carry):
        at = lanes(n, 256)
        branch = dot(act[0:ROWS, :], w2[:, at]) + biases[3:4, at]
        result_low[:, at] = (middle[:, at] + branch).astype(LOW)
        return carry + jnp.sum(branch * branch, axis=-1, keepdims=True)

    branch_square = lax.fori_loop(0, 3, mlp_branch, jnp.zeros((ROWS, 1), FULL))
    stat_mlp = sum_rows(valid_col[...] * branch_square)
    swap(result_low, result_own, S_RES)
    lane = lax.broadcasted_iota(jnp.int32, (1, 128), 1)
    stat_row = jnp.zeros((1, 128), FULL)
    for k, total in enumerate((stat_total, stat_input, stat_attn, stat_mlp)):
        stat_row = jnp.where(lane == k, total, stat_row)
    sums[12:13, 0:128] = stat_row

    def spread_rel(head, carry):
        rows = dot(gather_t[...], probs[head, 0:ROWS]).astype(LOW)
        rel_grads[pl.ds(pl.multiple_of(64 * head, 64), 64), :] = dot(rows, offsets_t[...])
        return carry

    lax.fori_loop(0, 24, spread_rel, 0, unroll=4)

    def gather_rel(i, carry):
        start = 13 * (i // 7) + i % 7
        rows = rel_grads[pl.ds(i, 24, stride=64), :]
        return carry + pltpu.roll(jnp.concatenate([rows, jnp.zeros((24, 128), FULL)], axis=1), start, 1)

    rel_sum = lax.fori_loop(0, 49, gather_rel, jnp.zeros((24, 256), FULL), unroll=7)
    for k in range(3):
        sums[16:24, 256 * k : 256 * k + 256] = rel_sum[8 * k : 8 * k + 8, :]

    send(sums, got_core, S_AR, mate)
    run_two_own("f1")
    got(sums, got_core, S_AR, mate)
    sums_one[...] = sums[:, lanes(core, 384)] + got_core[:, lanes(core, 384)]
    for k in (1, 2, 3):
        send(sums_one, got_wide.at[k - 1], S_AR + k, beside[k])
    begin("q", 1)
    run_three("f1")
    run_two("q")
    f2_aside()
    swapped(d_win, d_own, S_GRAD)
    in_order(d_own[...], out_tokens)
    store(1, out_tokens, to_tokens)
    f2_run_three(0, 1)
    run_four("f1")
    for k in (1, 2, 3):
        got(sums_one, got_wide.at[k - 1], S_AR + k, beside[k])
    sums_two[...] = (sums_one[...] + got_wide[0]) + (got_wide[1] + got_wide[2])
    send(sums_two, got_narrow.at[0], S_AR + 4, along[1])
    f2_run_four()
    got(sums_two, got_narrow.at[0], S_AR + 4, along[1])
    sums_three[...] = sums_two[...] + got_narrow[0]
    send(sums_three, got_narrow.at[1], S_AR + 5, along[2])
    swapped(result_low, result_own, S_RES)
    in_order(result_own[...], out_result)
    store(0, out_result, to_result)
    run_two_own("q")
    run_three("q")
    finish("f1")
    store(2, out_f1, to_f1)
    run_four("q", (0,))
    f2_run_two(2)
    run_four("q", (1,))
    got(sums_three, got_narrow.at[1], S_AR + 5, along[2])
    sums_all[core] = sums_three[...] + got_narrow[1]
    send(sums_all.at[core], sums_all.at[core], S_AR + 6, mate)
    f2_run_three(2)
    f2_finish()
    store(3, out_f2, to_f2)
    got(sums_all.at[core], sums_all.at[core], S_AR + 6, mate)
    small = jnp.concatenate([sums_all[0], sums_all[1]], axis=1)
    out_gains[...] = small[0:2]
    out_biases[...] = small[2:8]
    for k in range(4):
        out_fc1_bias[:, 768 * k : 768 * k + 768] = small[8 + k : 9 + k]
    for k in range(3):
        out_rel[8 * k : 8 * k + 8, :] = small[16:24, 256 * k : 256 * k + 169]
    out_stats[...] = jnp.sqrt(small[12:13, 1:4] / (model * small[12:13, 0:1]))
    for k, (src, dst) in enumerate(
        (
            (out_gains, to_gains),
            (out_biases, to_biases),
            (out_fc1_bias, to_fc1_bias),
            (out_rel, to_rel),
            (out_stats, to_stats),
        )
    ):
        store(4 + k, src, dst)
    finish("q")
    store(9, out_qkv, to_qkv)
    store(10, out_proj, to_proj)

    leave()


def fused_on_device(
    tokens, cotangent, crops, labels, norm_gains, biases, rel_table, w_qkv, w_proj, w_fc1, fc1_bias, w_fc2
):
    images, _, patches, model = tokens.shape
    hidden = w_fc1.shape[1]
    heads = rel_table.shape[1]
    vmem = pl.BlockSpec(memory_space=pltpu.VMEM)
    hbm = pl.BlockSpec(memory_space=pl.ANY)

    def low(*shape):
        return pltpu.VMEM(shape, LOW)

    def full(*shape):
        return pltpu.VMEM(shape, FULL)

    one_low = low(ROWS, model)
    one_t = low(model, ROWS)
    scratch = dict(
        wq=low(*w_qkv.shape),
        wp=low(*w_proj.shape),
        w1=low(*w_fc1.shape),
        w2=low(*w_fc2.shape),
        stack=full(256, model),
        result_low=one_low,
        x_own=full(ROWS, model),
        g_low=one_low,
        g_t=low(4, 2, 96, 256),
        g_both=low(4, 96, 512),
        tok_own=one_low,
        tok_win=one_low,
        g_own=one_low,
        result_own=one_low,
        xw=one_low,
        xw_t=low(model, 512),
        query=one_low,
        key=low(KEYS, model),
        value=low(KEYS, model),
        key_bias=low(heads, KEYS, 128),
        row_scale=full(ROWS, model),
        probs=low(heads, KEYS, KEYS),
        att=one_low,
        att_t=low(model, 512),
        middle=full(ROWS, model),
        h2=one_low,
        h2_t=low(model, 512),
        act=low(512, hidden),
        dh=low(512, hidden),
        gf1=low(4, 2, 4, 96, 384),
        gf2=low(4, 4, 2, 48, 768),
        rzf2=low(4, 2, 48, 768),
        gq=low(4, 2, 4, 96, 384),
        r1f1=low(2, 2, 4, 96, 384),
        r1f2=low(2, 2, 3, 48, 768),
        r1q=low(2, 2, 4, 96, 384),
        r2f1=low(2, 4, 96, 384),
        r2f2=low(2, 3, 48, 768),
        r3f2=low(2, 48, 768),
        r2q=low(2, 4, 96, 384),
        r3f1=low(2, 2, 96, 384),
        r3q=low(2, 2, 96, 384),
        r4f1=low(2, 96, 384),
        r4f2=low(2, 48, 768),
        r4q=low(2, 96, 384),
        d_mid=full(ROWS, model),
        d_branch=one_low,
        db_pack=low(2, 512, 512),
        d_att=one_low,
        d_proj=low(ROWS, 3 * model),
        dy_pack=low(2, 512, 1536),
        d_win=one_low,
        d_own=one_low,
        rel_rows=full(64 * 24, 128),
        rel_grads=full(64 * 24, 128),
        mask_add=full(ROWS, KEYS),
        valid_col=full(ROWS, 1),
        sums=full(24, 768),
        sums_one=full(24, 384),
        sums_two=full(24, 384),
        sums_three=full(24, 384),
        sums_all=full(2, 24, 384),
        got_core=full(24, 768),
        got_wide=full(3, 24, 384),
        got_narrow=full(2, 24, 384),
        local_sem=pltpu.SemaphoreType.DMA((32,)),
        send_sem=pltpu.SemaphoreType.DMA((S_COUNT,)),
        recv_sem=pltpu.SemaphoreType.DMA((S_COUNT,)),
    )
    shapes = (
        ((patches, images, model), LOW),
        ((patches, images, model), LOW),
        ((192, 288), FULL),
        ((192, 96), FULL),
        ((192, 384), FULL),
        ((96, 768), FULL),
        ((2, model), FULL),
        ((6, model), FULL),
        ((1, hidden), FULL),
        ((heads, 169), FULL),
        ((1, 3), FULL),
    )
    inputs = (
        ((patches, images, model), LOW),
        ((patches, images, model), LOW),
        ((2, images), jnp.int32),
        ((images, patches), jnp.int32),
        ((2, model), FULL),
        ((6, model), FULL),
        ((heads, 169), FULL),
        ((1, hidden), FULL),
        ((TABLE_ROWS, 256), LOW),
        ((ROWS, 8), jnp.int32),
    )
    outs = pl.pallas_call(
        block_kernel,
        out_shape=tuple(jax.ShapeDtypeStruct(*shape) for shape in shapes),
        in_specs=[hbm] * 14,
        out_specs=[hbm] * OUTPUTS,
        scratch_shapes=[pltpu.VMEM(*shape) for shape in inputs + shapes] + list(scratch.values()),
        compiler_params=pltpu.CompilerParams(
            collective_id=0, has_side_effects=True, vmem_limit_bytes=VMEM_LIMIT
        ),
    )(
        tokens[:, 0].transpose(1, 0, 2),
        cotangent[:, 0].transpose(1, 0, 2),
        crops.T,
        labels[:, 0],
        norm_gains,
        biases,
        rel_table.T,
        w_qkv,
        w_proj,
        w_fc1,
        fc1_bias.reshape(1, hidden),
        w_fc2,
        *[jnp.asarray(table) for table in place_tables()],
    )
    outs = pl.pallas_call(
        hand_over,
        out_shape=tuple(jax.ShapeDtypeStruct(*shape) for shape in shapes),
        in_specs=[hbm] * OUTPUTS,
        out_specs=[hbm] * OUTPUTS,
        scratch_shapes=[pltpu.VMEM(*shape) for shape in shapes]
        + [pltpu.SemaphoreType.DMA((2, OUTPUTS))],
    )(*outs)
    return (
        outs[0].transpose(1, 0, 2)[:, None],
        outs[1].transpose(1, 0, 2)[:, None],
        outs[2],
        outs[3],
        outs[4],
        outs[5].T,
        outs[6],
        outs[7],
        outs[8].reshape(hidden),
        outs[9].T,
        outs[10].reshape(3),
    )


def hand_over(*refs):
    sems = refs[-1]
    held = refs[2 * OUTPUTS : 3 * OUTPUTS]
    loads = [pltpu.make_async_copy(refs[k], held[k], sems.at[0, k]) for k in range(OUTPUTS)]
    stores = [pltpu.make_async_copy(held[k], refs[OUTPUTS + k], sems.at[1, k]) for k in range(OUTPUTS)]
    for load in loads:
        load.start()
    for load, store in zip(loads, stores):
        load.wait()
        store.start()
    for store in stores:
        store.wait()


VMEM_LIMIT = 62 * 1024 * 1024


def fused(mesh):
    each = P("wide", "narrow", None, None)
    cut = P("narrow", "wide")
    return jax.shard_map(
        fused_on_device,
        mesh=mesh,
        in_specs=(each, each, P("wide", None), P("wide", "narrow", None)) + (P(),) * 8,
        out_specs=(each, each) + (cut,) * 4 + (P(),) * 5,
        check_vma=False,
    )


def solution(mesh):
    if mesh.shape["wide"] == 8 and mesh.shape["narrow"] == 4:
        return fused(mesh)
    return plain(mesh)
```

```python
from functools import partial

import jax
import jax.numpy as jnp
import numpy as np
from jax import lax
from jax.experimental import pallas as pl
from jax.experimental.pallas import tpu as pltpu
from jax.sharding import PartitionSpec as P


def from_partner(shard, axis, stride):
    return lax.ppermute(shard, axis, [(i, i ^ 1 << stride) for i in range(lax.axis_size(axis))])


def layer_norm(values, gain, shift):
    centre = jnp.mean(values, axis=-1, keepdims=True)
    centred = values - centre
    spread = jnp.mean(centred * centred, axis=-1, keepdims=True)
    return centred * lax.rsqrt(spread + 1e-05) * gain + shift


def into_window(field, swap_rows, swap_cols):
    tall = jnp.concatenate([field[:, 3:], swap_rows(field[:, :3])], axis=1)
    return jnp.concatenate([tall[:, :, 3:], swap_cols(tall[:, :, :3])], axis=2)


def out_of_window(field, swap_rows, swap_cols):
    broad = jnp.concatenate([swap_cols(field[:, :, 4:]), field[:, :, :4]], axis=2)
    return jnp.concatenate([swap_rows(broad[:, 4:]), broad[:, :4]], axis=1)


def relative_index():
    positions = jnp.arange(49, dtype=jnp.int32)
    inner_rows = positions // 7
    inner_cols = positions % 7
    return (
        (inner_rows[:, None] - inner_rows[None, :] + 6) * 13
        + inner_cols[:, None]
        - inner_cols[None, :]
        + 6
    )


def column_sum(values):
    return jnp.sum(values, axis=0, dtype=jnp.float32)


def on_device(
    tokens,
    cotangent,
    crops,
    labels,
    norm_gains,
    biases,
    rel_table,
    w_qkv,
    w_proj,
    w_fc1,
    fc1_bias,
    w_fc2,
):
    images = tokens.shape[0]
    model_width = tokens.shape[-1]
    head_count = rel_table.shape[1]
    head_size = model_width // head_count
    rows_all = images * 49
    score_scale = head_size ** (-0.5)
    where_narrow = lax.axis_index("narrow")
    row_half = where_narrow // 2
    col_half = where_narrow % 2
    positions = jnp.arange(49, dtype=jnp.int32)
    own_row = 7 * row_half + positions // 7
    own_col = 7 * col_half + positions % 7
    shift_row = (own_row + 3) % 14
    shift_col = (own_col + 3) % 14
    valid_own = (own_row[None] < crops[:, 0:1]) & (own_col[None] < crops[:, 1:2])
    valid_shift = (shift_row[None] < crops[:, 0:1]) & (shift_col[None] < crops[:, 1:2])
    label_rows = labels[:, 0]
    allowed = (label_rows[:, :, None] == label_rows[:, None, :]) & valid_shift[
        :, None, :
    ] | jnp.eye(49, dtype=bool)[None]
    allowed_heads = allowed[:, None]
    inputs = tokens[:, 0].astype(jnp.float32)
    normed, ln1_back = jax.vjp(layer_norm, inputs, norm_gains[0], biases[4])
    normed_low = normed.astype(jnp.bfloat16).reshape(images, 7, 7, model_width)
    windows = into_window(
        normed_low,
        lambda strip: from_partner(strip, "narrow", 1),
        lambda strip: from_partner(strip, "narrow", 0),
    ).reshape(rows_all, model_width)
    projected = jnp.dot(windows, w_qkv, preferred_element_type=jnp.float32)
    head_shape = (images, 49, head_count, head_size)
    query_rows = (projected[:, :model_width] + biases[0]).astype(jnp.bfloat16).reshape(head_shape)
    key_rows = projected[:, model_width : 2 * model_width].astype(jnp.bfloat16).reshape(head_shape)
    value_rows = (
        (projected[:, 2 * model_width :] + biases[1]).astype(jnp.bfloat16).reshape(head_shape)
    )
    one_hot = (
        (relative_index()[:, :, None] == jnp.arange(169, dtype=jnp.int32))
        .reshape(2401, 169)
        .astype(jnp.float32)
    )
    bias_table = (
        jnp.dot(one_hot, rel_table, precision=lax.Precision.HIGHEST)
        .reshape(49, 49, head_count)
        .transpose(2, 0, 1)
    )

    def masked_scores():
        raw = jnp.einsum(
            "nphe,nqhe->nhpq", query_rows, key_rows, preferred_element_type=jnp.float32
        )
        return jnp.where(allowed_heads, raw * score_scale + bias_table[None], -1000000000.0)

    masked = masked_scores()
    row_top = jnp.max(masked, axis=-1, keepdims=True)
    log_total = row_top + jnp.log(jnp.sum(jnp.exp(masked - row_top), axis=-1, keepdims=True))
    attn_probs = jnp.exp(masked - log_total)
    probs_low = attn_probs.astype(jnp.bfloat16)
    attended = jnp.einsum(
        "nhpq,nqhe->nphe", probs_low, value_rows, preferred_element_type=jnp.float32
    ).astype(jnp.bfloat16)
    restored = out_of_window(
        attended.reshape(images, 7, 7, model_width),
        lambda strip: from_partner(strip, "narrow", 1),
        lambda strip: from_partner(strip, "narrow", 0),
    ).reshape(rows_all, model_width)
    branch_attn = jnp.dot(restored, w_proj, preferred_element_type=jnp.float32) + biases[2]
    middle = inputs.reshape(rows_all, model_width) + branch_attn
    normed_two, ln2_back = jax.vjp(layer_norm, middle, norm_gains[1], biases[5])
    normed_two_low = normed_two.astype(jnp.bfloat16)
    hidden = jnp.dot(normed_two_low, w_fc1, preferred_element_type=jnp.float32) + fc1_bias
    activated, gelu_back = jax.vjp(partial(jax.nn.gelu, approximate=False), hidden)
    activated_low = activated.astype(jnp.bfloat16)
    branch_mlp = jnp.dot(activated_low, w_fc2, preferred_element_type=jnp.float32) + biases[3]
    result = (middle + branch_mlp).astype(jnp.bfloat16).reshape(images, 1, 49, model_width)
    cot_rows = cotangent.reshape(rows_all, model_width)
    grad_fc2 = jnp.dot(activated_low.T, cot_rows, preferred_element_type=jnp.float32)
    d_activated = jnp.dot(cot_rows, w_fc2.T, preferred_element_type=jnp.float32)
    (d_hidden,) = gelu_back(d_activated)
    d_hidden_low = d_hidden.astype(jnp.bfloat16)
    grad_fc1 = jnp.dot(normed_two_low.T, d_hidden_low, preferred_element_type=jnp.float32)
    grad_fc1_bias = column_sum(d_hidden_low)
    d_normed_two = jnp.dot(d_hidden_low, w_fc1.T, preferred_element_type=jnp.float32)
    d_middle_norm, d_gain_two, d_shift_two = ln2_back(d_normed_two)
    d_middle = cot_rows.astype(jnp.float32) + d_middle_norm
    d_branch = d_middle.astype(jnp.bfloat16)
    grad_proj = jnp.dot(restored.T, d_branch, preferred_element_type=jnp.float32)
    d_restored = jnp.dot(d_branch, w_proj.T, preferred_element_type=jnp.float32).astype(
        jnp.bfloat16
    )
    d_attended = into_window(
        d_restored.reshape(images, 7, 7, model_width),
        lambda strip: from_partner(strip, "narrow", 1),
        lambda strip: from_partner(strip, "narrow", 0),
    ).reshape(head_shape)
    again = jnp.exp(masked_scores() - log_total)
    d_probs = jnp.einsum(
        "nphe,nqhe->nhpq", d_attended, value_rows, preferred_element_type=jnp.float32
    )
    d_scores = (again * (d_probs - jnp.sum(again * d_probs, axis=-1, keepdims=True))).astype(
        jnp.bfloat16
    )
    d_table = jnp.sum(d_scores, axis=0, dtype=jnp.float32).reshape(head_count, 2401)
    grad_rel = jnp.dot(d_table, one_hot, precision=lax.Precision.HIGHEST).T
    d_query = (
        jnp.einsum("nhpq,nqhe->nphe", d_scores, key_rows, preferred_element_type=jnp.float32)
        * score_scale
    ).astype(jnp.bfloat16)
    d_key = (
        jnp.einsum("nhpq,nphe->nqhe", d_scores, query_rows, preferred_element_type=jnp.float32)
        * score_scale
    ).astype(jnp.bfloat16)
    d_value = jnp.einsum(
        "nhpq,nphe->nqhe", probs_low, d_attended, preferred_element_type=jnp.float32
    ).astype(jnp.bfloat16)
    d_projected = jnp.concatenate(
        [
            d_query.reshape(rows_all, model_width),
            d_key.reshape(rows_all, model_width),
            d_value.reshape(rows_all, model_width),
        ],
        axis=1,
    )
    grad_qkv = jnp.dot(windows.T, d_projected, preferred_element_type=jnp.float32)
    d_windows = jnp.dot(d_projected, w_qkv.T, preferred_element_type=jnp.float32).astype(
        jnp.bfloat16
    )
    d_normed = out_of_window(
        d_windows.reshape(images, 7, 7, model_width),
        lambda strip: from_partner(strip, "narrow", 1),
        lambda strip: from_partner(strip, "narrow", 0),
    ).reshape(images, 49, model_width)
    d_inputs_norm, d_gain_one, d_shift_one = ln1_back(d_normed.astype(jnp.float32))
    grad_tokens = (
        (d_middle.reshape(images, 49, model_width) + d_inputs_norm)
        .astype(jnp.bfloat16)
        .reshape(images, 1, 49, model_width)
    )
    grad_biases = jnp.stack(
        [
            column_sum(d_query.reshape(rows_all, model_width)),
            column_sum(d_value.reshape(rows_all, model_width)),
            column_sum(d_branch),
            column_sum(cot_rows),
            d_shift_one,
            d_shift_two,
        ]
    )
    grad_gains = jnp.stack([d_gain_one, d_gain_two])
    valid_weight = valid_own.astype(jnp.float32).reshape(rows_all)
    flat_inputs = inputs.reshape(rows_all, model_width)
    stat_sums = jnp.stack(
        [
            jnp.sum(valid_weight),
            jnp.sum(valid_weight * jnp.sum(flat_inputs * flat_inputs, axis=-1)),
            jnp.sum(valid_weight * jnp.sum(branch_attn * branch_attn, axis=-1)),
            jnp.sum(valid_weight * jnp.sum(branch_mlp * branch_mlp, axis=-1)),
        ]
    )
    grad_biases, grad_gains, grad_fc1_bias, grad_rel, stat_sums = lax.psum(
        (grad_biases, grad_gains, grad_fc1_bias, grad_rel, stat_sums), ("wide", "narrow")
    )
    stats = jnp.sqrt(stat_sums[1:] / (model_width * stat_sums[0]))
    matrices = (grad_qkv, grad_proj, grad_fc1, grad_fc2)
    partial_sums = (
        lax.psum_scatter(matrices[0], "wide", scatter_dimension=1, tiled=True),
        lax.psum_scatter(matrices[1], "wide", scatter_dimension=1, tiled=True),
        lax.psum_scatter(matrices[2], "wide", scatter_dimension=1, tiled=True),
        lax.psum_scatter(matrices[3], "wide", scatter_dimension=1, tiled=True),
    )
    reduced = (
        lax.psum_scatter(
            partial_sums[0].astype(jnp.bfloat16), "narrow", scatter_dimension=0, tiled=True
        ).astype(jnp.float32),
        lax.psum_scatter(
            partial_sums[1].astype(jnp.bfloat16), "narrow", scatter_dimension=0, tiled=True
        ).astype(jnp.float32),
        lax.psum_scatter(
            partial_sums[2].astype(jnp.bfloat16), "narrow", scatter_dimension=0, tiled=True
        ).astype(jnp.float32),
        lax.psum_scatter(
            partial_sums[3].astype(jnp.bfloat16), "narrow", scatter_dimension=0, tiled=True
        ).astype(jnp.float32),
    )
    grad_qkv, grad_proj, grad_fc1, grad_fc2 = reduced
    return (
        result,
        grad_tokens,
        grad_qkv,
        grad_proj,
        grad_fc1,
        grad_fc2,
        grad_gains,
        grad_biases,
        grad_fc1_bias,
        grad_rel,
        stats,
    )


def plain(mesh):
    return jax.shard_map(
        on_device,
        mesh=mesh,
        in_specs=(
            P("wide", "narrow", None, None),
            P("wide", "narrow", None, None),
            P("wide", None),
            P("wide", "narrow", None),
            P(),
            P(),
            P(),
            P(),
            P(),
            P(),
            P(),
            P(),
        ),
        out_specs=(
            P("wide", "narrow", None, None),
            P("wide", "narrow", None, None),
            P("narrow", "wide"),
            P("narrow", "wide"),
            P("narrow", "wide"),
            P("narrow", "wide"),
            P(),
            P(),
            P(),
            P(),
            P(),
        ),
        check_vma=False,
    )


ROWS = 208
KEYS = 256
T_OWN, T_BACK, T_PICK, T_SPREAD, T_OFFSETS, T_GATHER, T_REPEAT = 0, 208, 464, 720, 928, 1184, 1248
TABLE_ROWS = 1504
MESH = pl.DeviceIdType.MESH
LOW = jnp.bfloat16
FULL = jnp.float32


def place_tables():
    places = []
    for tall, broad in ((0, 0), (1, 0), (0, 1), (1, 1)):
        for image in range(4):
            for i in range(4, 7) if tall else range(4):
                for j in range(4, 7) if broad else range(4):
                    places.append((image, i, j, i - 4 if tall else i + 3, j - 4 if broad else j + 3))
    own = np.zeros((ROWS, 256), np.float32)
    spread = np.zeros((ROWS, 128), np.float32)
    pick = np.zeros((256, 128), np.float32)
    repeat = np.zeros((KEYS, 64), np.float32)
    for spot in range(49):
        for lane in (spot, 64 + spot):
            pick[13 * (spot // 7) + spot % 7, lane] = 1
            pick[128 + 13 * (spot // 7) + spot % 7, lane] = 1
    gather = np.zeros((64, ROWS), np.float32)
    offsets = np.zeros((KEYS, 128), np.float32)
    info = np.zeros((ROWS, 8), np.int32)
    info[:, 3] = -1
    for row in range(ROWS):
        if row >= len(places):
            info[row, 0] = 4 + row - len(places)
            continue
        image, i, j, a, b = places[row]
        own[row, 4 * (7 * a + b) + image] = 1
        spread[row, 7 * i + j] = 1
        spread[row, 64 + 7 * i + j] = 1
        shift = (6 - i) * 13 + 6 - j
        repeat[row, 7 * i + j] = 1
        gather[7 * i + j, row] = 1
        offsets[row, shift] = 1
        info[row, :6] = (image, i, j, 7 * i + j, a, b)
    table = np.zeros((TABLE_ROWS, 256), np.float32)
    table[T_OWN : T_OWN + ROWS] = own
    table[T_BACK : T_BACK + 256, :ROWS] = own.T
    table[T_PICK : T_PICK + 256, :128] = pick
    table[T_REPEAT : T_REPEAT + KEYS, :64] = repeat
    table[T_SPREAD : T_SPREAD + ROWS, :128] = spread
    table[T_OFFSETS : T_OFFSETS + KEYS, :128] = offsets
    table[T_GATHER : T_GATHER + 64, :ROWS] = gather
    return table.astype(jnp.bfloat16), info


def dot(left, right):
    return jnp.dot(left, right, preferred_element_type=FULL)


def dot_t(left, right):
    return lax.dot_general(left, right, (((1,), (1,)), ((), ())), preferred_element_type=FULL)


def lanes(index, width):
    return pl.ds(pl.multiple_of(index * width, width), width)


def normed(values):
    centred = values - jnp.mean(values, axis=-1, keepdims=True)
    scale = lax.rsqrt(jnp.mean(centred * centred, axis=-1, keepdims=True) + 1e-05)
    return centred * scale, scale


def normed_back(grad, gain, unit, scale):
    inner = grad * gain
    along = jnp.mean(inner, axis=-1, keepdims=True)
    across = jnp.mean(inner * unit, axis=-1, keepdims=True)
    return scale * (inner - along - unit * across)


def sum_rows(values):
    return jnp.sum(values, axis=0, keepdims=True)


GROUPS = ((64, 48), (112, 48), (160, 48))

S_TOK = 0
S_COT = 3
S_RES = 6
S_GRAD = 9
S_GT = 12
S_XWT = 13
S_AOT = 14
S_H2T = 15
S_ACT = 16
S_DH = 20
S_DBK = 24
S_DYK = 25
S_AR = 26
S_F1 = 33
S_F2 = 51
S_Q = 75
S_COUNT = 93
OUTPUTS = 11
ROUTES = ((0, 0), (1, 0), (0, 1), (1, 1))


def block_kernel(
    tokens_hbm,
    cotangent_hbm,
    crops_hbm,
    labels_hbm,
    gains_hbm,
    biases_hbm,
    rel_hbm,
    wq_hbm,
    wp_hbm,
    w1_hbm,
    fc1_bias_hbm,
    w2_hbm,
    table_hbm,
    info_hbm,
    to_result,
    to_tokens,
    to_qkv,
    to_proj,
    to_f1,
    to_f2,
    to_gains,
    to_biases,
    to_fc1_bias,
    to_rel,
    to_stats,
    tokens,
    cotangent,
    crops,
    labels,
    gains,
    biases,
    rel_table,
    fc1_bias,
    table,
    info,
    out_result,
    out_tokens,
    out_qkv,
    out_proj,
    out_f1,
    out_f2,
    out_gains,
    out_biases,
    out_fc1_bias,
    out_rel,
    out_stats,
    wq,
    wp,
    w1,
    w2,
    stack,
    result_low,
    x_own,
    g_low,
    g_t,
    g_both,
    tok_own,
    tok_win,
    g_own,
    result_own,
    xw,
    xw_t,
    query,
    key,
    value,
    key_bias,
    row_scale,
    probs,
    att,
    att_t,
    middle,
    h2,
    h2_t,
    act,
    dh,
    gf1,
    gf2,
    rzf2,
    gq,
    r1f1,
    r1f2,
    r1q,
    r2f1,
    r2f2,
    r3f2,
    r2q,
    r3f1,
    r3q,
    r4f1,
    r4f2,
    r4q,
    d_mid,
    d_branch,
    db_pack,
    d_att,
    d_proj,
    dy_pack,
    d_win,
    d_own,
    rel_rows,
    rel_grads,
    mask_add,
    valid_col,
    sums,
    sums_one,
    sums_two,
    sums_three,
    sums_all,
    got_core,
    got_wide,
    got_narrow,
    local_sem,
    send_sem,
    recv_sem,
):
    model = x_own.shape[1]
    width = lax.axis_index("wide")
    depth = lax.axis_index("narrow")
    core = width % 2
    mine = width // 2
    mate = {"wide": width ^ 1, "narrow": depth}
    beside = [None] + [{"wide": width ^ (2 * k), "narrow": depth} for k in (1, 2, 3)]
    along = [None] + [{"wide": width, "narrow": depth ^ k} for k in (1, 2, 3)]
    partners = [mate] + beside[1:] + along[1:]
    quadrant = (along[2], along[1], along[3])

    started = {}

    def copy_of(src, dst, index, device):
        return pltpu.make_async_remote_copy(
            src_ref=src,
            dst_ref=dst,
            send_sem=send_sem.at[index],
            recv_sem=recv_sem.at[index],
            device_id=device,
            device_id_type=MESH,
        )

    def send(*args):
        copy_of(*args).start()
        started[args[2]] = [lambda n: [args], 1, False]

    def got(*args):
        copy_of(*args).wait_recv()
        started[args[2]][2] = True

    def each(copies, count, act):
        def step(n, carry):
            for args in copies(n):
                act(copy_of(*args))
            return carry

        if count == 1:
            step(0, 0)
        else:
            lax.fori_loop(0, count, step, 0)

    def got_all(name):
        copies, count, _ = started[name]
        each(copies, count, lambda copy: copy.wait_recv())
        started[name][2] = True

    def leave():
        for copies, count, arrived in started.values():
            if not arrived:
                each(copies, count, lambda copy: copy.wait_recv())
        for copies, count, _ in started.values():
            each(copies, count, lambda copy: copy.wait_send())
        for copy in stores:
            copy.wait()

    barrier = pltpu.get_barrier_semaphore()
    for partner in partners:
        pl.semaphore_signal(barrier, inc=1, device_id=partner, device_id_type=MESH)
    pairs = ((wq_hbm, wq), (wp_hbm, wp), (w1_hbm, w1), (w2_hbm, w2))
    pairs += ((tokens_hbm, tokens), (table_hbm, table), (gains_hbm, gains), (biases_hbm, biases))
    pairs += ((cotangent_hbm, cotangent), (info_hbm, info), (crops_hbm, crops), (labels_hbm, labels))
    pairs += ((rel_hbm, rel_table), (fc1_bias_hbm, fc1_bias))
    loads = [pltpu.make_async_copy(src, dst, local_sem.at[k]) for k, (src, dst) in enumerate(pairs)]
    for load in loads[4:] + loads[:4]:
        load.start()
    own_t = table.at[pl.ds(T_OWN, ROWS), :]
    back_t = table.at[pl.ds(T_BACK, 256), pl.ds(0, ROWS)]
    pick_t = table.at[pl.ds(T_PICK, 256), pl.ds(0, 128)]
    repeat_t = table.at[pl.ds(T_REPEAT, KEYS), pl.ds(0, 64)]
    spread_t = table.at[pl.ds(T_SPREAD, ROWS), pl.ds(0, 128)]
    offsets_t = table.at[pl.ds(T_OFFSETS, KEYS), pl.ds(0, 128)]
    gather_t = table.at[pl.ds(T_GATHER, 64), pl.ds(0, ROWS)]

    def store(k, src, dst):
        copy = pltpu.make_async_copy(src, dst, local_sem.at[len(pairs) + k])
        copy.start()
        stores.append(copy)

    stores = []

    def in_places(source):
        stack[192:256, :] = jnp.zeros((64, model), FULL)
        for patch in range(49):
            stack[4 * patch : 4 * patch + 4, :] = source[patch].astype(FULL)
        return dot(own_t[...], stack[...].astype(LOW))

    def in_order(values, out):
        stack[...] = dot(back_t[...], values)
        for patch in range(49):
            out[patch] = stack[4 * patch : 4 * patch + 4, :].astype(LOW)

    def swap(src, dst, base):
        dst[0:64, :] = src[0:64, :]
        for k in (2, 0, 1):
            row, count = GROUPS[k]
            rows = pl.ds(row, count)
            send(src.at[rows], dst.at[rows], base + k, quadrant[k])

    def swapped(src, dst, base):
        for k, (row, count) in enumerate(GROUPS):
            rows = pl.ds(row, count)
            got(src.at[rows], dst.at[rows], base + k, quadrant[k])

    for load in loads[4:8]:
        load.wait()
    tok_own[...] = in_places(tokens).astype(LOW)
    pl.semaphore_wait(barrier, len(partners))
    swap(tok_own, tok_win, S_TOK)

    for load in loads[8:]:
        load.wait()
    g_value = in_places(cotangent)
    g_own[...] = g_value.astype(LOW)
    for buffer in (xw_t, att_t, h2_t):
        buffer[:, 128:256] = jnp.zeros((model, 128), LOW)
    for buffer in (act, dh, dy_pack.at[0], dy_pack.at[1], db_pack.at[0], db_pack.at[1]):
        for row in (ROWS, 256 + ROWS):
            buffer[row : row + 48, :] = jnp.zeros((48, buffer.shape[1]), LOW)
    g_t[...] = jnp.zeros_like(g_t)

    sums[...] = jnp.zeros_like(sums)
    sums[5:6, :] = sum_rows(g_value)

    row_half = depth // 2
    col_half = depth % 2
    image_col = info[:, 0:1]
    i_col = info[:, 1:2]
    j_col = info[:, 2:3]
    place_col = info[:, 3:4]
    zero_col = jnp.zeros((ROWS, 1), jnp.int32)
    crop_row = zero_col
    crop_col = zero_col
    label = jnp.zeros((ROWS, 1), FULL)
    lane49 = lax.broadcasted_iota(jnp.int32, (ROWS, 49), 1)
    for image in range(4):
        is_image = image_col == image
        crop_row = jnp.where(is_image, crops[0:1, image : image + 1], crop_row)
        crop_col = jnp.where(is_image, crops[1:2, image : image + 1], crop_col)
        picked = jnp.where(
            lane49 == place_col, labels[image : image + 1, :].astype(FULL), jnp.zeros((ROWS, 49), FULL)
        )
        label = jnp.where(is_image, jnp.sum(picked, axis=1, keepdims=True), label)
    shift_row = 7 * row_half + i_col + 3
    shift_row = jnp.where(shift_row >= 14, shift_row - 14, shift_row)
    shift_col = 7 * col_half + j_col + 3
    shift_col = jnp.where(shift_col >= 14, shift_col - 14, shift_col)
    valid_key = (shift_row < crop_row) & (shift_col < crop_col)
    valid_value = jnp.where(valid_key, 1.0, 0.0).astype(FULL)
    valid_col[...] = valid_value
    code = label + 8.0 * image_col.astype(FULL)
    key_code = jnp.where(valid_key, code, -1.0)
    diagonal = lax.broadcasted_iota(jnp.int32, (ROWS, KEYS), 0) == lax.broadcasted_iota(
        jnp.int32, (ROWS, KEYS), 1
    )
    key_row = jnp.sum(jnp.where(diagonal, key_code + 2.0, 0.0), axis=0, keepdims=True) - 2.0
    mask_add[...] = jnp.where((code == key_row) | diagonal, 0.0, -1000000000.0)

    rel_wide = jnp.concatenate([rel_table[...] * 32**0.5, jnp.zeros((24, 87), FULL)], axis=1)
    rel_rows[1176:1536, :] = jnp.zeros((360, 128), FULL)

    def shifted(spot, carry):
        start = 84 - 13 * (spot // 7) - spot % 7
        rel_rows[pl.ds(pl.multiple_of(24 * spot, 8), 24), :] = pltpu.roll(rel_wide, 256 - start, 1)[:, 0:128]
        return carry

    lax.fori_loop(0, 49, shifted, 0, unroll=7)

    def picked_rows(n, carry):
        rows = pl.ds(pl.multiple_of(168 * n, 8), 168)
        values = rel_rows[rows, :]
        high = values.astype(LOW)
        below = (values - high.astype(FULL)).astype(LOW)
        rel_rows[rows, :] = dot(jnp.concatenate([high, below], axis=1), pick_t[...])
        return carry

    lax.fori_loop(0, 7, picked_rows, 0)
    is_high = lax.broadcasted_iota(jnp.int32, (64, 128), 1) < 64

    def head_bias(head, carry):
        values = rel_rows[pl.ds(head, 64, stride=24), :]
        high = values.astype(LOW).astype(FULL)
        parts = jnp.where(is_high, high, values - high).astype(LOW)
        key_bias[head] = dot(repeat_t[...], parts).astype(LOW)
        return carry

    lax.fori_loop(0, 24, head_bias, 0, unroll=4)

    key[ROWS:KEYS, :] = jnp.zeros((KEYS - ROWS, model), LOW)
    value[ROWS:KEYS, :] = jnp.zeros((KEYS - ROWS, model), LOW)
    swapped(tok_own, tok_win, S_TOK)
    swap(g_own, g_low, S_COT)
    flat = tok_win[...].astype(FULL)
    x_own[...] = flat
    unit, _ = normed(flat)
    xw[...] = (unit * gains[0:1, :] + biases[4:5, :]).astype(LOW)
    stat_total = jnp.sum(valid_value, axis=0, keepdims=True)
    stat_input = sum_rows(valid_value * jnp.sum(flat * flat, axis=-1, keepdims=True))

    loads[0].wait()

    def project(n, carry):
        at = lanes(n, 256)
        window = xw[...]
        query[:, at] = (dot(window, wq[:, at]) + biases[0:1, at]).astype(LOW)
        key[0:ROWS, at] = dot(window, wq[:, lanes(n + 3, 256)]).astype(LOW)
        value[0:ROWS, at] = (dot(window, wq[:, lanes(n + 6, 256)]) + biases[1:2, at]).astype(LOW)
        return carry

    lax.fori_loop(0, 3, project, 0, unroll=3)

    lane_head = lax.broadcasted_iota(jnp.int32, (1, 128), 1) // 32
    only = [(lane_head == h).astype(FULL).astype(LOW) for h in range(4)]
    row_head = lax.broadcasted_iota(jnp.int32, (128, 1), 0) // 32
    only_row = [(row_head == h).astype(FULL).astype(LOW) for h in range(4)]
    scale = 32 ** (-0.5)

    def attend(t, carry):
        at = lanes(t, 128)
        q = query[:, at]
        k = key[:, at]
        v = value[:, at]
        powers = []
        right = []
        for h in range(4):
            left = jnp.concatenate([q * only[h], spread_t[...]], axis=1)
            scores = dot_t(left, jnp.concatenate([k, key_bias[4 * t + h]], axis=1)) + mask_add[...]
            top = jnp.max(scores, axis=-1, keepdims=True)
            power = jnp.exp2((scores - top) * (scale * 1.4426950408889634)).astype(LOW)
            probs[4 * t + h, 0:ROWS] = power
            probs[4 * t + h, ROWS:KEYS] = jnp.zeros((KEYS - ROWS, KEYS), LOW)
            powers.append(power)
            right.append(jnp.concatenate([v * only[h], jnp.ones((KEYS, 128), LOW) * only[h]], axis=1))
        both = dot(jnp.concatenate(powers, axis=1), jnp.concatenate(right, axis=0))
        total = both[:, 0:128]
        below = 1.0 / both[:, 128:256]
        row_scale[:, at] = below
        total = (total * below).astype(LOW)
        att[:, at] = total
        return carry

    lax.fori_loop(0, 6, attend, 0)

    def share(buffer, index):
        return buffer.at[:, pl.ds(0, 256)], buffer.at[:, pl.ds(256, 256)], index, mate

    loads[1].wait()

    def attn_branch(n, carry):
        at = lanes(n, 256)
        branch = dot(att[...], wp[:, at]) + biases[2:3, at]
        middle[:, at] = x_own[:, at] + branch
        return carry + jnp.sum(branch * branch, axis=-1, keepdims=True)

    branch_square = lax.fori_loop(0, 3, attn_branch, jnp.zeros((ROWS, 1), FULL), unroll=3)
    stat_attn = sum_rows(valid_col[...] * branch_square)

    unit, _ = normed(middle[...])
    h2[...] = (unit * gains[1:2, :] + biases[5:6, :]).astype(LOW)
    h2_t[:, 0:ROWS] = h2[...].T
    send(*share(h2_t, S_H2T))
    loads[2].wait()
    loads[3].wait()
    swapped(g_own, g_low, S_COT)

    def turn(r):
        return mine ^ jnp.where(r == 0, 3, jnp.where(r == 3, 0, r))

    def mlp_copies(r):
        at = lanes(turn(r), 768)
        return [
            (dh.at[pl.ds(0, ROWS), at], dh.at[pl.ds(256, ROWS), at], S_DH + r, mate),
            (act.at[pl.ds(0, ROWS), at], act.at[pl.ds(256, ROWS), at], S_ACT + r, mate),
        ]

    def hidden_quarter(r):
        quarter = turn(r)

        def hidden_part(n, carry):
            at = lanes(quarter * 3 + n, 256)
            hidden = dot(h2[...], w1[:, at]) + fc1_bias[:, at]
            d_act = dot_t(g_low[...], w2[at, :])
            below = 0.5 + 0.5 * lax.erf(hidden * 0.7071067811865476)
            act[0:ROWS, at] = (hidden * below).astype(LOW)
            slope = below + hidden * (0.3989422804014327 * jnp.exp(-0.5 * hidden * hidden))
            d_hidden = (slope * d_act).astype(LOW)
            dh[0:ROWS, at] = d_hidden
            sums[pl.ds(8 + quarter, 1), lanes(n, 256)] = sum_rows(d_hidden.astype(FULL))
            return carry

        lax.fori_loop(0, 3, hidden_part, 0, unroll=3)
        for args in mlp_copies(r):
            copy_of(*args).start()

    first = (beside[1], beside[2])
    second = (beside[2], beside[1])
    second_block = (mine ^ 2, mine ^ 1)
    groups = {"f1": (gf1, r1f1, r2f1, r3f1, r4f1, S_F1)}
    groups["q"] = (gq, r1q, r2q, r3q, r4q, S_Q)
    places = (depth ^ 3, depth ^ 1, depth ^ 2, depth)

    def step_one(name, route, slot):
        grads, landing, _, _, _, base = groups[name]
        block = mine ^ 3 if slot == 0 else mine ^ (1 + route)
        return grads.at[block, route], landing.at[route, slot], base + 2 * route + slot, first[route]

    def step_two(name, route, slot):
        grads, _, landing, _, _, base = groups[name]
        place = places[slot]
        return (
            grads.at[second_block[route], route, place],
            landing.at[route, place],
            base + 4 + 4 * route + slot,
            second[route],
        )

    def step_three(name, route, slot):
        grads, _, _, landing, _, base = groups[name]
        return (
            grads.at[mine, route, places[slot]],
            landing.at[route, slot],
            base + 12 + 2 * route + slot,
            along[1],
        )

    def step_four(name, route):
        grads, _, _, _, landing, base = groups[name]
        return grads.at[mine, route, depth ^ 2], landing.at[route], base + 16 + route, along[2]

    kept = (depth ^ 3, depth ^ 2, depth)

    def aside():
        return gf2.at[depth ^ 1], rzf2, S_F2, along[1]

    def f2_one(route, slot, k):
        block = mine ^ 3 if slot == 0 else mine ^ (1 + route)
        return (
            gf2.at[kept[k], block, route],
            r1f2.at[route, slot, k],
            S_F2 + 1 + 6 * slot + 3 * route + k,
            first[route],
        )

    def f2_two(route, k):
        return gf2.at[kept[k], second_block[route], route], r2f2.at[route, k], S_F2 + 13 + 3 * route + k, second[route]

    def f2_three(route):
        return gf2.at[kept[0], mine, route], r3f2.at[route], S_F2 + 19 + route, along[1]

    def f2_four(route):
        return gf2.at[kept[1], mine, route], r4f2.at[route], S_F2 + 21 + route, along[2]

    def f2_begin(*which):
        for slot in range(2):
            for k in which:
                for route in range(2):
                    send(*f2_one(route, slot, k))

    def begin(name, slot):
        for route in range(2):
            send(*step_one(name, route, slot))

    def fc1_quarter(r):
        quarter = turn(r)
        copy_of(*mlp_copies(r)[0]).wait_recv()
        at = lanes(2 * quarter + core, 384)

        total = dot(h2_t[...], dh[:, at])
        for n in range(4):
            for half in range(2):
                row = 192 * n + 96 * half
                gf1[quarter, half, n] = total[row : row + 96].astype(LOW)

        @pl.when(r == 0)
        def _():
            copy_of(*step_one("f1", 0, 0)).start()
            copy_of(*step_one("f1", 1, 0)).start()

        @pl.when(r == 1)
        def _():
            copy_of(*step_one("f1", 0, 1)).start()

        @pl.when(r == 2)
        def _():
            copy_of(*step_one("f1", 1, 1)).start()

    def fc2_quarter(r):
        quarter = turn(r)
        copy_of(*mlp_copies(r)[1]).wait_recv()
        total = dot(g_both[...].reshape(384, 512), act[:, lanes(quarter, 768)])
        for n in range(4):
            for half in range(2):
                row = 96 * n + 48 * half
                gf2[quarter, n, half] = total[row : row + 48].astype(LOW)

        @pl.when(quarter == depth ^ 1)
        def _():
            copy_of(*aside()).start()


    hidden_quarter(jnp.int32(0))
    turned = g_low[...].T
    for j in range(8):
        g_t[j // 2, j % 2, :, 0:ROWS] = turned[96 * j : 96 * j + 96]
    g_both[:, :, 0:256] = g_t[:, core]
    send(g_t.at[:, 1 - core], g_both.at[:, :, pl.ds(256, 256)], S_GT, mate)
    got(*share(h2_t, S_H2T))
    fc1_quarter(jnp.int32(0))
    got(g_t.at[:, 1 - core], g_both.at[:, :, pl.ds(256, 256)], S_GT, mate)
    fc2_quarter(jnp.int32(0))
    hidden_quarter(jnp.int32(1))

    def quarters(r, carry):
        hidden_quarter(r)
        fc1_quarter(r - 1)
        fc2_quarter(r - 1)
        return carry

    lax.fori_loop(2, 4, quarters, 0)
    fc1_quarter(jnp.int32(3))
    fc2_quarter(jnp.int32(3))
    started["mlp"] = [mlp_copies, 4, True]
    for route, slot in ROUTES:
        args = step_one("f1", route, slot)
        started[args[2]] = [lambda n, args=args: [args], 1, False]
    started["aside"] = [lambda n: [aside()], 1, False]
    f2_begin(0, 1)
    xw_t[:, 0:ROWS] = xw[...].T
    send(*share(xw_t, S_XWT))
    att_t[:, 0:ROWS] = att[...].T
    send(*share(att_t, S_AOT))

    def d_normed_part(n, carry):
        at = lanes(n, 256)
        d_mid[:, at] = dot_t(dh[0:ROWS, :], w1[at, :])
        return carry

    lax.fori_loop(0, 3, d_normed_part, 0)
    unit, spread_two = normed(middle[...])
    d_normed = d_mid[...]
    sums[1:2, :] = sum_rows(d_normed * unit)
    sums[7:8, :] = sum_rows(d_normed)
    d_middle = g_low[...].astype(FULL) + normed_back(d_normed, gains[1:2, :], unit, spread_two)
    d_mid[...] = d_middle
    d_low = d_middle.astype(LOW)
    d_branch[...] = d_low
    sums[4:5, :] = sum_rows(d_low.astype(FULL))

    def d_res_part(n, carry):
        at = lanes(n, 256)
        d_att[:, at] = dot_t(d_branch[...], wp[at, :]).astype(LOW)
        return carry

    lax.fori_loop(0, 3, d_res_part, 0)

    for j in range(8):
        db_pack[j % 2, 0:ROWS, 128 * (j // 2) : 128 * (j // 2) + 128] = jnp.concatenate(
            [jnp.zeros((ROWS, 32), LOW), d_branch[:, 96 * j : 96 * j + 96]], axis=1
        )

    def share_pack(buffer, index):
        return buffer.at[1 - core, pl.ds(0, ROWS)], buffer.at[1 - core, pl.ds(256, ROWS)], index, mate

    send(*share_pack(db_pack, S_DBK))

    def add_in(grads, index, landing):
        grads[index] = (grads[index].astype(FULL) + landing[...].astype(FULL)).astype(LOW)

    def run_two(name):
        grads, landing, _, _, _, _ = groups[name]
        for route in range(2):
            got(*step_one(name, route, 0))
            for slot in range(4):
                place = places[slot]
                add_in(grads, (second_block[route], route, place), landing.at[route, 0, place])
                send(*step_two(name, route, slot))

    def run_two_own(name):
        grads, landing, _, _, _, _ = groups[name]
        for route in range(2):
            got(*step_one(name, route, 1))

            def add(n, carry):
                add_in(grads, (mine, route, n), landing.at[route, 1, n])
                return carry

            lax.fori_loop(0, 4, add, 0)

    def f2_aside():
        got_all("aside")

        def add(block, carry):
            for route in range(2):
                add_in(gf2, (depth, block, route), rzf2.at[block, route])
            return carry

        lax.fori_loop(0, 4, add, 0)
        f2_begin(2)

    def f2_run_two(*which):
        for k in which:
            for route in range(2):
                got(*f2_one(route, 0, k))
                add_in(gf2, (kept[k], second_block[route], route), r1f2.at[route, 0, k])
                send(*f2_two(route, k))
        for k in which:
            for route in range(2):
                got(*f2_one(route, 1, k))
                add_in(gf2, (kept[k], mine, route), r1f2.at[route, 1, k])

    def f2_run_three(*which):
        for k in which:
            for route in range(2):
                got(*f2_two(route, k))
                add_in(gf2, (kept[k], mine, route), r2f2.at[route, k])
                if k == 0:
                    send(*f2_three(route))

    def f2_run_four():
        for route in range(2):
            got(*f2_three(route))
            add_in(gf2, (kept[1], mine, route), r3f2.at[route])
            send(*f2_four(route))

    def f2_finish():
        for route in range(2):
            got(*f2_four(route))
            out_f2[48 * route : 48 * route + 48, :] = gf2[depth, mine, route].astype(FULL) + r4f2[route].astype(FULL)

    def run_three(name):
        grads, _, landing, _, _, _ = groups[name]
        for slot in range(4):
            for route in range(2):
                got(*step_two(name, route, slot))
                add_in(grads, (mine, route, places[slot]), landing.at[route, places[slot]])
                if slot < 2:
                    send(*step_three(name, route, slot))

    def run_four(name, slots=(0, 1)):
        grads, _, _, landing, _, _ = groups[name]
        for slot in slots:
            for route in range(2):
                got(*step_three(name, route, slot))
                add_in(grads, (mine, route, places[2 + slot]), landing.at[route, slot])
                if slot == 0:
                    send(*step_four(name, route))

    def finish(name):
        grads, _, _, _, landing, _ = groups[name]
        for route in range(2):
            got(*step_four(name, route))
            total = grads[mine, route, depth].astype(FULL) + landing[route].astype(FULL)
            if name == "q":
                out_qkv[96 * route : 96 * route + 96, :] = total[:, 0:288]
                out_proj[96 * route : 96 * route + 96, :] = total[:, 288:384]
                rows = pl.ds(96 * route, 96)
                store(9 + 2 * route, out_qkv.at[rows], to_qkv.at[rows])
                store(10 + 2 * route, out_proj.at[rows], to_proj.at[rows])
            else:
                out_f1[96 * route : 96 * route + 96, :] = total

    def attend_back(t, carry):
        at = lanes(t, 128)
        q = query[:, at]
        k = key[:, at]
        v = value[:, at]
        d_out = d_att[:, at].astype(FULL) * row_scale[:, at]
        common = (d_out * att[:, at].astype(FULL)).astype(LOW)
        d_out = d_out.astype(LOW)
        rest = jnp.zeros((KEYS - ROWS, 128), LOW)
        q_t = jnp.concatenate([q, rest], axis=0).T
        d_out_t = jnp.concatenate([d_out, rest], axis=0).T
        all_scores = []
        right = jnp.concatenate([v, jnp.full((KEYS, 128), -1.0, LOW)], axis=1)
        for h in range(4):
            d_probs = dot_t(jnp.concatenate([d_out * only[h], common * only[h]], axis=1), right)
            low_probs = probs[4 * t + h, 0:ROWS]
            d_scores = (low_probs.astype(FULL) * d_probs).astype(LOW)
            all_scores.append(d_scores)
        d_query = dot(
            jnp.concatenate(all_scores, axis=1), jnp.concatenate([k * only[h] for h in range(4)], axis=0)
        )
        four = pl.ds(4 * t, 4)
        d_value = dot(
            jnp.concatenate([d_out_t * only_row[h] for h in range(4)], axis=1),
            probs[four].reshape(4 * KEYS, KEYS),
        )
        for h in range(4):
            probs[4 * t + h, 0:ROWS] = all_scores[h]
        d_key = dot(
            jnp.concatenate([q_t * only_row[h] for h in range(4)], axis=1),
            probs[four].reshape(4 * KEYS, KEYS),
        )
        d_query = (d_query * scale).astype(LOW)
        d_key = (d_key * scale).astype(LOW).T[0:ROWS]
        d_value = d_value.astype(LOW).T[0:ROWS]
        d_proj[:, at] = d_query
        d_proj[:, lanes(6 + t, 128)] = d_key
        d_proj[:, lanes(12 + t, 128)] = d_value
        sums[2:3, at] = sum_rows(d_query.astype(FULL))
        sums[3:4, at] = sum_rows(d_value.astype(FULL))
        return carry

    run_two("f1")
    lax.fori_loop(0, 6, attend_back, 0)

    for j in range(8):
        dy_pack[j % 2, 0:ROWS, 384 * (j // 2) : 384 * (j // 2) + 384] = jnp.concatenate(
            [d_proj[:, 288 * j : 288 * j + 288], jnp.zeros((ROWS, 96), LOW)], axis=1
        )
    send(*share_pack(dy_pack, S_DYK))

    def d_win_part(n, carry):
        at = lanes(n, 256)
        d_win[:, at] = dot_t(d_proj[...], wq[at, :]).astype(LOW)
        return carry

    lax.fori_loop(0, 3, d_win_part, 0)
    unit, spread_one = normed(x_own[...])
    d_normed = d_win[...].astype(FULL)
    sums[0:1, :] = sum_rows(d_normed * unit)
    sums[6:7, :] = sum_rows(d_normed)
    d_win[...] = (d_mid[...] + normed_back(d_normed, gains[0:1, :], unit, spread_one)).astype(LOW)
    swap(d_win, d_own, S_GRAD)

    got(*share(xw_t, S_XWT))
    got(*share(att_t, S_AOT))
    got(*share_pack(db_pack, S_DBK))
    got(*share_pack(dy_pack, S_DYK))

    def qp_block(block):
        total = dot(xw_t[...], dy_pack[core, :, lanes(block, 384)])
        more = dot(att_t[...], db_pack[core, :, lanes(block, 128)])
        for n in range(4):
            for half in range(2):
                row = 192 * n + 96 * half
                cut = slice(row, row + 96)
                gq[block, half, n, :, 0:256] = total[cut, 0:256].astype(LOW)
                gq[block, half, n, :, 256:384] = (total[cut, 256:384] + more[cut]).astype(LOW)

    for block in range(4):
        qp_block(block)

    begin("q", 0)
    f2_run_two(0, 1)
    def mlp_branch(n, carry):
        at = lanes(n, 256)
        branch = dot(act[0:ROWS, :], w2[:, at]) + biases[3:4, at]
        result_low[:, at] = (middle[:, at] + branch).astype(LOW)
        return carry + jnp.sum(branch * branch, axis=-1, keepdims=True)

    branch_square = lax.fori_loop(0, 3, mlp_branch, jnp.zeros((ROWS, 1), FULL))
    stat_mlp = sum_rows(valid_col[...] * branch_square)
    swap(result_low, result_own, S_RES)
    lane = lax.broadcasted_iota(jnp.int32, (1, 128), 1)
    stat_row = jnp.zeros((1, 128), FULL)
    for k, total in enumerate((stat_total, stat_input, stat_attn, stat_mlp)):
        stat_row = jnp.where(lane == k, total, stat_row)
    sums[12:13, 0:128] = stat_row

    def spread_rel(head, carry):
        rows = dot(gather_t[...], probs[head, 0:ROWS]).astype(LOW)
        rel_grads[pl.ds(pl.multiple_of(64 * head, 64), 64), :] = dot(rows, offsets_t[...])
        return carry

    lax.fori_loop(0, 24, spread_rel, 0, unroll=4)

    def gather_rel(i, carry):
        start = 13 * (i // 7) + i % 7
        rows = rel_grads[pl.ds(i, 24, stride=64), :]
        return carry + pltpu.roll(jnp.concatenate([rows, jnp.zeros((24, 128), FULL)], axis=1), start, 1)

    rel_sum = lax.fori_loop(0, 49, gather_rel, jnp.zeros((24, 256), FULL), unroll=7)
    for k in range(3):
        sums[16:24, 256 * k : 256 * k + 256] = rel_sum[8 * k : 8 * k + 8, :]

    send(sums, got_core, S_AR, mate)
    run_two_own("f1")
    got(sums, got_core, S_AR, mate)
    sums_one[...] = sums[:, lanes(core, 384)] + got_core[:, lanes(core, 384)]
    for k in (1, 2, 3):
        send(sums_one, got_wide.at[k - 1], S_AR + k, beside[k])
    begin("q", 1)
    run_three("f1")
    run_two("q")
    f2_aside()
    swapped(d_win, d_own, S_GRAD)
    in_order(d_own[...], out_tokens)
    store(1, out_tokens, to_tokens)
    f2_run_three(0, 1)
    run_four("f1")
    for k in (1, 2, 3):
        got(sums_one, got_wide.at[k - 1], S_AR + k, beside[k])
    sums_two[...] = (sums_one[...] + got_wide[0]) + (got_wide[1] + got_wide[2])
    send(sums_two, got_narrow.at[0], S_AR + 4, along[1])
    f2_run_four()
    got(sums_two, got_narrow.at[0], S_AR + 4, along[1])
    sums_three[...] = sums_two[...] + got_narrow[0]
    send(sums_three, got_narrow.at[1], S_AR + 5, along[2])
    swapped(result_low, result_own, S_RES)
    in_order(result_own[...], out_result)
    store(0, out_result, to_result)
    run_two_own("q")
    run_three("q")
    finish("f1")
    store(2, out_f1, to_f1)
    run_four("q", (0,))
    f2_run_two(2)
    run_four("q", (1,))
    got(sums_three, got_narrow.at[1], S_AR + 5, along[2])
    sums_all[core] = sums_three[...] + got_narrow[1]
    send(sums_all.at[core], sums_all.at[core], S_AR + 6, mate)
    f2_run_three(2)
    f2_finish()
    store(3, out_f2, to_f2)
    got(sums_all.at[core], sums_all.at[core], S_AR + 6, mate)
    small = jnp.concatenate([sums_all[0], sums_all[1]], axis=1)
    out_gains[...] = small[0:2]
    out_biases[...] = small[2:8]
    for k in range(4):
        out_fc1_bias[:, 768 * k : 768 * k + 768] = small[8 + k : 9 + k]
    for k in range(3):
        out_rel[8 * k : 8 * k + 8, :] = small[16:24, 256 * k : 256 * k + 169]
    out_stats[...] = jnp.sqrt(small[12:13, 1:4] / (model * small[12:13, 0:1]))
    for k, (src, dst) in enumerate(
        (
            (out_gains, to_gains),
            (out_biases, to_biases),
            (out_fc1_bias, to_fc1_bias),
            (out_rel, to_rel),
            (out_stats, to_stats),
        )
    ):
        store(4 + k, src, dst)
    finish("q")

    leave()


def fused_on_device(
    tokens, cotangent, crops, labels, norm_gains, biases, rel_table, w_qkv, w_proj, w_fc1, fc1_bias, w_fc2
):
    images, _, patches, model = tokens.shape
    hidden = w_fc1.shape[1]
    heads = rel_table.shape[1]
    vmem = pl.BlockSpec(memory_space=pltpu.VMEM)
    hbm = pl.BlockSpec(memory_space=pl.ANY)

    def low(*shape):
        return pltpu.VMEM(shape, LOW)

    def full(*shape):
        return pltpu.VMEM(shape, FULL)

    one_low = low(ROWS, model)
    one_t = low(model, ROWS)
    scratch = dict(
        wq=low(*w_qkv.shape),
        wp=low(*w_proj.shape),
        w1=low(*w_fc1.shape),
        w2=low(*w_fc2.shape),
        stack=full(256, model),
        result_low=one_low,
        x_own=full(ROWS, model),
        g_low=one_low,
        g_t=low(4, 2, 96, 256),
        g_both=low(4, 96, 512),
        tok_own=one_low,
        tok_win=one_low,
        g_own=one_low,
        result_own=one_low,
        xw=one_low,
        xw_t=low(model, 512),
        query=one_low,
        key=low(KEYS, model),
        value=low(KEYS, model),
        key_bias=low(heads, KEYS, 128),
        row_scale=full(ROWS, model),
        probs=low(heads, KEYS, KEYS),
        att=one_low,
        att_t=low(model, 512),
        middle=full(ROWS, model),
        h2=one_low,
        h2_t=low(model, 512),
        act=low(512, hidden),
        dh=low(512, hidden),
        gf1=low(4, 2, 4, 96, 384),
        gf2=low(4, 4, 2, 48, 768),
        rzf2=low(4, 2, 48, 768),
        gq=low(4, 2, 4, 96, 384),
        r1f1=low(2, 2, 4, 96, 384),
        r1f2=low(2, 2, 3, 48, 768),
        r1q=low(2, 2, 4, 96, 384),
        r2f1=low(2, 4, 96, 384),
        r2f2=low(2, 3, 48, 768),
        r3f2=low(2, 48, 768),
        r2q=low(2, 4, 96, 384),
        r3f1=low(2, 2, 96, 384),
        r3q=low(2, 2, 96, 384),
        r4f1=low(2, 96, 384),
        r4f2=low(2, 48, 768),
        r4q=low(2, 96, 384),
        d_mid=full(ROWS, model),
        d_branch=one_low,
        db_pack=low(2, 512, 512),
        d_att=one_low,
        d_proj=low(ROWS, 3 * model),
        dy_pack=low(2, 512, 1536),
        d_win=one_low,
        d_own=one_low,
        rel_rows=full(64 * 24, 128),
        rel_grads=full(64 * 24, 128),
        mask_add=full(ROWS, KEYS),
        valid_col=full(ROWS, 1),
        sums=full(24, 768),
        sums_one=full(24, 384),
        sums_two=full(24, 384),
        sums_three=full(24, 384),
        sums_all=full(2, 24, 384),
        got_core=full(24, 768),
        got_wide=full(3, 24, 384),
        got_narrow=full(2, 24, 384),
        local_sem=pltpu.SemaphoreType.DMA((32,)),
        send_sem=pltpu.SemaphoreType.DMA((S_COUNT,)),
        recv_sem=pltpu.SemaphoreType.DMA((S_COUNT,)),
    )
    shapes = (
        ((patches, images, model), LOW),
        ((patches, images, model), LOW),
        ((192, 288), FULL),
        ((192, 96), FULL),
        ((192, 384), FULL),
        ((96, 768), FULL),
        ((2, model), FULL),
        ((6, model), FULL),
        ((1, hidden), FULL),
        ((heads, 169), FULL),
        ((1, 3), FULL),
    )
    inputs = (
        ((patches, images, model), LOW),
        ((patches, images, model), LOW),
        ((2, images), jnp.int32),
        ((images, patches), jnp.int32),
        ((2, model), FULL),
        ((6, model), FULL),
        ((heads, 169), FULL),
        ((1, hidden), FULL),
        ((TABLE_ROWS, 256), LOW),
        ((ROWS, 8), jnp.int32),
    )
    outs = pl.pallas_call(
        block_kernel,
        out_shape=tuple(jax.ShapeDtypeStruct(*shape) for shape in shapes),
        in_specs=[hbm] * 14,
        out_specs=[hbm] * OUTPUTS,
        scratch_shapes=[pltpu.VMEM(*shape) for shape in inputs + shapes] + list(scratch.values()),
        compiler_params=pltpu.CompilerParams(
            collective_id=0, has_side_effects=True, vmem_limit_bytes=VMEM_LIMIT
        ),
    )(
        tokens[:, 0].transpose(1, 0, 2),
        cotangent[:, 0].transpose(1, 0, 2),
        crops.T,
        labels[:, 0],
        norm_gains,
        biases,
        rel_table.T,
        w_qkv,
        w_proj,
        w_fc1,
        fc1_bias.reshape(1, hidden),
        w_fc2,
        *[jnp.asarray(table) for table in place_tables()],
    )
    outs = pl.pallas_call(
        hand_over,
        out_shape=tuple(jax.ShapeDtypeStruct(*shape) for shape in shapes),
        in_specs=[hbm] * OUTPUTS,
        out_specs=[hbm] * OUTPUTS,
        scratch_shapes=[pltpu.VMEM(*shape) for shape in shapes]
        + [pltpu.SemaphoreType.DMA((2, OUTPUTS))],
    )(*outs)
    return (
        outs[0].transpose(1, 0, 2)[:, None],
        outs[1].transpose(1, 0, 2)[:, None],
        outs[2],
        outs[3],
        outs[4],
        outs[5].T,
        outs[6],
        outs[7],
        outs[8].reshape(hidden),
        outs[9].T,
        outs[10].reshape(3),
    )


def hand_over(*refs):
    sems = refs[-1]
    held = refs[2 * OUTPUTS : 3 * OUTPUTS]
    loads = [pltpu.make_async_copy(refs[k], held[k], sems.at[0, k]) for k in range(OUTPUTS)]
    stores = [pltpu.make_async_copy(held[k], refs[OUTPUTS + k], sems.at[1, k]) for k in range(OUTPUTS)]
    for load in loads:
        load.start()
    for load, store in zip(loads, stores):
        load.wait()
        store.start()
    for store in stores:
        store.wait()


VMEM_LIMIT = 62 * 1024 * 1024


def fused(mesh):
    each = P("wide", "narrow", None, None)
    cut = P("narrow", "wide")
    return jax.shard_map(
        fused_on_device,
        mesh=mesh,
        in_specs=(each, each, P("wide", None), P("wide", "narrow", None)) + (P(),) * 8,
        out_specs=(each, each) + (cut,) * 4 + (P(),) * 5,
        check_vma=False,
    )


def solution(mesh):
    if mesh.shape["wide"] == 8 and mesh.shape["narrow"] == 4:
        return fused(mesh)
    return plain(mesh)
```
